32 devices in a mesh: seq: 16 (over z, y, x), head: 2 (over core).
Axes of the slice: x: 2, y: 2, z: 4, core: 2. Of those that a mesh axis runs over, the one named last changes fastest.
Arguments:
- hidden: bfloat16 [2048, 2048], P('seq'), may hold values from -6 to 6
- queries: bfloat16 [2048, 3072], P('seq', 'head'), may hold values from -90 to 90
- req_len: int32 [2], replicated, may hold values from 1 to 1920, 2048 in all
- req_offset: int32 [2], replicated, may hold values from 0 to 4095
- expert_ids: int32 [2048, 6], P('seq'), may hold values from 0 to 15, all different within a row; in each aligned block of 128 rows (0 to 127, 128 to 255, ...) at most 64 rows name the same one
- decode_slot: int32 [128], replicated, may hold values from 0 to 127, as said below
- attn_gain: float32 [2048], replicated, may hold values from 0.25 to 1.75
- kv_down: bfloat16 [2048, 576], replicated, may hold values from -0.125 to 0.125
- kv_gain: float32 [512], replicated, may hold values from 0.25 to 1.75
- key_up: bfloat16 [16, 128, 512], P('head'), may hold values from -0.5 to 0.5
- value_up: bfloat16 [16, 512, 128], P('head'), may hold values from -0.25 to 0.25
- out_proj: bfloat16 [2048, 2048], P('head'), may hold values from -0.5 to 0.5
- ffn_gain: float32 [2048], replicated, may hold values from 0.25 to 1.75
- router: float32 [2048, 16], replicated, may hold values from -0.125 to 0.125
- expert_gate_up: bfloat16 [16, 2, 2048, 1408], P('seq', None, None, 'head'), may hold values from -0.125 to 0.125
- expert_down: bfloat16 [16, 1408, 2048], P('seq', 'head'), may hold values from -0.15625 to 0.15625
Outputs:
- output: bfloat16 [2048, 2048], P('seq', 'head')
- decode_latent: bfloat16 [128, 16, 512], P(('seq', 'head'))
- decode_rope: bfloat16 [128, 1024], P(('seq', 'head'))
The draws below stay inside these ranges and needn't reach their ends.
Inputs may be any that keep to these rules, and one draw needn't show every extreme that they name: `req_len`: the lengths sum to 2048. `expert_ids`: the 128 rows of one index of seq name one expert at most 64 times in all. `decode_slot`: all entries differ; slot g belongs to device g // 4 in the order seq then head, and all 4 slots of some device are named.
All inputs are finite; a program needn't handle non-finite values.
Results may differ from the reference program's by a relative error of at most 0.02.
Values may be sent and summed in bfloat16 or wider, within the bound.
A program may use at most 128 MiB of HBM per device.

```python
import math
import jax
import jax.numpy as jnp
import numpy as np
from jax import lax

D = 2048
N_HEADS = 16
NOPE = 128
ROPE = 64
V_HEAD = 128
KV_RANK = 512
FF = 1408
TOP = 6
TOK_DEV = 128
BLOCK = 16
DEC_SLOTS = 4
EXPERTS = 16
TOKENS = 2048
NREQ = 2
MAXLEN = 1920
NBLK = 128
TOTAL_SLOTS = 128
CAP = 64
N_SEQ = 16
N_HEAD = 2


def draw_queries(key, part):
    shape_all = (TOKENS, N_HEADS * (NOPE + ROPE))
    values = jax.random.normal(key, shape_all, jnp.float32)
    return jnp.clip(values, -90.0, 90.0).astype(jnp.bfloat16)


def draw_decode_slot(key, part):
    first_key, second_key, third_key = jax.random.split(key, 3)
    owners = TOTAL_SLOTS // DEC_SLOTS
    full_owner = jax.random.randint(first_key, (), 0, owners)
    slot_ids = jnp.arange(TOTAL_SLOTS, dtype=jnp.int32)
    ranking = jax.random.randint(second_key, (TOTAL_SLOTS,), 0, 65536)
    ranking = jnp.where(slot_ids // DEC_SLOTS == full_owner, 65536, ranking)
    ranking = ranking * TOTAL_SLOTS + slot_ids
    chosen = lax.top_k(ranking, NBLK)[1].astype(jnp.int32)
    return jax.random.permutation(third_key, chosen).astype(jnp.int32)


def level_of(stream_key, extent, cuts, smallest, largest):
    def one(dim, parts):
        heights = jax.random.uniform(jax.random.fold_in(jax.random.fold_in(stream_key, 6), dim), (parts,), jnp.float32, smallest / len(cuts), largest / len(cuts))
        return jnp.repeat(jnp.exp(heights), extent[dim] // parts).reshape((-1,) + (1,) * (len(extent) - dim - 1))

    factor_of = one(*cuts[0])
    for cut in cuts[1:]:
        factor_of = factor_of * one(*cut)
    return factor_of


def length_profile(amount, total, limit, slope):
    loads = [(1 << 20) // math.isqrt(grade ** slope) + 1 for grade in range(2, amount + 1)]
    rest, given = total - limit - (amount - 1), [1] * (amount - 1)
    while rest > 0:
        free = [i for i in range(amount - 1) if given[i] < limit]
        whole, left = sum([loads[i] for i in free]), rest
        for i in free:
            addition = min(limit - given[i], max(1, left * loads[i] // whole), rest)
            given[i] = given[i] + addition
            rest = rest - addition
    return np.array([limit] + given)


def uneven(stream_key, number_of, total, limit, skew):
    if number_of == 2:
        one = jax.random.randint(stream_key, (), max(1, total - limit), min(limit, total - 1) + 1)
        return jnp.stack([one, total - one])
    sizes = jnp.asarray(length_profile(number_of, total, limit, skew), jnp.int32)
    couples = (number_of - 1) // 2
    giver, sink = sizes[1:1 + 2 * couples:2], sizes[2:2 + 2 * couples:2]
    room = jnp.minimum(giver - 1, limit - sink)
    shifted = jax.random.randint(jax.random.fold_in(stream_key, 1), (couples,), 0, 1 << 20) % (room + 1)
    sizes = sizes.at[1:1 + 2 * couples:2].set(giver - shifted).at[2:2 + 2 * couples:2].set(sink + shifted)
    return sizes[jax.random.permutation(jax.random.fold_in(stream_key, 2), number_of)]


def deal_out(stream_key, own, number, rows, number_of, top, limit, skew):
    order = jax.random.permutation(stream_key, number_of)
    crowded, common = load_shares(number_of, rows * top, limit, skew, True), load_shares(number_of, rows * top, limit, skew, False)
    places = jnp.arange(number_of)

    def named(sizes, turn):
        used = int((sizes > 0).sum())
        fixed = max(1, used // 4)
        passed = fixed + (places - fixed + turn * (used - fixed)) % max(1, number_of - fixed)
        return jnp.zeros((number_of,), jnp.int32).at[order[jnp.where(places < fixed, places, passed)]].set(jnp.asarray(sizes, jnp.int32))

    sizes = jnp.where(number % 4 == 0, named(crowded, number // 4), named(common, number - number // 4 - 1))
    mixed = jax.random.permutation(jax.random.fold_in(own, 3), number_of)
    donor, sink = mixed[0:number_of // 2 * 2:2], mixed[1:number_of // 2 * 2:2]
    margin = jnp.minimum(sizes[donor] - 1, limit - sizes[sink]) // 2
    margin = jnp.where((donor == order[0]) | (sink == order[0]) | (sizes[sink] == 0), 0, jnp.maximum(margin, 0))
    passed = jax.random.randint(jax.random.fold_in(own, 4), (number_of // 2,), 0, 1 << 20) % (margin + 1)
    sizes = sizes.at[donor].add(-passed).at[sink].add(passed)
    members = jnp.searchsorted(jnp.cumsum(sizes), jnp.arange(rows * top), side="right").astype(jnp.int32)
    table = members.reshape(top, rows).T
    table = table[jax.random.permutation(jax.random.fold_in(own, 1), rows)]
    turn = jax.random.randint(jax.random.fold_in(own, 2), (rows, 1), 0, top)
    return jnp.take_along_axis(table, (jnp.arange(top)[None, :] + turn) % top, axis=1)


def load_shares(number_of, total, limit, slope, full):
    weights = [(1 << 20) // math.isqrt(grade ** slope) + 1 for grade in range(1, number_of + 1)]
    largest = limit if full else min(limit, max(-(-total // number_of), total * weights[0] // sum(weights)))
    least = 1 if total - largest >= number_of - 1 else 0
    given, spare = [largest] + [least] * (number_of - 1), total - largest - least * (number_of - 1)
    while spare > 0:
        candidates = [i for i in range(1, number_of) if given[i] < largest] or [i for i in range(1, number_of) if given[i] < limit]
        whole, budget = sum([weights[i] for i in candidates]), spare
        for i in candidates:
            more = min(limit - given[i], max(1, budget * weights[i] // whole), spare)
            given[i] = given[i] + more
            spare = spare - more
    return np.array(given)


def scatter_about(own_key, shape, spread, reach, cuts=(), kind=jnp.bfloat16):
    loudness = level_of(own_key, shape, cuts, -0.22, 0.18) if cuts else 1.0
    values = jax.random.normal(own_key, shape, jnp.float32) * spread * loudness
    return jnp.minimum(jnp.maximum(values, -reach), reach).astype(kind)


def setup_inputs(seed: int = 0) -> dict:
    keys = jax.random.split(jax.random.key(seed), 17)
    hidden = scatter_about(keys[0], (TOKENS, D), 1.0, 6.0, ((0, 16),))
    queries = draw_queries(jax.random.fold_in(keys[16], 71), 0)
    req_len = uneven(keys[2], NREQ, TOKENS, MAXLEN, 2).astype(jnp.int32)
    req_offset = jax.random.randint(keys[3], (NREQ,), 0, 4096).astype(jnp.int32)
    expert_ids_keys = jax.random.split(jax.random.fold_in(keys[4], 1), TOKENS // TOK_DEV)
    expert_ids_turns = jax.random.permutation(jax.random.fold_in(keys[4], 3), TOKENS // TOK_DEV)
    expert_ids = jax.vmap(lambda own, number: deal_out(jax.random.fold_in(keys[4], 2), own, number, TOK_DEV, EXPERTS, TOP, CAP, 2))(expert_ids_keys, expert_ids_turns).reshape((TOKENS, TOP))
    decode_slot = draw_decode_slot(jax.random.fold_in(keys[16], 71), 0)
    attn_gain = jnp.clip(1.0 + 0.15 * jax.random.normal(keys[6], (D,), jnp.float32), 0.25, 1.75)
    kv_down = scatter_about(keys[7], (D, KV_RANK + ROPE), D ** -0.5, 0.125)
    kv_gain = jnp.clip(1.0 + 0.15 * jax.random.normal(keys[8], (KV_RANK,), jnp.float32), 0.25, 1.75)
    key_up = scatter_about(keys[9], (N_HEADS, NOPE, KV_RANK), NOPE ** -0.5, 0.5, ((0, 2),))
    value_up = scatter_about(keys[10], (N_HEADS, KV_RANK, V_HEAD), KV_RANK ** -0.5, 0.25, ((0, 2),))
    out_proj = scatter_about(keys[11], (N_HEADS * V_HEAD, D), (N_HEADS * V_HEAD // 16) ** -0.5, 0.5, ((0, 2),))
    ffn_gain = jnp.clip(1.0 + 0.15 * jax.random.normal(keys[12], (D,), jnp.float32), 0.25, 1.75)
    router = scatter_about(keys[13], (D, EXPERTS), D ** -0.5, 0.125, (), jnp.float32)
    expert_gate_up = scatter_about(keys[14], (EXPERTS, 2, D, FF), D ** -0.5, 0.125, ((0, 16), (3, 2)))
    expert_down = scatter_about(keys[15], (EXPERTS, FF, D), FF ** -0.5, 0.15625, ((0, 16), (1, 2)))
    return dict(hidden=hidden, queries=queries, req_len=req_len, req_offset=req_offset, expert_ids=expert_ids, decode_slot=decode_slot, attn_gain=attn_gain, kv_down=kv_down, kv_gain=kv_gain, key_up=key_up, value_up=value_up, out_proj=out_proj, ffn_gain=ffn_gain, router=router, expert_gate_up=expert_gate_up, expert_down=expert_down)


ROPE_BASE = 50000.0
ROUTE_SCALE = 2.446
EPSILON = 1e-06
MASKED = -1e+30

def rms_rows(values, scale_gain):
    values = values.astype(jnp.float32)
    inverse = lax.rsqrt(lax.optimization_barrier(jnp.mean(values * values, axis=-1, keepdims=True)) + EPSILON)
    return values * inverse * scale_gain

def angles(position, rope_width):
    half_width = rope_width // 2
    freq_steps = jnp.arange(half_width).astype(jnp.float32) * (2.0 / rope_width)
    frequency = jnp.exp(-math.log(ROPE_BASE) * freq_steps)
    return position.astype(jnp.float32)[:, None] * frequency[None, :]

def rotate(values, rot_angle):
    half_width = values.shape[-1] // 2
    first_half = values[..., :half_width].astype(jnp.float32)
    second_half = values[..., half_width:].astype(jnp.float32)
    cosine = jnp.cos(rot_angle)
    sine_part = jnp.sin(rot_angle)
    return jnp.concatenate([first_half * cosine - second_half * sine_part, first_half * sine_part + second_half * cosine], axis=-1)

def request_of(req_len, token_index):
    req_ends = jnp.cumsum(req_len).astype(jnp.int32)
    return lax.optimization_barrier(jnp.sum((token_index[:, None] >= req_ends[None, :]).astype(jnp.int32), axis=1)).astype(jnp.int32)

def position_of(req_len, req_offset, token_index):
    request = request_of(req_len, token_index)
    req_ends = jnp.cumsum(req_len).astype(jnp.int32)
    starts = req_ends - req_len
    member = request[:, None] == jnp.arange(req_len.shape[0]).astype(jnp.int32)[None, :]
    start_at = lax.optimization_barrier(jnp.sum(jnp.where(member, starts[None, :], 0), axis=1))
    offset = lax.optimization_barrier(jnp.sum(jnp.where(member, req_offset[None, :], 0), axis=1))
    return (offset + token_index - start_at).astype(jnp.int32)

def reference(hidden, queries, req_len, req_offset, expert_ids, decode_slot, attn_gain, kv_down, kv_gain, key_up, value_up, out_proj, ffn_gain, router, expert_gate_up, expert_down):
    normed = rms_rows(hidden, attn_gain).astype(jnp.bfloat16)
    kv_full = jnp.dot(normed, kv_down, preferred_element_type=jnp.float32)
    latent = rms_rows(kv_full[:, :KV_RANK], kv_gain).astype(jnp.bfloat16)
    token_index = jnp.arange(TOKENS).astype(jnp.int32)
    request = request_of(req_len, token_index)
    token_turn = angles(position_of(req_len, req_offset, token_index), ROPE)
    key_rope = rotate(kv_full[:, KV_RANK:], token_turn).astype(jnp.bfloat16)
    head_view = queries.reshape(TOKENS, N_HEADS, NOPE + ROPE)
    query_rope = rotate(head_view[:, :, NOPE:], token_turn[:, None, :]).astype(jnp.bfloat16)
    query_latent = jnp.einsum('thn,hnc->thc', head_view[:, :, :NOPE].astype(jnp.float32), key_up.astype(jnp.float32)).astype(jnp.bfloat16)
    latent_wide = latent.astype(jnp.float32)
    rope_wide = key_rope.astype(jnp.float32)
    value_wide = value_up.astype(jnp.float32)
    score_scale = 1.0 / math.sqrt(NOPE + ROPE)
    block_rows = 512 if TOKENS % 512 == 0 else TOKENS

    def attend(block_no):
        first_row = block_no * block_rows
        q_latent = lax.dynamic_slice_in_dim(query_latent, first_row, block_rows, 0).astype(jnp.float32)
        q_rope = lax.dynamic_slice_in_dim(query_rope, first_row, block_rows, 0).astype(jnp.float32)
        q_index = first_row + jnp.arange(block_rows).astype(jnp.int32)
        q_request = lax.dynamic_slice_in_dim(request, first_row, block_rows, 0)
        scores = (jnp.einsum('thc,sc->ths', q_latent, latent_wide) + jnp.einsum('thr,sr->ths', q_rope, rope_wide)) * score_scale
        allowed = (token_index[None, :] <= q_index[:, None]) & (request[None, :] == q_request[:, None])
        allowed = allowed[:, None, :]
        scores = jnp.where(allowed, scores, MASKED)
        row_peak = lax.optimization_barrier(jnp.max(scores, axis=2, keepdims=True))
        exp_terms = jnp.where(allowed, jnp.exp(scores - row_peak), 0.0)
        weights = lax.optimization_barrier(exp_terms.astype(jnp.bfloat16)).astype(jnp.float32)
        attended = (jnp.einsum('ths,sc->thc', weights, latent_wide) / lax.optimization_barrier(jnp.sum(exp_terms, axis=2, keepdims=True))).astype(jnp.bfloat16)
        head_out = jnp.einsum('thc,hcv->thv', attended.astype(jnp.float32), value_wide).astype(jnp.bfloat16)
        attn_out = jnp.dot(head_out.reshape(block_rows, N_HEADS * V_HEAD), out_proj, preferred_element_type=jnp.float32)
        return lax.dynamic_slice_in_dim(hidden, first_row, block_rows, 0).astype(jnp.float32) + attn_out
    mixed_rows = lax.map(attend, jnp.arange(TOKENS // block_rows)).reshape(TOKENS, D)
    moe_in = rms_rows(mixed_rows, ffn_gain).astype(jnp.bfloat16)
    gate_score = jax.nn.sigmoid(jnp.dot(moe_in.astype(jnp.float32), router, precision=lax.Precision.HIGHEST))
    chosen = jnp.take_along_axis(gate_score, expert_ids, axis=1)
    gate_weight = ROUTE_SCALE * chosen / lax.optimization_barrier(jnp.sum(chosen, axis=1, keepdims=True))
    rows_most = N_SEQ * CAP
    quarter_units = FF // N_HEAD

    def expert_step(moe_sum, expert):
        hit_mask = expert_ids == expert
        routed = jnp.any(hit_mask, axis=1)
        weight = lax.optimization_barrier(jnp.sum(jnp.where(hit_mask, gate_weight, 0.0), axis=1))
        picked = jnp.nonzero(routed, size=rows_most, fill_value=0)[0]
        is_valid = jnp.arange(rows_most) < jnp.sum(routed.astype(jnp.int32))
        row_data = moe_in[picked]
        gate_up = expert_gate_up[expert]
        gate_part = jnp.dot(row_data, gate_up[0], preferred_element_type=jnp.float32)
        up_part = jnp.dot(row_data, gate_up[1], preferred_element_type=jnp.float32)
        activated = (jax.nn.silu(gate_part) * up_part).astype(jnp.bfloat16)
        quarters = activated.reshape(rows_most, N_HEAD, quarter_units).astype(jnp.float32)
        down_quarters = expert_down[expert].reshape(N_HEAD, quarter_units, D).astype(jnp.float32)
        part_out = jnp.einsum('rqf,qfd->rqd', quarters, down_quarters).astype(jnp.bfloat16)
        summed = lax.optimization_barrier(jnp.sum(part_out.astype(jnp.float32), axis=1))
        contribution = jnp.where(is_valid[:, None], weight[picked][:, None] * summed, 0.0)
        return (moe_sum.at[picked].add(contribution), None)
    moe_total, _ = lax.scan(expert_step, jnp.zeros((TOKENS, D), jnp.float32), jnp.arange(EXPERTS).astype(jnp.int32))
    output = (mixed_rows + moe_total).astype(jnp.bfloat16)
    decode_latent = jnp.zeros((TOTAL_SLOTS, BLOCK, KV_RANK), jnp.bfloat16).at[decode_slot].set(latent.reshape(NBLK, BLOCK, KV_RANK))
    decode_rope = jnp.zeros((TOTAL_SLOTS, BLOCK * ROPE), jnp.bfloat16).at[decode_slot].set(key_rope.reshape(NBLK, BLOCK * ROPE))
    return (output, decode_latent, decode_rope)
```

```python
import functools
import math

import jax
import jax.numpy as jnp
from jax import lax
from jax.experimental import pallas as pl
from jax.experimental.pallas import tpu as pltpu
from jax.sharding import PartitionSpec as P

D = 2048
NOPE = 128
ROPE = 64
V_HEAD = 128
KV_RANK = 512
TOP = 6
BLOCK = 16
DEC_SLOTS = 4


ROPE_BASE = 50000.0
ROUTE_SCALE = 2.446
EPSILON = 1e-06
MASKED = -1e30


def rms_rows(values, scale_gain):
    values = values.astype(jnp.float32)
    inverse = lax.rsqrt(jnp.mean(values * values, axis=-1, keepdims=True) + EPSILON)
    return values * inverse * scale_gain


def angles(position, rope_width):
    half_width = rope_width // 2
    freq_steps = jnp.arange(half_width).astype(jnp.float32) * (2.0 / rope_width)
    frequency = jnp.exp(-math.log(ROPE_BASE) * freq_steps)
    return position.astype(jnp.float32)[:, None] * frequency[None, :]


def rotate(values, rot_angle):
    half_width = values.shape[-1] // 2
    first_half = values[..., :half_width].astype(jnp.float32)
    second_half = values[..., half_width:].astype(jnp.float32)
    cosine = jnp.cos(rot_angle)
    sine_part = jnp.sin(rot_angle)
    return jnp.concatenate(
        [
            first_half * cosine - second_half * sine_part,
            first_half * sine_part + second_half * cosine,
        ],
        axis=-1,
    )


def running(lengths):
    index = jnp.arange(lengths.shape[0])
    return jnp.sum(jnp.where(index[None, :] <= index[:, None], lengths[None, :], 0), axis=1)


def ranks(member):
    count = member.shape[-1]
    index = jnp.arange(count)
    before = (index[:, None] < index[None, :]).astype(jnp.bfloat16)
    return jnp.dot(member, before, preferred_element_type=jnp.float32).astype(jnp.int32)


def request_of(req_len, token_index):
    req_ends = running(req_len)
    return jnp.sum((token_index[:, None] >= req_ends[None, :]).astype(jnp.int32), axis=1)


def position_of(req_len, req_offset, token_index):
    request = request_of(req_len, token_index)
    req_ends = running(req_len)
    starts = req_ends - req_len
    member = request[:, None] == jnp.arange(req_len.shape[0])[None, :]
    start_at = jnp.sum(jnp.where(member, starts[None, :], 0), axis=1)
    offset = jnp.sum(jnp.where(member, req_offset[None, :], 0), axis=1)
    return offset + token_index - start_at


def key_width(piece_rows):
    for option_width in (1024, 512, 256, 128):
        return option_width
    return piece_rows


MESH = pl.DeviceIdType.MESH


def flip(place, step):
    return place + step * (1 - 2 * lax.rem(lax.div(place, step), 2))


def place_of(s, h, nz, back, turn):
    line = lax.rem(lax.div(s, 4) - back + nz, nz)
    block = line * 4 + lax.rem(s, 4)
    if turn & 1:
        block = flip(block, 2 - h)
    if turn & 2:
        block = flip(block, 1 + h)
    return block


def meet(s, h, nz):
    barrier = pltpu.get_barrier_semaphore()
    peers = [(place_of(s, h, nz, back, 0), h) for back in range(1, nz)]
    peers += [(flip(s, 2 - h), h), (flip(s, 1 + h), h), (s, 1 - h)]
    for peer in peers:
        pl.semaphore_signal(barrier, inc=1, device_id=peer, device_id_type=MESH)
    pl.semaphore_wait(barrier, len(peers))


class Spread:
    def __init__(self, buf, s, h, nz, sems, blocks_first=False):
        self.blocks_first = blocks_first
        self.buf, self.s, self.h, self.nz = buf, s, h, nz
        self.sems = sems

    def move(self, block, kind, index, device):
        view = self.buf.at[block, self.h] if self.blocks_first else self.buf.at[self.h, block]
        return pltpu.make_async_remote_copy(
            src_ref=view,
            dst_ref=view,
            send_sem=self.sems[2 * kind].at[index],
            recv_sem=self.sems[2 * kind + 1].at[index],
            device_id=device,
            device_id_type=MESH,
        )

    def block(self, back, turn):
        return place_of(self.s, self.h, self.nz, back, turn)

    def line(self, ahead):
        device = (place_of(self.s, self.h, self.nz, self.nz - ahead, 0), self.h)
        return self.move(self.block(0, 0), 0, ahead, device)

    def line_in(self, back):
        return self.move(self.block(back, 0), 0, back, (self.s, 1 - self.h))

    def second(self, back, turn=0):
        return self.move(self.block(back, turn), 1, back, (flip(self.s, 2 - self.h), self.h))

    def third(self, back, side, turn=0):
        device = (flip(self.s, 1 + self.h), self.h)
        return self.move(self.block(back, turn + side), 2, 2 * back + side, device)

    def sibling(self, back, mine):
        half = self.h if mine else 1 - self.h
        line = lax.rem(lax.div(self.s, 4) - back + self.nz, self.nz)
        four = pl.ds(line * 4, 4)
        view = self.buf.at[four, half] if self.blocks_first else self.buf.at[half, four]
        return pltpu.make_async_remote_copy(
            src_ref=view,
            dst_ref=view,
            send_sem=self.sems[6].at[back],
            recv_sem=self.sems[7].at[back],
            device_id=(self.s, 1 - self.h),
            device_id_type=MESH,
        )

    def send_all(self):
        for ahead in range(1, self.nz):
            self.line(ahead).start()
        for back in range(self.nz):
            if back:
                self.line_in(back).wait_recv()
            self.third(back, 0).start()
            self.second(back).start()
            self.second(back, 1).wait_recv()
            self.third(back, 1).start()

    def pass_on(self, back):
        for side in range(2):
            self.third(back, side, 2).wait_recv()
        self.sibling(back, True).start()

    def drain(self):
        for ahead in range(1, self.nz):
            self.line(ahead).wait_send()
        for back in range(self.nz):
            self.second(back).wait_send()
            self.third(back, 0).wait_send()
            self.third(back, 1).wait_send()
            self.sibling(back, True).wait_send()


def spread_sems(nz):
    dma = pltpu.SemaphoreType.DMA
    return [dma((nz,)), dma((nz,)), dma((nz,)), dma((nz,)), dma((2 * nz,)), dma((2 * nz,)), dma((nz,)), dma((nz,))]


def gather_kernel(nz, rows_ref, out_ref, *sems):
    s, h = lax.axis_index("seq"), lax.axis_index("head")
    out_ref[s, h] = rows_ref[h]
    meet(s, h, nz)
    spread = Spread(out_ref, s, h, nz, sems, True)
    spread.send_all()
    for back in range(nz):
        spread.pass_on(back)
    for back in range(nz):
        spread.sibling(back, False).wait_recv()
    spread.drain()


def gather_rows(rows, seq_count):
    tok_rows, width = rows.shape
    nz = seq_count // 4
    out = pl.pallas_call(
        functools.partial(gather_kernel, nz),
        out_shape=jax.ShapeDtypeStruct((seq_count, 2, tok_rows // 2, width), rows.dtype),
        in_specs=[pl.BlockSpec(memory_space=pltpu.VMEM)],
        out_specs=pl.BlockSpec(memory_space=pltpu.VMEM),
        scratch_shapes=spread_sems(nz),
        compiler_params=pltpu.CompilerParams(
            collective_id=0, has_side_effects=True, vmem_limit_bytes=16 * 1024 * 1024
        ),
    )(rows.reshape(2, tok_rows // 2, width))
    return out.reshape(seq_count * tok_rows, width)


def line_place(line, s):
    return line * 4 + lax.rem(s, 4)


def across(s, step):
    if step & 1:
        s = flip(s, 1)
    if step & 2:
        s = flip(s, 2)
    return s


def turn_line(z, k):
    upper = lax.div(z, 2)
    near = z + upper * (3 - 2 * z)
    late = lax.div(k, 2)
    line = late * k + (1 - late) * (near + k * (1 - 2 * near))
    return line + upper * (3 - 2 * line)


def expert_kernel(
    hidden_ref,
    attn_ref,
    gain_ref,
    tail_ref,
    router_ref,
    gate_up_hbm,
    down_hbm,
    out_ref,
    attn_in,
    mixed,
    x_buf,
    stage,
    rows_in,
    res,
    sib_in,
    ret_in,
    z_out,
    z_in,
    pick_buf,
    place_buf,
    chosen_buf,
    router_buf,
    gate_up,
    down,
    load_sem,
    attn_sem,
    up_send,
    up_recv,
    down_send,
    down_recv,
    go_send,
    go_recv,
    share_send,
    share_recv,
    part_send,
    part_recv,
    ret_send,
    ret_recv,
    home_send,
    home_recv,
):
    s, h = lax.axis_index("seq"), lax.axis_index("head")
    z, c = lax.div(s, 4), lax.rem(s, 4)
    cols = hidden_ref.shape[1]
    half = cols // 2
    slots = stage.shape[2]
    tok_rows = hidden_ref.shape[0]
    expert_count = router_ref.shape[0]
    sibling = (s, 1 - h)
    loads = [
        pltpu.make_async_copy(gate_up_hbm, gate_up, load_sem.at[0]),
        pltpu.make_async_copy(down_hbm, down, load_sem.at[1]),
    ]
    for load in loads:
        load.start()

    def remote(src, dst, send, recv, device):
        return pltpu.make_async_remote_copy(
            src_ref=src,
            dst_ref=dst,
            send_sem=send,
            recv_sem=recv,
            device_id=device,
            device_id_type=MESH,
        )

    barrier = pltpu.get_barrier_semaphore()
    peers = [(line_place(lax.rem(z + back, 4), s), h) for back in range(1, 4)]
    peers += [(across(s, step), h) for step in range(1, 4)] + [sibling]
    for peer in peers:
        pl.semaphore_signal(barrier, inc=1, device_id=peer, device_id_type=MESH)
    pl.semaphore_wait(barrier, len(peers))

    def up(t):
        view = x_buf.at[z - t]
        device = (line_place(lax.rem(z + 1, 4), s), h)
        return remote(view, view, up_send.at[t], up_recv.at[t], device)

    def up_in(t):
        view = x_buf.at[z - t]
        return remote(view, view, up_send.at[t - 1], up_recv.at[t - 1], sibling)

    def low(t):
        view = x_buf.at[z + t]
        device = (line_place(lax.rem(z + 3, 4), s), h)
        return remote(view, view, down_send.at[t], down_recv.at[t], device)

    def low_in(t):
        view = x_buf.at[z + t]
        return remote(view, view, down_send.at[t - 1], down_recv.at[t - 1], sibling)

    def go(k, step):
        other = across(s, step)
        index = 3 * k + step - 1
        return remote(
            stage.at[k, lax.rem(other, 4)],
            rows_in.at[k, h, c],
            go_send.at[index],
            go_recv.at[index],
            (other, h),
        )

    def go_in(k, step):
        index = 3 * k + step - 1
        view = rows_in.at[k, h, lax.rem(across(s, step), 4)]
        return remote(view, view, go_send.at[index], go_recv.at[index], sibling)

    def share(k):
        view = rows_in.at[k, h]
        return remote(view, view, share_send.at[k], share_recv.at[k], sibling)

    def share_in(k):
        view = rows_in.at[k, 1 - h]
        return remote(view, view, share_send.at[k], share_recv.at[k], sibling)

    def part(k):
        return remote(res.at[k, 1 - h], sib_in.at[k], part_send.at[k], part_recv.at[k], sibling)

    def ret(k, step):
        other = across(s, step)
        index = 3 * k + step - 1
        return remote(
            res.at[k, h, lax.rem(other, 4)],
            ret_in.at[k, c],
            ret_send.at[index],
            ret_recv.at[index],
            (other, h),
        )

    def ret_back(k, step):
        index = 3 * k + step - 1
        view = ret_in.at[k, lax.rem(across(s, step), 4)]
        return remote(view, view, ret_send.at[index], ret_recv.at[index], sibling)

    def home(k):
        owner = (line_place(turn_line(z, k), s), h)
        return remote(z_out.at[k], z_in.at[z], home_send.at[k], home_recv.at[z], owner)

    def home_in(back):
        line = lax.rem(z + back, 4)
        return remote(z_in.at[line], z_in.at[line], home_send.at[0], home_recv.at[line], sibling)

    swap = remote(attn_ref, attn_in, attn_sem.at[0], attn_sem.at[1], sibling)
    swap.start()

    def iota(shape, dim):
        return lax.broadcasted_iota(jnp.int32, shape, dim)

    bf16, f32 = jnp.bfloat16, jnp.float32
    pair = (((1,), (1,)), ((), ()))
    four = 4 * slots
    lane = (tok_rows, 128)
    before = (iota((tok_rows, tok_rows), 0) < iota((tok_rows, tok_rows), 1)).astype(bf16)
    after = (iota((tok_rows, tok_rows), 0) > iota((tok_rows, tok_rows), 1)).astype(bf16)

    def one_hot(flags):
        return jnp.where(flags, 1.0, 0.0).astype(bf16)

    def prepare(k):
        line = turn_line(z, k)
        tail = tail_ref[line * 4 + c]
        shape = (four, 128)
        named = one_hot(iota(shape, 1) == ROPE + 4 * z + lax.div(iota(shape, 0), slots))
        slot = lax.rem(iota((four, tok_rows), 0), slots).astype(f32)
        member = lax.dot_general(named, tail, pair, preferred_element_type=f32)
        rank = jnp.dot(member.astype(bf16), before, preferred_element_type=f32)
        pick_buf[k] = one_hot((rank == slot) & (member > 0.0))
        shape = (128, four)
        named = one_hot(iota(shape, 0) == ROPE + 4 * z + lax.div(iota(shape, 1), slots))
        slot = lax.rem(iota((tok_rows, four), 1), slots).astype(f32)
        member = jnp.dot(tail, named, preferred_element_type=f32)
        rank = jnp.dot(after, member.astype(bf16), preferred_element_type=f32)
        place_buf[k] = one_hot((rank == slot) & (member > 0.0))
        named = one_hot(iota((slots, 128), 1) == ROPE + s)
        slot = iota((slots, tok_rows), 0).astype(f32)
        for block in range(4):
            tail = tail_ref[line * 4 + block]
            member = lax.dot_general(named, tail, pair, preferred_element_type=f32)
            rank = jnp.dot(member.astype(bf16), before, preferred_element_type=f32)
            mine = one_hot((rank == slot) & (member > 0.0))
            chosen = jnp.dot(mine, tail, preferred_element_type=f32)
            known = iota((slots, 128), 1)
            known = (known >= ROPE) & (known < ROPE + expert_count)
            chosen_buf[k, block * slots : (block + 1) * slots] = jnp.where(known, chosen, 0.0)

    prepare(0)
    router = router_ref[...]
    high = router.astype(bf16)
    rest = router - high.astype(f32)
    middle = rest.astype(bf16)
    last = (rest - middle.astype(f32)).astype(bf16)
    top_pad = jnp.zeros((ROPE, cols), bf16)
    low_pad = jnp.zeros((128 - ROPE - 3 * expert_count, cols), bf16)
    router_buf[...] = jnp.concatenate([top_pad, high, middle, last, low_pad], axis=0)

    swap.wait_recv()
    total = hidden_ref[...].astype(f32) + (attn_ref[...].astype(f32) + attn_in[...].astype(f32))
    inverse = lax.rsqrt(jnp.mean(total * total, axis=1, keepdims=True) + EPSILON)
    gain = gain_ref[...]
    mine = jnp.where(h == 0, total[:, :half], total[:, half:])
    mixed[...] = mine
    own_gain = jnp.where(h == 0, gain[:, :half], gain[:, half:])
    x_buf[z] = (mine * inverse * own_gain).astype(bf16)

    def ring(t):
        @pl.when((t >= 1) & (t <= z))
        def _():
            up_in(t).wait_recv()

        @pl.when((t <= z) & (z < 3))
        def _():
            up(t).start()

        @pl.when((t >= 1) & (t <= 3 - z))
        def _():
            low_in(t).wait_recv()

        @pl.when((t <= 3 - z) & (z > 0))
        def _():
            low(t).start()

    def pick(k):
        rows = jnp.dot(pick_buf[k], x_buf[turn_line(z, k)], preferred_element_type=f32)
        stage[k] = rows.astype(bf16).reshape(4, slots, half)
        for step in (3, 1, 2):
            go(k, step).start()
        rows_in[k, h, c] = stage[k, c]

    def meet_rows(k):
        for step in (1, 2, 3):
            go_in(k, step).wait_recv()
        share(k).start()

    def work(k):
        share_in(k).wait_recv()
        rows = jnp.concatenate(
            [rows_in[k, 0].reshape(four, half), rows_in[k, 1].reshape(four, half)], axis=1
        )
        logit = lax.dot_general(rows, router_buf[...], pair, preferred_element_type=f32)
        logit = logit + (
            pltpu.roll(logit, 128 - expert_count, 1) + pltpu.roll(logit, 128 - 2 * expert_count, 1)
        )
        score = 1.0 / (1.0 + jnp.exp(-logit))
        chosen = jnp.where(chosen_buf[k] > 0.0, score, 0.0)
        own = jnp.where(iota(chosen.shape, 1) == ROPE + s, chosen, 0.0)
        own = jnp.sum(own, axis=1, keepdims=True)
        every = jnp.sum(chosen, axis=1, keepdims=True)
        weight = ROUTE_SCALE * own / jnp.where(every > 0.0, every, 1.0)
        gate = lax.dot_general(rows, gate_up[0], pair, preferred_element_type=f32)
        rise = lax.dot_general(rows, gate_up[1], pair, preferred_element_type=f32)
        act = (gate / (1.0 + jnp.exp(-gate)) * rise * weight).astype(bf16)
        out = jnp.dot(act, down[...], preferred_element_type=f32).astype(bf16)
        res[k, 0] = out[:, :half].reshape(4, slots, half)
        res[k, 1] = out[:, half:].reshape(4, slots, half)
        part(k).start()

    def send_back(k):
        part(k).wait_recv()
        res[k, h] = (res[k, h].astype(f32) + sib_in[k].astype(f32)).astype(bf16)
        for step in (3, 1, 2):
            ret(k, step).start()
        ret_in[k, c] = res[k, h, c]

    def place(k):
        for step in (1, 2, 3):
            ret_back(k, step).wait_recv()
        return jnp.dot(place_buf[k], ret_in[k].reshape(four, half), preferred_element_type=f32)

    @pl.loop(0, 6)
    def _(t):
        @pl.when(t >= 3)
        def _():
            send_back(t - 2)

        @pl.when(t <= 3)
        def _():
            ring(t)
            pick(t)

        @pl.when(t <= 2)
        def _():
            prepare(t + 1)

        @pl.when(t == 1)
        def _():
            for load in loads:
                load.wait()

        @pl.when((t >= 1) & (t <= 4))
        def _():
            meet_rows(t - 1)
            work(t - 1)

    send_back(0)

    @pl.loop(1, 4)
    def _(k):
        z_out[k] = place(k).astype(bf16)
        home(k).start()

    result = mixed[...] + place(0)
    for back in (1, 2, 3):
        home_in(back).wait_recv()
        result = result + z_in[lax.rem(z + back, 4)].astype(f32)
    out_ref[...] = result.astype(out_ref.dtype)
    swap.wait_send()

    @pl.loop(0, 4)
    def _(k):
        @pl.when((k <= z) & (z < 3))
        def _():
            up(k).wait_send()

        @pl.when((k <= 3 - z) & (z > 0))
        def _():
            low(k).wait_send()

        for step in (1, 2, 3):
            go(k, step).wait_send()
            ret(k, step).wait_send()
        share(k).wait_send()
        part(k).wait_send()

        @pl.when(k > 0)
        def _():
            home(k).wait_send()


def expert_layer(hidden, attn_part, tail, ffn_gain, router, gate_up, down):
    tok_rows, cols = hidden.shape
    half = cols // 2
    expert_count = router.shape[1]
    slots = max(2, tok_rows * TOP * 4 // (3 * expert_count))
    vmem = pl.BlockSpec(memory_space=pltpu.VMEM)
    hbm = pl.BlockSpec(memory_space=pl.ANY)
    dma = pltpu.SemaphoreType.DMA
    bf16, f32 = jnp.bfloat16, jnp.float32
    sizes = [2, 2] + [4] * 4 + [12] * 2 + [4] * 4 + [12] * 2 + [4] * 2
    return pl.pallas_call(
        expert_kernel,
        out_shape=jax.ShapeDtypeStruct((tok_rows, half), bf16),
        in_specs=[vmem] * 5 + [hbm] * 2,
        out_specs=vmem,
        scratch_shapes=[
            pltpu.VMEM((tok_rows, cols), bf16),
            pltpu.VMEM((tok_rows, half), f32),
            pltpu.VMEM((4, tok_rows, half), bf16),
            pltpu.VMEM((4, 4, slots, half), bf16),
            pltpu.VMEM((4, 2, 4, slots, half), bf16),
            pltpu.VMEM((4, 2, 4, slots, half), bf16),
            pltpu.VMEM((4, 4, slots, half), bf16),
            pltpu.VMEM((4, 4, slots, half), bf16),
            pltpu.VMEM((4, tok_rows, half), bf16),
            pltpu.VMEM((4, tok_rows, half), bf16),
            pltpu.VMEM((4, 4 * slots, tok_rows), bf16),
            pltpu.VMEM((4, tok_rows, 4 * slots), bf16),
            pltpu.VMEM((4, 4 * slots, 128), f32),
            pltpu.VMEM((128, cols), bf16),
            pltpu.VMEM(gate_up.shape, bf16),
            pltpu.VMEM(down.shape, bf16),
        ]
        + [dma((size,)) for size in sizes],
        compiler_params=pltpu.CompilerParams(
            collective_id=1, has_side_effects=True, vmem_limit_bytes=56 * 1024 * 1024
        ),
    )(hidden, attn_part, ffn_gain[None, :], tail, router.T, gate_up, down)


def attend_kernel(
    key_tile,
    span_ref,
    first_ref,
    nope_ref,
    rope_ref,
    keys_ref,
    key_up_ref,
    value_up_ref,
    out_proj_ref,
    out_ref,
    query,
    acc,
    peak,
    total,
    heads_buf,
):
    heads, tok_rows = nope_ref.shape[0], nope_ref.shape[1]
    group = 4
    group_rows = group * tok_rows
    score_scale = 1.0 / math.sqrt(NOPE + ROPE)
    contract = (((1,), (1,)), ((), ()))
    for head in range(heads):
        here = slice(head * tok_rows, (head + 1) * tok_rows)
        query[here, :KV_RANK] = jnp.dot(
            nope_ref[head], key_up_ref[head], preferred_element_type=jnp.float32
        ).astype(jnp.bfloat16)
        query[here, KV_RANK:] = rope_ref[head]
    first = jnp.concatenate([first_ref[...]] * group, axis=0)
    own = span_ref[2] + lax.broadcasted_iota(jnp.int32, (tok_rows, 1), 0)
    own = jnp.concatenate([own] * group, axis=0)

    @pl.loop(0, heads // group)
    def _(part_no):
        base = pl.multiple_of(part_no * group_rows, group_rows)
        here = pl.ds(base, group_rows)
        peak[...] = jnp.full_like(peak, MASKED)
        total[...] = jnp.zeros_like(total)
        acc[...] = jnp.zeros_like(acc)

        @pl.loop(span_ref[0], span_ref[1])
        def _(tile):
            start = pl.multiple_of(tile * key_tile, key_tile)
            keys = keys_ref[pl.ds(start, key_tile), :]
            scores = score_scale * lax.dot_general(
                query[here, :], keys, contract, preferred_element_type=jnp.float32
            )
            index = start + lax.broadcasted_iota(jnp.int32, scores.shape, 1)
            allowed = (index <= own) & (index >= first)
            scores = jnp.where(allowed, scores, MASKED)
            old = peak[:, :1]
            new = jnp.maximum(old, jnp.max(scores, axis=1, keepdims=True))
            terms = jnp.where(allowed, jnp.exp(scores - new), 0.0)
            fade = jnp.exp(old - new)
            total[:, :1] = total[:, :1] * fade + jnp.sum(terms, axis=1, keepdims=True)
            peak[:, :1] = new
            acc[...] = acc[...] * fade + jnp.dot(
                terms.astype(jnp.bfloat16), keys[:, :KV_RANK], preferred_element_type=jnp.float32
            )

        attended = (acc[...] / total[:, :1]).astype(jnp.bfloat16)
        for member in range(group):
            heads_buf[part_no * group + member] = jnp.dot(
                attended[member * tok_rows : (member + 1) * tok_rows],
                value_up_ref[part_no * group + member],
                preferred_element_type=jnp.float32,
            ).astype(jnp.bfloat16)

    joined = jnp.concatenate([heads_buf[head] for head in range(heads)], axis=1)
    out_ref[...] = jnp.dot(
        joined, out_proj_ref[...], preferred_element_type=jnp.float32
    ).astype(out_ref.dtype)


def attend_rows(nope, rope, keys, key_up, value_up, out_proj, first, first_token):
    heads, tok_rows = nope.shape[0], nope.shape[1]
    key_tile = 512 if keys.shape[0] % 512 == 0 else 128
    width = keys.shape[1]
    span = jnp.stack(
        [
            jnp.min(first) // key_tile,
            (first_token + tok_rows + key_tile - 1) // key_tile,
            first_token,
        ]
    ).astype(jnp.int32)
    vmem = pl.BlockSpec(memory_space=pltpu.VMEM)
    rows = 4 * tok_rows
    return pl.pallas_call(
        functools.partial(attend_kernel, key_tile),
        out_shape=jax.ShapeDtypeStruct((tok_rows, out_proj.shape[1]), jnp.bfloat16),
        in_specs=[pl.BlockSpec(memory_space=pltpu.SMEM)] + [vmem] * 7,
        out_specs=vmem,
        scratch_shapes=[
            pltpu.VMEM((heads * tok_rows, width), jnp.bfloat16),
            pltpu.VMEM((rows, KV_RANK), jnp.float32),
            pltpu.VMEM((rows, 128), jnp.float32),
            pltpu.VMEM((rows, 128), jnp.float32),
            pltpu.VMEM((heads, tok_rows, V_HEAD), jnp.bfloat16),
        ],
        compiler_params=pltpu.CompilerParams(vmem_limit_bytes=40 * 1024 * 1024),
    )(span, first[:, None], nope, rope, keys, key_up, value_up, out_proj)


def body(
    hidden,
    queries,
    req_len,
    req_offset,
    expert_ids,
    decode_slot,
    attn_gain,
    kv_down,
    kv_gain,
    key_up,
    value_up,
    out_proj,
    ffn_gain,
    router,
    expert_gate_up,
    expert_down,
):
    head_count = lax.axis_size("head")
    seq_place = lax.axis_index("seq")
    head_place = lax.axis_index("head")
    tok_rows = hidden.shape[0]
    heads_here = key_up.shape[0]
    my_index = seq_place * tok_rows + jnp.arange(tok_rows, dtype=jnp.int32)
    my_request = request_of(req_len, my_index)
    my_turn = angles(position_of(req_len, req_offset, my_index), ROPE)
    normed = rms_rows(hidden, attn_gain).astype(jnp.bfloat16)
    head_view = queries.reshape(tok_rows, heads_here, NOPE + ROPE)
    query_rope = rotate(head_view[:, :, NOPE:], my_turn[:, None, :]).astype(jnp.bfloat16)
    query_latent = jnp.einsum(
        "thn,hnc->thc", head_view[:, :, :NOPE], key_up, preferred_element_type=jnp.float32
    ).astype(jnp.bfloat16)
    query_rows = tok_rows * heads_here
    flat_latent = query_latent.reshape(query_rows, KV_RANK)
    flat_rope = query_rope.reshape(query_rows, ROPE)
    row_token = jnp.repeat(my_index, heads_here)
    row_request = jnp.repeat(my_request, heads_here)
    score_scale = 1.0 / math.sqrt(NOPE + ROPE)
    my_device = seq_place * head_count + head_place
    slot_ids = my_device * DEC_SLOTS + jnp.arange(DEC_SLOTS, dtype=jnp.int32)
    block_ids = jnp.arange(decode_slot.shape[0], dtype=jnp.int32)
    slot_match = decode_slot[None, :] == slot_ids[:, None]
    source_block = jnp.sum(jnp.where(slot_match, block_ids[None, :], 0), axis=1)
    slot_filled = jnp.any(slot_match, axis=1)
    kv_full = jnp.dot(normed, kv_down, preferred_element_type=jnp.float32)
    latent = rms_rows(kv_full[:, :KV_RANK], kv_gain).astype(jnp.bfloat16)
    key_rope = rotate(kv_full[:, KV_RANK:], my_turn).astype(jnp.bfloat16)
    run_peak = jnp.full((query_rows,), MASKED, jnp.float32)
    run_total = jnp.zeros((query_rows,), jnp.float32)
    run_acc = jnp.zeros((query_rows, KV_RANK), jnp.float32)
    expert_count = router.shape[1]
    expert_axis = jnp.arange(expert_count, dtype=jnp.int32)
    seq_count = lax.axis_size("seq")
    fast = seq_count == 16 and head_count == 2 and expert_count == 16
    if fast:
        route_mask = jnp.any(expert_ids[:, :, None] == expert_axis[None, None, :], axis=1)
        payload = jnp.concatenate([latent, key_rope, route_mask.astype(jnp.bfloat16)], axis=1)
        payload = jnp.pad(payload, ((0, 0), (0, -payload.shape[1] % 128)))
        gathered = gather_rows(payload, seq_count)
        by_head = jnp.swapaxes(head_view, 0, 1)
        rope_pad = gathered.shape[1] - KV_RANK - ROPE
        by_head_rope = jnp.pad(jnp.swapaxes(query_rope, 0, 1), ((0, 0), (0, 0), (0, rope_pad)))
        req_ends = running(req_len)
        member = my_request[:, None] == jnp.arange(req_len.shape[0])[None, :]
        first = jnp.sum(jnp.where(member, (req_ends - req_len)[None, :], 0), axis=1)
        attn_part = attend_rows(
            by_head[:, :, :NOPE],
            by_head_rope,
            gathered,
            key_up,
            value_up,
            out_proj,
            first,
            seq_place * tok_rows,
        )
        source_row = source_block[:, None] * BLOCK + jnp.arange(BLOCK, dtype=jnp.int32)[None, :]
        pick_rows = source_row[:, :, None] == jnp.arange(gathered.shape[0], dtype=jnp.int32)
        pick_rows = (pick_rows & slot_filled[:, None, None]).reshape(DEC_SLOTS * BLOCK, -1)
        slot_rows = jnp.dot(
            pick_rows.astype(jnp.bfloat16), gathered, preferred_element_type=jnp.float32
        ).astype(jnp.bfloat16)
        decode_latent = slot_rows[:, :KV_RANK].reshape(DEC_SLOTS, BLOCK, KV_RANK)
        decode_rope = slot_rows[:, KV_RANK : KV_RANK + ROPE].reshape(DEC_SLOTS, BLOCK * ROPE)
        tail = gathered[:, KV_RANK : KV_RANK + 128].reshape(seq_count, tok_rows, 128)
        output = expert_layer(
            hidden,
            attn_part,
            tail,
            ffn_gain,
            router,
            jnp.swapaxes(expert_gate_up[0], 1, 2),
            expert_down[0],
        )
        return (output, decode_latent, decode_rope)
    else:
        piece_latent = lax.all_gather(latent, "seq", axis=0, tiled=True)
        piece_rope = lax.all_gather(key_rope, "seq", axis=0, tiled=True)
    piece_rows = piece_latent.shape[0]
    block_width = key_width(piece_rows)

    def key_block(block_no, loop_state):
        peak_now, total_now, acc_now = loop_state
        offset_rows = block_no * block_width
        block_latent = lax.dynamic_slice_in_dim(piece_latent, offset_rows, block_width, 0)
        block_rope = lax.dynamic_slice_in_dim(piece_rope, offset_rows, block_width, 0)
        key_index = offset_rows + jnp.arange(block_width, dtype=jnp.int32)
        key_request = request_of(req_len, key_index)
        contract = (((1,), (1,)), ((), ()))
        scores = lax.dot_general(
            flat_latent, block_latent, contract, preferred_element_type=jnp.float32
        )
        scores = (
            scores
            + lax.dot_general(flat_rope, block_rope, contract, preferred_element_type=jnp.float32)
        ) * score_scale
        allowed = (key_index[None, :] <= row_token[:, None]) & (
            key_request[None, :] == row_request[:, None]
        )
        scores = jnp.where(allowed, scores, MASKED)
        new_peak = jnp.maximum(peak_now, jnp.max(scores, axis=1))
        exp_terms = jnp.where(allowed, jnp.exp(scores - new_peak[:, None]), 0.0)
        fade_factor = jnp.exp(peak_now - new_peak)
        total_now = total_now * fade_factor + jnp.sum(exp_terms, axis=1)
        acc_now = acc_now * fade_factor[:, None] + jnp.dot(
            exp_terms.astype(jnp.bfloat16), block_latent, preferred_element_type=jnp.float32
        )
        return (new_peak, total_now, acc_now)

    run_peak, run_total, run_acc = lax.fori_loop(
        0, piece_rows // block_width, key_block, (run_peak, run_total, run_acc)
    )
    block_count = piece_rows // BLOCK
    pick_matrix = (
        source_block[:, None] == jnp.arange(block_count, dtype=jnp.int32)[None, :]
    ) & slot_filled[:, None]
    pick_matrix = pick_matrix.astype(jnp.bfloat16)
    slot_latent = jnp.dot(
        pick_matrix,
        piece_latent.reshape(block_count, BLOCK * KV_RANK),
        preferred_element_type=jnp.float32,
    )
    slot_rope = jnp.dot(
        pick_matrix,
        piece_rope.reshape(block_count, BLOCK * ROPE),
        preferred_element_type=jnp.float32,
    )
    folded = (run_peak, run_total, run_acc, slot_latent, slot_rope)
    run_total = folded[1]
    run_acc = folded[2]
    slot_latent = folded[3]
    slot_rope = folded[4]
    attended = (
        (run_acc / run_total[:, None]).astype(jnp.bfloat16).reshape(tok_rows, heads_here, KV_RANK)
    )
    head_out = jnp.einsum(
        "thc,hcv->thv", attended, value_up, preferred_element_type=jnp.float32
    ).astype(jnp.bfloat16)
    attn_part = jnp.dot(
        head_out.reshape(tok_rows, heads_here * V_HEAD),
        out_proj,
        preferred_element_type=jnp.float32,
    )
    decode_latent = slot_latent.astype(jnp.bfloat16).reshape(DEC_SLOTS, BLOCK, KV_RANK)
    decode_rope = slot_rope.astype(jnp.bfloat16)
    mixed_rows = hidden.astype(jnp.float32) + lax.psum(
        attn_part.astype(jnp.bfloat16), "head"
    ).astype(jnp.float32)
    moe_in = rms_rows(mixed_rows, ffn_gain).astype(jnp.bfloat16)
    capacity = max(2, tok_rows * TOP * 4 // (3 * expert_count))
    gate_score = jax.nn.sigmoid(
        jnp.dot(moe_in.astype(jnp.float32), router, precision=lax.Precision.HIGHEST)
    )
    id_match = expert_ids[:, :, None] == expert_axis[None, None, :]
    chosen = jnp.sum(jnp.where(id_match, gate_score[:, None, :], 0.0), axis=2)
    gate_weight = ROUTE_SCALE * chosen / jnp.sum(chosen, axis=1, keepdims=True)
    flat_ids = expert_ids.reshape(-1)
    one_hot = (flat_ids[:, None] == expert_axis[None, :]).astype(jnp.int32)
    earlier = ranks(one_hot.T.astype(jnp.bfloat16)).T
    slot_rank = jnp.sum(earlier * one_hot, axis=1)
    flat_slot = flat_ids * capacity + slot_rank
    owner_token = jnp.repeat(jnp.arange(tok_rows, dtype=jnp.int32), TOP)
    slot_token = jnp.zeros((expert_count * capacity,), jnp.int32).at[flat_slot].set(owner_token)
    slot_used = jnp.zeros((expert_count * capacity,), jnp.bool_).at[flat_slot].set(True)
    send_rows = jnp.where(
        slot_used[:, None], moe_in[slot_token], jnp.zeros((), jnp.bfloat16)
    ).reshape(expert_count, capacity, D)
    gate_up_local = expert_gate_up[0]
    down_local = expert_down[0]
    quarter_cols = D // head_count
    arrived = lax.all_to_all(send_rows, "seq", split_axis=0, concat_axis=0, tiled=True)
    sources, item_count, width_cols = arrived.shape
    flat_rows = arrived.reshape(sources * item_count, width_cols)
    gate_part = jnp.dot(flat_rows, gate_up_local[0], preferred_element_type=jnp.float32)
    up_part = jnp.dot(flat_rows, gate_up_local[1], preferred_element_type=jnp.float32)
    activated = (jax.nn.silu(gate_part) * up_part).astype(jnp.bfloat16)
    part_out = (
        jnp.dot(activated, down_local, preferred_element_type=jnp.float32)
        .astype(jnp.bfloat16)
        .reshape(sources, item_count, width_cols)
    )
    returned = lax.all_to_all(part_out, "seq", split_axis=0, concat_axis=0, tiled=True)
    back_cols = returned.shape[2]
    picked = returned.reshape(expert_count * capacity, back_cols)[flat_slot].reshape(
        tok_rows, TOP, back_cols
    )
    weighted = jnp.sum(picked.astype(jnp.float32) * gate_weight[:, :, None], axis=1)
    moe_out = lax.psum_scatter(
        weighted.astype(jnp.bfloat16), "head", scatter_dimension=1, tiled=True
    ).astype(jnp.float32)
    residual_part = lax.dynamic_slice_in_dim(mixed_rows, head_place * quarter_cols, quarter_cols, 1)
    output = (residual_part + moe_out).astype(jnp.bfloat16)
    return (output, decode_latent, decode_rope)


def solution(mesh):
    placed = (
        P("seq", None),
        P("seq", "head"),
        P(),
        P(),
        P("seq", None),
        P(),
        P(),
        P(),
        P(),
        P("head", None, None),
        P("head", None, None),
        P("head", None),
        P(),
        P(),
        P("seq", None, None, "head"),
        P("seq", "head", None),
    )
    return jax.shard_map(
        body,
        mesh=mesh,
        in_specs=placed,
        out_specs=(P("seq", "head"), P(("seq", "head"), None, None), P(("seq", "head"), None)),
        check_vma=False,
    )
```

```python
import functools
import math

import jax
import jax.numpy as jnp
import numpy as np
from jax import lax
from jax.experimental import pallas as pl
from jax.experimental.pallas import tpu as pltpu
from jax.sharding import PartitionSpec as P

D = 2048
NOPE = 128
ROPE = 64
V_HEAD = 128
KV_RANK = 512
TOP = 6
BLOCK = 16
DEC_SLOTS = 4


ROPE_BASE = 50000.0
ROUTE_SCALE = 2.446
EPSILON = 1e-06
MASKED = -1e30


def rms_rows(values, scale_gain):
    values = values.astype(jnp.float32)
    inverse = lax.rsqrt(jnp.mean(values * values, axis=-1, keepdims=True) + EPSILON)
    return values * inverse * scale_gain


def angles(position, rope_width):
    half_width = rope_width // 2
    freq_steps = jnp.arange(half_width).astype(jnp.float32) * (2.0 / rope_width)
    frequency = jnp.exp(-math.log(ROPE_BASE) * freq_steps)
    return position.astype(jnp.float32)[:, None] * frequency[None, :]


def rotate(values, rot_angle):
    half_width = values.shape[-1] // 2
    first_half = values[..., :half_width].astype(jnp.float32)
    second_half = values[..., half_width:].astype(jnp.float32)
    cosine = jnp.cos(rot_angle)
    sine_part = jnp.sin(rot_angle)
    return jnp.concatenate(
        [
            first_half * cosine - second_half * sine_part,
            first_half * sine_part + second_half * cosine,
        ],
        axis=-1,
    )


def running(lengths):
    index = jnp.arange(lengths.shape[0])
    return jnp.sum(jnp.where(index[None, :] <= index[:, None], lengths[None, :], 0), axis=1)


def ranks(member):
    count = member.shape[-1]
    index = jnp.arange(count)
    before = (index[:, None] < index[None, :]).astype(jnp.bfloat16)
    return jnp.dot(member, before, preferred_element_type=jnp.float32).astype(jnp.int32)


def request_of(req_len, token_index):
    req_ends = running(req_len)
    return jnp.sum((token_index[:, None] >= req_ends[None, :]).astype(jnp.int32), axis=1)


def position_of(req_len, req_offset, token_index):
    request = request_of(req_len, token_index)
    req_ends = running(req_len)
    starts = req_ends - req_len
    member = request[:, None] == jnp.arange(req_len.shape[0])[None, :]
    start_at = jnp.sum(jnp.where(member, starts[None, :], 0), axis=1)
    offset = jnp.sum(jnp.where(member, req_offset[None, :], 0), axis=1)
    return offset + token_index - start_at


def key_width(piece_rows):
    for option_width in (1024, 512, 256, 128):
        return option_width
    return piece_rows


MESH = pl.DeviceIdType.MESH


def flip(place, step):
    return place + step * (1 - 2 * lax.rem(lax.div(place, step), 2))


def line_place(line, s):
    return line * 4 + lax.rem(s, 4)


def across(s, step):
    if step & 1:
        s = flip(s, 1)
    if step & 2:
        s = flip(s, 2)
    return s


def turn_line(z, k):
    upper = lax.div(z, 2)
    near = z + upper * (3 - 2 * z)
    late = lax.div(k, 2)
    line = late * k + (1 - late) * (near + k * (1 - 2 * near))
    return line + upper * (3 - 2 * line)


def expert_kernel(
    hidden_ref,
    attn_ref,
    gain_ref,
    tail_ref,
    router_ref,
    gate_up_hbm,
    down_hbm,
    out_ref,
    attn_in,
    mixed,
    x_buf,
    stage,
    rows_in,
    res,
    sib_in,
    ret_in,
    z_out,
    z_in,
    pick_buf,
    place_buf,
    chosen_buf,
    router_buf,
    gate_up,
    down,
    load_sem,
    attn_sem,
    up_send,
    up_recv,
    down_send,
    down_recv,
    go_send,
    go_recv,
    share_send,
    share_recv,
    part_send,
    part_recv,
    ret_send,
    ret_recv,
    home_send,
    home_recv,
):
    s, h = lax.axis_index("seq"), lax.axis_index("head")
    z, c = lax.div(s, 4), lax.rem(s, 4)
    cols = hidden_ref.shape[1]
    half = cols // 2
    slots = stage.shape[2]
    tok_rows = hidden_ref.shape[0]
    expert_count = router_ref.shape[0]
    sibling = (s, 1 - h)
    loads = [
        pltpu.make_async_copy(gate_up_hbm, gate_up, load_sem.at[0]),
        pltpu.make_async_copy(down_hbm, down, load_sem.at[1]),
    ]
    for load in loads:
        load.start()

    def remote(src, dst, send, recv, device):
        return pltpu.make_async_remote_copy(
            src_ref=src,
            dst_ref=dst,
            send_sem=send,
            recv_sem=recv,
            device_id=device,
            device_id_type=MESH,
        )

    barrier = pltpu.get_barrier_semaphore()
    peers = [(line_place(lax.rem(z + back, 4), s), h) for back in range(1, 4)]
    peers += [(across(s, step), h) for step in range(1, 4)] + [sibling]
    for peer in peers:
        pl.semaphore_signal(barrier, inc=1, device_id=peer, device_id_type=MESH)
    pl.semaphore_wait(barrier, len(peers))

    def up(t):
        view = x_buf.at[z - t]
        device = (line_place(lax.rem(z + 1, 4), s), h)
        return remote(view, view, up_send.at[t], up_recv.at[t], device)

    def up_in(t):
        view = x_buf.at[z - t]
        return remote(view, view, up_send.at[t - 1], up_recv.at[t - 1], sibling)

    def low(t):
        view = x_buf.at[z + t]
        device = (line_place(lax.rem(z + 3, 4), s), h)
        return remote(view, view, down_send.at[t], down_recv.at[t], device)

    def low_in(t):
        view = x_buf.at[z + t]
        return remote(view, view, down_send.at[t - 1], down_recv.at[t - 1], sibling)

    def go(k, step):
        other = across(s, step)
        index = 3 * k + step - 1
        return remote(
            stage.at[k, lax.rem(other, 4)],
            rows_in.at[k, h, c],
            go_send.at[index],
            go_recv.at[index],
            (other, h),
        )

    def go_in(k, step):
        index = 3 * k + step - 1
        view = rows_in.at[k, h, lax.rem(across(s, step), 4)]
        return remote(view, view, go_send.at[index], go_recv.at[index], sibling)

    def share(k):
        view = rows_in.at[k, h]
        return remote(view, view, share_send.at[k], share_recv.at[k], sibling)

    def share_in(k):
        view = rows_in.at[k, 1 - h]
        return remote(view, view, share_send.at[k], share_recv.at[k], sibling)

    def part(k):
        return remote(res.at[k, 1 - h], sib_in.at[k], part_send.at[k], part_recv.at[k], sibling)

    def ret(k, step):
        other = across(s, step)
        index = 3 * k + step - 1
        return remote(
            res.at[k, h, lax.rem(other, 4)],
            ret_in.at[k, c],
            ret_send.at[index],
            ret_recv.at[index],
            (other, h),
        )

    def ret_back(k, step):
        index = 3 * k + step - 1
        view = ret_in.at[k, lax.rem(across(s, step), 4)]
        return remote(view, view, ret_send.at[index], ret_recv.at[index], sibling)

    def home(k):
        owner = (line_place(turn_line(z, k), s), h)
        return remote(z_out.at[k], z_in.at[z], home_send.at[k], home_recv.at[z], owner)

    def home_in(back):
        line = lax.rem(z + back, 4)
        return remote(z_in.at[line], z_in.at[line], home_send.at[0], home_recv.at[line], sibling)

    swap = remote(attn_ref, attn_in, attn_sem.at[0], attn_sem.at[1], sibling)
    swap.start()

    def iota(shape, dim):
        return lax.broadcasted_iota(jnp.int32, shape, dim)

    bf16, f32 = jnp.bfloat16, jnp.float32
    pair = (((1,), (1,)), ((), ()))
    four = 4 * slots
    lane = (tok_rows, 128)
    before = (iota((tok_rows, tok_rows), 0) < iota((tok_rows, tok_rows), 1)).astype(bf16)
    after = (iota((tok_rows, tok_rows), 0) > iota((tok_rows, tok_rows), 1)).astype(bf16)

    def one_hot(flags):
        return jnp.where(flags, 1.0, 0.0).astype(bf16)

    def prepare(k):
        line = turn_line(z, k)
        tail = tail_ref[line * 4 + c]
        shape = (four, 128)
        named = one_hot(iota(shape, 1) == ROPE + 4 * z + lax.div(iota(shape, 0), slots))
        slot = lax.rem(iota((four, tok_rows), 0), slots).astype(f32)
        member = lax.dot_general(named, tail, pair, preferred_element_type=f32)
        rank = jnp.dot(member.astype(bf16), before, preferred_element_type=f32)
        pick_buf[k] = one_hot((rank == slot) & (member > 0.0))
        shape = (128, four)
        named = one_hot(iota(shape, 0) == ROPE + 4 * z + lax.div(iota(shape, 1), slots))
        slot = lax.rem(iota((tok_rows, four), 1), slots).astype(f32)
        member = jnp.dot(tail, named, preferred_element_type=f32)
        rank = jnp.dot(after, member.astype(bf16), preferred_element_type=f32)
        place_buf[k] = one_hot((rank == slot) & (member > 0.0))
        named = one_hot(iota((slots, 128), 1) == ROPE + s)
        slot = iota((slots, tok_rows), 0).astype(f32)
        for block in range(4):
            tail = tail_ref[line * 4 + block]
            member = lax.dot_general(named, tail, pair, preferred_element_type=f32)
            rank = jnp.dot(member.astype(bf16), before, preferred_element_type=f32)
            mine = one_hot((rank == slot) & (member > 0.0))
            chosen = jnp.dot(mine, tail, preferred_element_type=f32)
            known = iota((slots, 128), 1)
            known = (known >= ROPE) & (known < ROPE + expert_count)
            chosen_buf[k, block * slots : (block + 1) * slots] = jnp.where(known, chosen, 0.0)

    prepare(0)
    router = router_ref[...]
    high = router.astype(bf16)
    rest = router - high.astype(f32)
    middle = rest.astype(bf16)
    last = (rest - middle.astype(f32)).astype(bf16)
    top_pad = jnp.zeros((ROPE, cols), bf16)
    low_pad = jnp.zeros((128 - ROPE - 3 * expert_count, cols), bf16)
    router_buf[...] = jnp.concatenate([top_pad, high, middle, last, low_pad], axis=0)

    swap.wait_recv()
    total = hidden_ref[...].astype(f32) + (attn_ref[...].astype(f32) + attn_in[...].astype(f32))
    inverse = lax.rsqrt(jnp.mean(total * total, axis=1, keepdims=True) + EPSILON)
    gain = gain_ref[...]
    mine = jnp.where(h == 0, total[:, :half], total[:, half:])
    mixed[...] = mine
    own_gain = jnp.where(h == 0, gain[:, :half], gain[:, half:])
    x_buf[z] = (mine * inverse * own_gain).astype(bf16)

    def ring(t):
        @pl.when((t >= 1) & (t <= z))
        def _():
            up_in(t).wait_recv()

        @pl.when((t <= z) & (z < 3))
        def _():
            up(t).start()

        @pl.when((t >= 1) & (t <= 3 - z))
        def _():
            low_in(t).wait_recv()

        @pl.when((t <= 3 - z) & (z > 0))
        def _():
            low(t).start()

    def pick(k):
        rows = jnp.dot(pick_buf[k], x_buf[turn_line(z, k)], preferred_element_type=f32)
        stage[k] = rows.astype(bf16).reshape(4, slots, half)
        for step in (3, 1, 2):
            go(k, step).start()
        rows_in[k, h, c] = stage[k, c]

    def meet_rows(k):
        for step in (1, 2, 3):
            go_in(k, step).wait_recv()
        share(k).start()

    def work(k):
        share_in(k).wait_recv()
        rows = jnp.concatenate(
            [rows_in[k, 0].reshape(four, half), rows_in[k, 1].reshape(four, half)], axis=1
        )
        logit = lax.dot_general(rows, router_buf[...], pair, preferred_element_type=f32)
        logit = logit + (
            pltpu.roll(logit, 128 - expert_count, 1) + pltpu.roll(logit, 128 - 2 * expert_count, 1)
        )
        score = 1.0 / (1.0 + jnp.exp(-logit))
        chosen = jnp.where(chosen_buf[k] > 0.0, score, 0.0)
        own = jnp.where(iota(chosen.shape, 1) == ROPE + s, chosen, 0.0)
        own = jnp.sum(own, axis=1, keepdims=True)
        every = jnp.sum(chosen, axis=1, keepdims=True)
        weight = ROUTE_SCALE * own / jnp.where(every > 0.0, every, 1.0)
        gate = lax.dot_general(rows, gate_up[0], pair, preferred_element_type=f32)
        rise = lax.dot_general(rows, gate_up[1], pair, preferred_element_type=f32)
        act = (gate / (1.0 + jnp.exp(-gate)) * rise * weight).astype(bf16)
        out = jnp.dot(act, down[...], preferred_element_type=f32).astype(bf16)
        res[k, 0] = out[:, :half].reshape(4, slots, half)
        res[k, 1] = out[:, half:].reshape(4, slots, half)
        part(k).start()

    def send_back(k):
        part(k).wait_recv()
        res[k, h] = (res[k, h].astype(f32) + sib_in[k].astype(f32)).astype(bf16)
        for step in (3, 1, 2):
            ret(k, step).start()
        ret_in[k, c] = res[k, h, c]

    def place(k):
        for step in (1, 2, 3):
            ret_back(k, step).wait_recv()
        return jnp.dot(place_buf[k], ret_in[k].reshape(four, half), preferred_element_type=f32)

    @pl.loop(0, 6)
    def _(t):
        @pl.when(t >= 3)
        def _():
            send_back(t - 2)

        @pl.when(t <= 3)
        def _():
            ring(t)
            pick(t)

        @pl.when(t <= 2)
        def _():
            prepare(t + 1)

        @pl.when(t == 1)
        def _():
            for load in loads:
                load.wait()

        @pl.when((t >= 1) & (t <= 4))
        def _():
            meet_rows(t - 1)
            work(t - 1)

    send_back(0)

    @pl.loop(1, 4)
    def _(k):
        z_out[k] = place(k).astype(bf16)
        home(k).start()

    result = mixed[...] + place(0)
    for back in (1, 2, 3):
        home_in(back).wait_recv()
        result = result + z_in[lax.rem(z + back, 4)].astype(f32)
    out_ref[...] = result.astype(out_ref.dtype)
    swap.wait_send()

    @pl.loop(0, 4)
    def _(k):
        @pl.when((k <= z) & (z < 3))
        def _():
            up(k).wait_send()

        @pl.when((k <= 3 - z) & (z > 0))
        def _():
            low(k).wait_send()

        for step in (1, 2, 3):
            go(k, step).wait_send()
            ret(k, step).wait_send()
        share(k).wait_send()
        part(k).wait_send()

        @pl.when(k > 0)
        def _():
            home(k).wait_send()


def expert_layer(hidden, attn_part, tail, ffn_gain, router, gate_up, down):
    tok_rows, cols = hidden.shape
    half = cols // 2
    expert_count = router.shape[1]
    slots = max(2, tok_rows * TOP * 4 // (3 * expert_count))
    vmem = pl.BlockSpec(memory_space=pltpu.VMEM)
    hbm = pl.BlockSpec(memory_space=pl.ANY)
    dma = pltpu.SemaphoreType.DMA
    bf16, f32 = jnp.bfloat16, jnp.float32
    sizes = [2, 2] + [4] * 4 + [12] * 2 + [4] * 4 + [12] * 2 + [4] * 2
    return pl.pallas_call(
        expert_kernel,
        out_shape=jax.ShapeDtypeStruct((tok_rows, half), bf16),
        in_specs=[vmem] * 5 + [hbm] * 2,
        out_specs=vmem,
        scratch_shapes=[
            pltpu.VMEM((tok_rows, cols), bf16),
            pltpu.VMEM((tok_rows, half), f32),
            pltpu.VMEM((4, tok_rows, half), bf16),
            pltpu.VMEM((4, 4, slots, half), bf16),
            pltpu.VMEM((4, 2, 4, slots, half), bf16),
            pltpu.VMEM((4, 2, 4, slots, half), bf16),
            pltpu.VMEM((4, 4, slots, half), bf16),
            pltpu.VMEM((4, 4, slots, half), bf16),
            pltpu.VMEM((4, tok_rows, half), bf16),
            pltpu.VMEM((4, tok_rows, half), bf16),
            pltpu.VMEM((4, 4 * slots, tok_rows), bf16),
            pltpu.VMEM((4, tok_rows, 4 * slots), bf16),
            pltpu.VMEM((4, 4 * slots, 128), f32),
            pltpu.VMEM((128, cols), bf16),
            pltpu.VMEM(gate_up.shape, bf16),
            pltpu.VMEM(down.shape, bf16),
        ]
        + [dma((size,)) for size in sizes],
        compiler_params=pltpu.CompilerParams(
            collective_id=1, has_side_effects=True, vmem_limit_bytes=56 * 1024 * 1024
        ),
    )(hidden, attn_part, ffn_gain[None, :], tail, router.T, gate_up, down)


def front_kernel(
    req_len_ref,
    req_offset_ref,
    freq_ref,
    hidden_ref,
    gain_ref,
    kv_ref,
    kv_gain_ref,
    ids_ref,
    queries_hbm,
    key_up_hbm,
    value_up_hbm,
    out_proj_hbm,
    out_ref,
    attn_ref,
    queries,
    key_up,
    value_up,
    out_proj,
    query,
    acc,
    peak,
    total,
    heads_buf,
    load_sem,
    up_send,
    up_recv,
    down_send,
    down_recv,
    plane_send,
    plane_recv,
    share_send,
    share_recv,
):
    s, h = lax.axis_index("seq"), lax.axis_index("head")
    z, c = lax.div(s, 4), lax.rem(s, 4)
    bf16, f32 = jnp.bfloat16, jnp.float32
    pair = (((1,), (1,)), ((), ()))
    tok_rows = hidden_ref.shape[0]
    rows_half = tok_rows // 2
    heads = key_up.shape[0]
    part_heads = heads // 2
    part_rows = part_heads * tok_rows
    tile_keys = 4 * tok_rows
    sibling = (s, 1 - h)
    pairs = [(queries_hbm, queries), (key_up_hbm, key_up)]
    pairs += [(value_up_hbm, value_up), (out_proj_hbm, out_proj)]
    loads = [pltpu.make_async_copy(*both, load_sem.at[i]) for i, both in enumerate(pairs)]
    for load in loads:
        load.start()

    barrier = pltpu.get_barrier_semaphore()
    peers = [(line_place(lax.rem(z + back, 4), s), h) for back in (1, 3)]
    peers += [(across(s, step), h) for step in range(1, 4)] + [sibling]
    for peer in peers:
        pl.semaphore_signal(barrier, inc=1, device_id=peer, device_id_type=MESH)

    def iota(shape, dim):
        return lax.broadcasted_iota(jnp.int32, shape, dim)

    def remote(src, dst, send, recv, device):
        return pltpu.make_async_remote_copy(
            src_ref=src,
            dst_ref=dst,
            send_sem=send,
            recv_sem=recv,
            device_id=device,
            device_id_type=MESH,
        )

    def up(t):
        view = out_ref.at[(z - t) * 4 + c, h]
        device = (line_place(lax.rem(z + 1, 4), s), h)
        return remote(view, view, up_send.at[t], up_recv.at[t], device)

    def up_in(t):
        view = out_ref.at[(z - t) * 4 + c, h]
        return remote(view, view, up_send.at[t - 1], up_recv.at[t - 1], sibling)

    def low(t):
        view = out_ref.at[(z + t) * 4 + c, h]
        device = (line_place(lax.rem(z + 3, 4), s), h)
        return remote(view, view, down_send.at[t], down_recv.at[t], device)

    def low_in(t):
        view = out_ref.at[(z + t) * 4 + c, h]
        return remote(view, view, down_send.at[t - 1], down_recv.at[t - 1], sibling)

    def line_of(k):
        return jnp.where(k <= z, z - k, k)

    def plane(k, step):
        view = out_ref.at[line_of(k) * 4 + c, h]
        index = 3 * k + step - 1
        device = (across(s, step), h)
        return remote(view, view, plane_send.at[index], plane_recv.at[index], device)

    def plane_in(k, step):
        view = out_ref.at[line_of(k) * 4 + lax.rem(across(s, step), 4), h]
        index = 3 * k + step - 1
        return remote(view, view, plane_send.at[index], plane_recv.at[index], sibling)

    def share(k):
        view = out_ref.at[pl.ds(line_of(k) * 4, 4), h]
        return remote(view, view, share_send.at[k], share_recv.at[k], sibling)

    def share_in(k):
        view = out_ref.at[pl.ds(line_of(k) * 4, 4), 1 - h]
        return remote(view, view, share_send.at[k], share_recv.at[k], sibling)

    def starts_of(token):
        first = jnp.zeros_like(token)
        offset = jnp.full_like(token, req_offset_ref[0])
        end = req_len_ref[0]
        for r in range(1, req_len_ref.shape[0]):
            later = token >= end
            first = jnp.where(later, end, first)
            offset = jnp.where(later, req_offset_ref[r], offset)
            end = end + req_len_ref[r]
        return first, offset

    def turns(token):
        first, offset = starts_of(token)
        angle = (offset + token - first).astype(f32) * freq_ref[...]
        lane = iota(angle.shape, 1)
        sine = jnp.sin(angle)
        sine = jnp.where(lane < ROPE // 2, -sine, sine)
        rotary = lane < ROPE
        return jnp.where(rotary, jnp.cos(angle), 0.0), jnp.where(rotary, sine, 0.0)

    def spin(values, turn):
        lane = iota(values.shape, 1)
        other = jnp.where(
            lane < ROPE // 2,
            pltpu.roll(values, 128 - ROPE // 2, 1),
            pltpu.roll(values, ROPE // 2, 1),
        )
        return (values * turn[0] + other * turn[1]).astype(bf16)

    base = s * tok_rows
    rows = hidden_ref[pl.ds(pl.multiple_of(h * rows_half, rows_half), rows_half), :].astype(f32)
    inverse = lax.rsqrt(jnp.mean(rows * rows, axis=1, keepdims=True) + EPSILON)
    normed = (rows * inverse * gain_ref[...]).astype(bf16)
    full = lax.dot_general(normed, kv_ref[:KV_RANK], pair, preferred_element_type=f32)
    end = lax.dot_general(
        normed, kv_ref[KV_RANK + ROPE - 128 :], pair, preferred_element_type=f32
    )
    inverse = lax.rsqrt(jnp.mean(full * full, axis=1, keepdims=True) + EPSILON)
    out_ref[s, h, :, :KV_RANK] = (full * inverse * kv_gain_ref[...]).astype(bf16)
    half_token = base + h * rows_half + iota((rows_half, 1), 0)
    key_rope = spin(pltpu.roll(end, ROPE, 1), turns(half_token))
    named = jnp.zeros((128, tok_rows), f32)
    place = iota(named.shape, 0) - ROPE
    for k in range(ids_ref.shape[0]):
        named = jnp.where(ids_ref[k : k + 1, :] == place, 1.0, named)
    row_pick = iota((rows_half, tok_rows), 1) == h * rows_half + iota((rows_half, tok_rows), 0)
    row_pick = jnp.where(row_pick, 1.0, 0.0).astype(bf16)
    mask = lax.dot_general(row_pick, named.astype(bf16), pair, preferred_element_type=f32)
    out_ref[s, h, :, KV_RANK:] = (key_rope.astype(f32) + mask).astype(bf16)
    pl.semaphore_wait(barrier, len(peers))

    def ring(t):
        @pl.when((t >= 1) & (t <= z))
        def _():
            up_in(t).wait_recv()

        @pl.when((t <= z) & (z < 3))
        def _():
            up(t).start()

        @pl.when((t >= 1) & (t <= 3 - z))
        def _():
            low_in(t).wait_recv()

        @pl.when((t <= 3 - z) & (z > 0))
        def _():
            low(t).start()

        for step in (3, 1, 2):
            plane(t, step).start()

    def meet_rows(k):
        for step in (1, 2, 3):
            plane_in(k, step).wait_recv()
        share(k).start()

    ring(0)
    token = base + iota((tok_rows, 1), 0)
    turn = turns(token)
    loads[0].wait()
    loads[1].wait()
    for two in range(heads // 2):
        left = queries[:, 384 * two : 384 * two + 128]
        middle = queries[:, 384 * two + 128 : 384 * two + 256].astype(f32)
        right = queries[:, 384 * two + 256 : 384 * two + 384].astype(f32)
        lane = iota(middle.shape, 1)
        turned = pltpu.roll(right, 64, 1)
        nope = jnp.where(lane < 64, pltpu.roll(middle, 64, 1), turned).astype(bf16)
        for odd, columns, rotary in ((0, left, middle), (1, nope, turned)):
            head = 2 * two + odd
            here = slice(head * tok_rows, (head + 1) * tok_rows)
            query[here, :KV_RANK] = jnp.dot(
                columns, key_up[head], preferred_element_type=f32
            ).astype(bf16)
            query[here, KV_RANK:] = spin(rotary, turn)
    peak[...] = jnp.full_like(peak, MASKED)
    total[...] = jnp.zeros_like(total)
    acc[...] = jnp.zeros_like(acc)
    first = jnp.concatenate([starts_of(token)[0]] * part_heads, axis=0)
    own = jnp.concatenate([token] * part_heads, axis=0)
    scale = math.log2(math.e) / math.sqrt(NOPE + ROPE)

    def attend(k, part_no):
        line = line_of(k)
        keys = out_ref[pl.ds(line * 4, 4)].reshape(tile_keys, out_ref.shape[3])
        here = slice(part_no * part_rows, (part_no + 1) * part_rows)
        scores = scale * lax.dot_general(query[here, :], keys, pair, preferred_element_type=f32)
        index = line * tile_keys + iota(scores.shape, 1)
        scores = jnp.where((index <= own) & (index >= first), scores, MASKED)
        old = peak[part_no, :, :1]
        new = jnp.maximum(old, jnp.max(scores, axis=1, keepdims=True))
        terms = jnp.exp2(scores - new)
        fade = jnp.exp2(old - new)
        total[part_no, :, :1] = total[part_no, :, :1] * fade + jnp.sum(
            terms, axis=1, keepdims=True
        )
        peak[part_no, :, :1] = new
        acc[part_no] = acc[part_no] * fade + jnp.dot(
            terms.astype(bf16), keys[:, :KV_RANK], preferred_element_type=f32
        )

    ring(1)
    meet_rows(0)

    @pl.loop(0, 4)
    def _(k):
        share_in(k).wait_recv()

        @pl.when(k <= z)
        def _():
            attend(k, 0)

        @pl.when(k <= 1)
        def _():
            ring(k + 2)

        @pl.when(k <= 2)
        def _():
            meet_rows(k + 1)

        @pl.when(k <= z)
        def _():
            attend(k, 1)

    loads[2].wait()
    loads[3].wait()
    for head in range(heads):
        part_no, member = head // part_heads, head % part_heads
        here = slice(member * tok_rows, (member + 1) * tok_rows)
        attended = (acc[part_no, here, :] / total[part_no, here, :1]).astype(bf16)
        heads_buf[:, head * V_HEAD : (head + 1) * V_HEAD] = jnp.dot(
            attended, value_up[head], preferred_element_type=f32
        ).astype(bf16)
    attn_ref[...] = jnp.dot(
        heads_buf[...], out_proj[...], preferred_element_type=f32
    ).astype(attn_ref.dtype)

    @pl.loop(0, 4)
    def _(k):
        @pl.when((k <= z) & (z < 3))
        def _():
            up(k).wait_send()

        @pl.when((k <= 3 - z) & (z > 0))
        def _():
            low(k).wait_send()

        for step in (1, 2, 3):
            plane(k, step).wait_send()
        share(k).wait_send()


def front(
    req_len,
    req_offset,
    hidden,
    attn_gain,
    kv_down,
    kv_gain,
    expert_ids,
    queries,
    key_up,
    value_up,
    out_proj,
    seq_count,
):
    tok_rows = hidden.shape[0]
    heads = key_up.shape[0]
    width = KV_RANK + 128
    lanes = np.arange(128) % (ROPE // 2)
    frequency = np.exp(-math.log(ROPE_BASE) * lanes * (2.0 / ROPE)).astype(np.float32)[None, :]
    bf16, f32 = jnp.bfloat16, jnp.float32
    vmem = pl.BlockSpec(memory_space=pltpu.VMEM)
    smem = pl.BlockSpec(memory_space=pltpu.SMEM)
    hbm = pl.BlockSpec(memory_space=pl.ANY)
    dma = pltpu.SemaphoreType.DMA
    part_rows = heads * tok_rows // 2
    return pl.pallas_call(
        front_kernel,
        out_shape=(
            jax.ShapeDtypeStruct((seq_count, 2, tok_rows // 2, width), bf16),
            jax.ShapeDtypeStruct((tok_rows, out_proj.shape[1]), bf16),
        ),
        in_specs=[smem] * 2 + [vmem] * 6 + [hbm] * 4,
        out_specs=(vmem, vmem),
        scratch_shapes=[
            pltpu.VMEM(queries.shape, bf16),
            pltpu.VMEM(key_up.shape, bf16),
            pltpu.VMEM(value_up.shape, bf16),
            pltpu.VMEM(out_proj.shape, bf16),
            pltpu.VMEM((heads * tok_rows, width), bf16),
            pltpu.VMEM((2, part_rows, KV_RANK), f32),
            pltpu.VMEM((2, part_rows, 128), f32),
            pltpu.VMEM((2, part_rows, 128), f32),
            pltpu.VMEM((tok_rows, heads * V_HEAD), bf16),
        ]
        + [dma((size,)) for size in [4] + [4] * 4 + [12] * 2 + [4] * 2],
        compiler_params=pltpu.CompilerParams(
            collective_id=0, has_side_effects=True, vmem_limit_bytes=60 * 1024 * 1024
        ),
    )(
        req_len,
        req_offset,
        jnp.asarray(frequency),
        hidden,
        attn_gain[None, :],
        kv_down.T,
        kv_gain[None, :],
        expert_ids.T,
        queries,
        key_up,
        value_up,
        out_proj,
    )


def body(
    hidden,
    queries,
    req_len,
    req_offset,
    expert_ids,
    decode_slot,
    attn_gain,
    kv_down,
    kv_gain,
    key_up,
    value_up,
    out_proj,
    ffn_gain,
    router,
    expert_gate_up,
    expert_down,
):
    head_count = lax.axis_size("head")
    seq_place = lax.axis_index("seq")
    head_place = lax.axis_index("head")
    tok_rows = hidden.shape[0]
    heads_here = key_up.shape[0]
    my_index = seq_place * tok_rows + jnp.arange(tok_rows, dtype=jnp.int32)
    my_request = request_of(req_len, my_index)
    my_turn = angles(position_of(req_len, req_offset, my_index), ROPE)
    normed = rms_rows(hidden, attn_gain).astype(jnp.bfloat16)
    head_view = queries.reshape(tok_rows, heads_here, NOPE + ROPE)
    query_rope = rotate(head_view[:, :, NOPE:], my_turn[:, None, :]).astype(jnp.bfloat16)
    query_latent = jnp.einsum(
        "thn,hnc->thc", head_view[:, :, :NOPE], key_up, preferred_element_type=jnp.float32
    ).astype(jnp.bfloat16)
    query_rows = tok_rows * heads_here
    flat_latent = query_latent.reshape(query_rows, KV_RANK)
    flat_rope = query_rope.reshape(query_rows, ROPE)
    row_token = jnp.repeat(my_index, heads_here)
    row_request = jnp.repeat(my_request, heads_here)
    score_scale = 1.0 / math.sqrt(NOPE + ROPE)
    my_device = seq_place * head_count + head_place
    slot_ids = my_device * DEC_SLOTS + jnp.arange(DEC_SLOTS, dtype=jnp.int32)
    block_ids = jnp.arange(decode_slot.shape[0], dtype=jnp.int32)
    slot_match = decode_slot[None, :] == slot_ids[:, None]
    source_block = jnp.sum(jnp.where(slot_match, block_ids[None, :], 0), axis=1)
    slot_filled = jnp.any(slot_match, axis=1)
    kv_full = jnp.dot(normed, kv_down, preferred_element_type=jnp.float32)
    latent = rms_rows(kv_full[:, :KV_RANK], kv_gain).astype(jnp.bfloat16)
    key_rope = rotate(kv_full[:, KV_RANK:], my_turn).astype(jnp.bfloat16)
    run_peak = jnp.full((query_rows,), MASKED, jnp.float32)
    run_total = jnp.zeros((query_rows,), jnp.float32)
    run_acc = jnp.zeros((query_rows, KV_RANK), jnp.float32)
    expert_count = router.shape[1]
    expert_axis = jnp.arange(expert_count, dtype=jnp.int32)
    seq_count = lax.axis_size("seq")
    fast = seq_count == 16 and head_count == 2 and expert_count == 16
    if fast:
        blocks, attn_part = front(
            req_len,
            req_offset,
            hidden,
            attn_gain,
            kv_down,
            kv_gain,
            expert_ids,
            queries,
            key_up,
            value_up,
            out_proj,
            seq_count,
        )
        gathered = blocks.reshape(seq_count * tok_rows, blocks.shape[3])
        source_row = source_block[:, None] * BLOCK + jnp.arange(BLOCK, dtype=jnp.int32)[None, :]
        pick_rows = source_row[:, :, None] == jnp.arange(gathered.shape[0], dtype=jnp.int32)
        pick_rows = (pick_rows & slot_filled[:, None, None]).reshape(DEC_SLOTS * BLOCK, -1)
        slot_rows = jnp.dot(
            pick_rows.astype(jnp.bfloat16), gathered, preferred_element_type=jnp.float32
        ).astype(jnp.bfloat16)
        decode_latent = slot_rows[:, :KV_RANK].reshape(DEC_SLOTS, BLOCK, KV_RANK)
        decode_rope = slot_rows[:, KV_RANK : KV_RANK + ROPE].reshape(DEC_SLOTS, BLOCK * ROPE)
        tail = gathered[:, KV_RANK : KV_RANK + 128].reshape(seq_count, tok_rows, 128)
        output = expert_layer(
            hidden,
            attn_part,
            tail,
            ffn_gain,
            router,
            jnp.swapaxes(expert_gate_up[0], 1, 2),
            expert_down[0],
        )
        return (output, decode_latent, decode_rope)
    else:
        piece_latent = lax.all_gather(latent, "seq", axis=0, tiled=True)
        piece_rope = lax.all_gather(key_rope, "seq", axis=0, tiled=True)
    piece_rows = piece_latent.shape[0]
    block_width = key_width(piece_rows)

    def key_block(block_no, loop_state):
        peak_now, total_now, acc_now = loop_state
        offset_rows = block_no * block_width
        block_latent = lax.dynamic_slice_in_dim(piece_latent, offset_rows, block_width, 0)
        block_rope = lax.dynamic_slice_in_dim(piece_rope, offset_rows, block_width, 0)
        key_index = offset_rows + jnp.arange(block_width, dtype=jnp.int32)
        key_request = request_of(req_len, key_index)
        contract = (((1,), (1,)), ((), ()))
        scores = lax.dot_general(
            flat_latent, block_latent, contract, preferred_element_type=jnp.float32
        )
        scores = (
            scores
            + lax.dot_general(flat_rope, block_rope, contract, preferred_element_type=jnp.float32)
        ) * score_scale
        allowed = (key_index[None, :] <= row_token[:, None]) & (
            key_request[None, :] == row_request[:, None]
        )
        scores = jnp.where(allowed, scores, MASKED)
        new_peak = jnp.maximum(peak_now, jnp.max(scores, axis=1))
        exp_terms = jnp.where(allowed, jnp.exp(scores - new_peak[:, None]), 0.0)
        fade_factor = jnp.exp(peak_now - new_peak)
        total_now = total_now * fade_factor + jnp.sum(exp_terms, axis=1)
        acc_now = acc_now * fade_factor[:, None] + jnp.dot(
            exp_terms.astype(jnp.bfloat16), block_latent, preferred_element_type=jnp.float32
        )
        return (new_peak, total_now, acc_now)

    run_peak, run_total, run_acc = lax.fori_loop(
        0, piece_rows // block_width, key_block, (run_peak, run_total, run_acc)
    )
    block_count = piece_rows // BLOCK
    pick_matrix = (
        source_block[:, None] == jnp.arange(block_count, dtype=jnp.int32)[None, :]
    ) & slot_filled[:, None]
    pick_matrix = pick_matrix.astype(jnp.bfloat16)
    slot_latent = jnp.dot(
        pick_matrix,
        piece_latent.reshape(block_count, BLOCK * KV_RANK),
        preferred_element_type=jnp.float32,
    )
    slot_rope = jnp.dot(
        pick_matrix,
        piece_rope.reshape(block_count, BLOCK * ROPE),
        preferred_element_type=jnp.float32,
    )
    folded = (run_peak, run_total, run_acc, slot_latent, slot_rope)
    run_total = folded[1]
    run_acc = folded[2]
    slot_latent = folded[3]
    slot_rope = folded[4]
    attended = (
        (run_acc / run_total[:, None]).astype(jnp.bfloat16).reshape(tok_rows, heads_here, KV_RANK)
    )
    head_out = jnp.einsum(
        "thc,hcv->thv", attended, value_up, preferred_element_type=jnp.float32
    ).astype(jnp.bfloat16)
    attn_part = jnp.dot(
        head_out.reshape(tok_rows, heads_here * V_HEAD),
        out_proj,
        preferred_element_type=jnp.float32,
    )
    decode_latent = slot_latent.astype(jnp.bfloat16).reshape(DEC_SLOTS, BLOCK, KV_RANK)
    decode_rope = slot_rope.astype(jnp.bfloat16)
    mixed_rows = hidden.astype(jnp.float32) + lax.psum(
        attn_part.astype(jnp.bfloat16), "head"
    ).astype(jnp.float32)
    moe_in = rms_rows(mixed_rows, ffn_gain).astype(jnp.bfloat16)
    capacity = max(2, tok_rows * TOP * 4 // (3 * expert_count))
    gate_score = jax.nn.sigmoid(
        jnp.dot(moe_in.astype(jnp.float32), router, precision=lax.Precision.HIGHEST)
    )
    id_match = expert_ids[:, :, None] == expert_axis[None, None, :]
    chosen = jnp.sum(jnp.where(id_match, gate_score[:, None, :], 0.0), axis=2)
    gate_weight = ROUTE_SCALE * chosen / jnp.sum(chosen, axis=1, keepdims=True)
    flat_ids = expert_ids.reshape(-1)
    one_hot = (flat_ids[:, None] == expert_axis[None, :]).astype(jnp.int32)
    earlier = ranks(one_hot.T.astype(jnp.bfloat16)).T
    slot_rank = jnp.sum(earlier * one_hot, axis=1)
    flat_slot = flat_ids * capacity + slot_rank
    owner_token = jnp.repeat(jnp.arange(tok_rows, dtype=jnp.int32), TOP)
    slot_token = jnp.zeros((expert_count * capacity,), jnp.int32).at[flat_slot].set(owner_token)
    slot_used = jnp.zeros((expert_count * capacity,), jnp.bool_).at[flat_slot].set(True)
    send_rows = jnp.where(
        slot_used[:, None], moe_in[slot_token], jnp.zeros((), jnp.bfloat16)
    ).reshape(expert_count, capacity, D)
    gate_up_local = expert_gate_up[0]
    down_local = expert_down[0]
    quarter_cols = D // head_count
    arrived = lax.all_to_all(send_rows, "seq", split_axis=0, concat_axis=0, tiled=True)
    sources, item_count, width_cols = arrived.shape
    flat_rows = arrived.reshape(sources * item_count, width_cols)
    gate_part = jnp.dot(flat_rows, gate_up_local[0], preferred_element_type=jnp.float32)
    up_part = jnp.dot(flat_rows, gate_up_local[1], preferred_element_type=jnp.float32)
    activated = (jax.nn.silu(gate_part) * up_part).astype(jnp.bfloat16)
    part_out = (
        jnp.dot(activated, down_local, preferred_element_type=jnp.float32)
        .astype(jnp.bfloat16)
        .reshape(sources, item_count, width_cols)
    )
    returned = lax.all_to_all(part_out, "seq", split_axis=0, concat_axis=0, tiled=True)
    back_cols = returned.shape[2]
    picked = returned.reshape(expert_count * capacity, back_cols)[flat_slot].reshape(
        tok_rows, TOP, back_cols
    )
    weighted = jnp.sum(picked.astype(jnp.float32) * gate_weight[:, :, None], axis=1)
    moe_out = lax.psum_scatter(
        weighted.astype(jnp.bfloat16), "head", scatter_dimension=1, tiled=True
    ).astype(jnp.float32)
    residual_part = lax.dynamic_slice_in_dim(mixed_rows, head_place * quarter_cols, quarter_cols, 1)
    output = (residual_part + moe_out).astype(jnp.bfloat16)
    return (output, decode_latent, decode_rope)


def solution(mesh):
    placed = (
        P("seq", None),
        P("seq", "head"),
        P(),
        P(),
        P("seq", None),
        P(),
        P(),
        P(),
        P(),
        P("head", None, None),
        P("head", None, None),
        P("head", None),
        P(),
        P(),
        P("seq", None, None, "head"),
        P("seq", "head", None),
    )
    return jax.shard_map(
        body,
        mesh=mesh,
        in_specs=placed,
        out_specs=(P("seq", "head"), P(("seq", "head"), None, None), P(("seq", "head"), None)),
        check_vma=False,
    )
```

```python
import functools
import math

import jax
import jax.numpy as jnp
import numpy as np
from jax import lax
from jax.experimental import pallas as pl
from jax.experimental.pallas import tpu as pltpu
from jax.sharding import PartitionSpec as P

D = 2048
NOPE = 128
ROPE = 64
V_HEAD = 128
KV_RANK = 512
TOP = 6
BLOCK = 16
DEC_SLOTS = 4


ROPE_BASE = 50000.0
ROUTE_SCALE = 2.446
EPSILON = 1e-06
MASKED = -1e30


def rms_rows(values, scale_gain):
    values = values.astype(jnp.float32)
    inverse = lax.rsqrt(jnp.mean(values * values, axis=-1, keepdims=True) + EPSILON)
    return values * inverse * scale_gain


def angles(position, rope_width):
    half_width = rope_width // 2
    freq_steps = jnp.arange(half_width).astype(jnp.float32) * (2.0 / rope_width)
    frequency = jnp.exp(-math.log(ROPE_BASE) * freq_steps)
    return position.astype(jnp.float32)[:, None] * frequency[None, :]


def rotate(values, rot_angle):
    half_width = values.shape[-1] // 2
    first_half = values[..., :half_width].astype(jnp.float32)
    second_half = values[..., half_width:].astype(jnp.float32)
    cosine = jnp.cos(rot_angle)
    sine_part = jnp.sin(rot_angle)
    return jnp.concatenate(
        [
            first_half * cosine - second_half * sine_part,
            first_half * sine_part + second_half * cosine,
        ],
        axis=-1,
    )


def running(lengths):
    index = jnp.arange(lengths.shape[0])
    return jnp.sum(jnp.where(index[None, :] <= index[:, None], lengths[None, :], 0), axis=1)


def ranks(member):
    count = member.shape[-1]
    index = jnp.arange(count)
    before = (index[:, None] < index[None, :]).astype(jnp.bfloat16)
    return jnp.dot(member, before, preferred_element_type=jnp.float32).astype(jnp.int32)


def request_of(req_len, token_index):
    req_ends = running(req_len)
    return jnp.sum((token_index[:, None] >= req_ends[None, :]).astype(jnp.int32), axis=1)


def position_of(req_len, req_offset, token_index):
    request = request_of(req_len, token_index)
    req_ends = running(req_len)
    starts = req_ends - req_len
    member = request[:, None] == jnp.arange(req_len.shape[0])[None, :]
    start_at = jnp.sum(jnp.where(member, starts[None, :], 0), axis=1)
    offset = jnp.sum(jnp.where(member, req_offset[None, :], 0), axis=1)
    return offset + token_index - start_at


def key_width(piece_rows):
    for option_width in (1024, 512, 256, 128):
        return option_width
    return piece_rows


MESH = pl.DeviceIdType.MESH


def flip(place, step):
    return place + step * (1 - 2 * lax.rem(lax.div(place, step), 2))


def line_place(line, s):
    return line * 4 + lax.rem(s, 4)


def across(s, step):
    if step & 1:
        s = flip(s, 1)
    if step & 2:
        s = flip(s, 2)
    return s


def turn_line(z, k):
    upper = lax.div(z, 2)
    near = z + upper * (3 - 2 * z)
    late = lax.div(k, 2)
    line = late * k + (1 - late) * (near + k * (1 - 2 * near))
    return line + upper * (3 - 2 * line)


def layer_kernel(
    req_len_ref,
    req_offset_ref,
    freq_ref,
    hidden_ref,
    gain_ref,
    kv_ref,
    kv_gain_ref,
    ids_ref,
    slot_ref,
    ffn_gain_ref,
    router_ref,
    queries_hbm,
    key_up_hbm,
    value_up_hbm,
    out_proj_hbm,
    gate_up_hbm,
    down_hbm,
    out_ref,
    decode_ref,
    keys_buf,
    queries,
    key_up,
    value_up,
    out_proj,
    query,
    acc,
    peak,
    total,
    heads_buf,
    attn_buf,
    attn_in,
    mixed,
    x_buf,
    stage,
    rows_in,
    res,
    sib_in,
    ret_in,
    z_out,
    z_in,
    pick_buf,
    place_buf,
    chosen_buf,
    router_buf,
    gate_up,
    down,
    load_sem,
    ku_send,
    ku_recv,
    kl_send,
    kl_recv,
    plane_send,
    plane_recv,
    share_keys_send,
    share_keys_recv,
    swap_send,
    swap_recv,
    up_send,
    up_recv,
    down_send,
    down_recv,
    go_send,
    go_recv,
    share_send,
    share_recv,
    part_send,
    part_recv,
    ret_send,
    ret_recv,
    home_send,
    home_recv,
):
    s, h = lax.axis_index("seq"), lax.axis_index("head")
    z, c = lax.div(s, 4), lax.rem(s, 4)
    bf16, f32 = jnp.bfloat16, jnp.float32
    pair = (((1,), (1,)), ((), ()))
    tok_rows = hidden_ref.shape[0]
    rows_half = tok_rows // 2
    heads = key_up.shape[0]
    part_heads = heads // 2
    part_rows = part_heads * tok_rows
    tile_keys = 4 * tok_rows
    sibling = (s, 1 - h)
    pairs = [(queries_hbm, queries), (key_up_hbm, key_up)]
    pairs += [(value_up_hbm, value_up), (out_proj_hbm, out_proj)]
    pairs += [(gate_up_hbm, gate_up), (down_hbm, down)]
    loads = [pltpu.make_async_copy(*both, load_sem.at[i]) for i, both in enumerate(pairs)]
    for load in loads:
        load.start()

    barrier = pltpu.get_barrier_semaphore()
    peers = [(line_place(lax.rem(z + back, 4), s), h) for back in range(1, 4)]
    peers += [(across(s, step), h) for step in range(1, 4)] + [sibling]
    for peer in peers:
        pl.semaphore_signal(barrier, inc=1, device_id=peer, device_id_type=MESH)

    def iota(shape, dim):
        return lax.broadcasted_iota(jnp.int32, shape, dim)

    def remote(src, dst, send, recv, device):
        return pltpu.make_async_remote_copy(
            src_ref=src,
            dst_ref=dst,
            send_sem=send,
            recv_sem=recv,
            device_id=device,
            device_id_type=MESH,
        )

    def key_up_move(t):
        view = keys_buf.at[(z - t) * 4 + c, h]
        device = (line_place(lax.rem(z + 1, 4), s), h)
        return remote(view, view, ku_send.at[t], ku_recv.at[t], device)

    def key_up_in(t):
        view = keys_buf.at[(z - t) * 4 + c, h]
        return remote(view, view, ku_send.at[t - 1], ku_recv.at[t - 1], sibling)

    def key_low_move(t):
        view = keys_buf.at[(z + t) * 4 + c, h]
        device = (line_place(lax.rem(z + 3, 4), s), h)
        return remote(view, view, kl_send.at[t], kl_recv.at[t], device)

    def key_low_in(t):
        view = keys_buf.at[(z + t) * 4 + c, h]
        return remote(view, view, kl_send.at[t - 1], kl_recv.at[t - 1], sibling)

    def line_of(k):
        return jnp.where(k <= z, z - k, k)

    def plane(k, step):
        view = keys_buf.at[line_of(k) * 4 + c, h]
        index = 3 * k + step - 1
        device = (across(s, step), h)
        return remote(view, view, plane_send.at[index], plane_recv.at[index], device)

    def plane_in(k, step):
        view = keys_buf.at[line_of(k) * 4 + lax.rem(across(s, step), 4), h]
        index = 3 * k + step - 1
        return remote(view, view, plane_send.at[index], plane_recv.at[index], sibling)

    def share_keys(k):
        view = keys_buf.at[pl.ds(line_of(k) * 4, 4), h]
        return remote(view, view, share_keys_send.at[k], share_keys_recv.at[k], sibling)

    def share_keys_in(k):
        view = keys_buf.at[pl.ds(line_of(k) * 4, 4), 1 - h]
        return remote(view, view, share_keys_send.at[k], share_keys_recv.at[k], sibling)

    def starts_of(token):
        first = jnp.zeros_like(token)
        offset = jnp.full_like(token, req_offset_ref[0])
        end = req_len_ref[0]
        for r in range(1, req_len_ref.shape[0]):
            later = token >= end
            first = jnp.where(later, end, first)
            offset = jnp.where(later, req_offset_ref[r], offset)
            end = end + req_len_ref[r]
        return first, offset

    def turns(token):
        first, offset = starts_of(token)
        angle = (offset + token - first).astype(f32) * freq_ref[...]
        lane = iota(angle.shape, 1)
        sine = jnp.sin(angle)
        sine = jnp.where(lane < ROPE // 2, -sine, sine)
        rotary = lane < ROPE
        return jnp.where(rotary, jnp.cos(angle), 0.0), jnp.where(rotary, sine, 0.0)

    def spin(values, turn):
        lane = iota(values.shape, 1)
        other = jnp.where(
            lane < ROPE // 2,
            pltpu.roll(values, 128 - ROPE // 2, 1),
            pltpu.roll(values, ROPE // 2, 1),
        )
        return (values * turn[0] + other * turn[1]).astype(bf16)

    base = s * tok_rows
    rows = hidden_ref[pl.ds(pl.multiple_of(h * rows_half, rows_half), rows_half), :].astype(f32)
    inverse = lax.rsqrt(jnp.mean(rows * rows, axis=1, keepdims=True) + EPSILON)
    normed = (rows * inverse * gain_ref[...]).astype(bf16)
    full = lax.dot_general(normed, kv_ref[:KV_RANK], pair, preferred_element_type=f32)
    end = lax.dot_general(
        normed, kv_ref[KV_RANK + ROPE - 128 :], pair, preferred_element_type=f32
    )
    inverse = lax.rsqrt(jnp.mean(full * full, axis=1, keepdims=True) + EPSILON)
    keys_buf[s, h, :, :KV_RANK] = (full * inverse * kv_gain_ref[...]).astype(bf16)
    half_token = base + h * rows_half + iota((rows_half, 1), 0)
    key_rope = spin(pltpu.roll(end, ROPE, 1), turns(half_token))
    named = jnp.zeros((128, tok_rows), f32)
    place = iota(named.shape, 0) - ROPE
    for k in range(ids_ref.shape[0]):
        named = jnp.where(ids_ref[k : k + 1, :] == place, 1.0, named)
    row_pick = iota((rows_half, tok_rows), 1) == h * rows_half + iota((rows_half, tok_rows), 0)
    row_pick = jnp.where(row_pick, 1.0, 0.0).astype(bf16)
    mask = lax.dot_general(row_pick, named.astype(bf16), pair, preferred_element_type=f32)
    keys_buf[s, h, :, KV_RANK:] = (key_rope.astype(f32) + mask).astype(bf16)
    pl.semaphore_wait(barrier, len(peers))

    def key_ring(t):
        @pl.when((t >= 1) & (t <= z))
        def _():
            key_up_in(t).wait_recv()

        @pl.when((t <= z) & (z < 3))
        def _():
            key_up_move(t).start()

        @pl.when((t >= 1) & (t <= 3 - z))
        def _():
            key_low_in(t).wait_recv()

        @pl.when((t <= 3 - z) & (z > 0))
        def _():
            key_low_move(t).start()

        for step in (3, 1, 2):
            plane(t, step).start()

    def meet_keys(k):
        for step in (1, 2, 3):
            plane_in(k, step).wait_recv()
        share_keys(k).start()

    key_ring(0)
    token = base + iota((tok_rows, 1), 0)
    turn = turns(token)
    loads[0].wait()
    loads[1].wait()
    for two in range(heads // 2):
        left = queries[:, 384 * two : 384 * two + 128]
        middle = queries[:, 384 * two + 128 : 384 * two + 256].astype(f32)
        right = queries[:, 384 * two + 256 : 384 * two + 384].astype(f32)
        lane = iota(middle.shape, 1)
        turned = pltpu.roll(right, 64, 1)
        nope = jnp.where(lane < 64, pltpu.roll(middle, 64, 1), turned).astype(bf16)
        for odd, columns, rotary in ((0, left, middle), (1, nope, turned)):
            head = 2 * two + odd
            here = slice(head * tok_rows, (head + 1) * tok_rows)
            query[here, :KV_RANK] = jnp.dot(
                columns, key_up[head], preferred_element_type=f32
            ).astype(bf16)
            query[here, KV_RANK:] = spin(rotary, turn)
    peak[...] = jnp.full_like(peak, MASKED)
    total[...] = jnp.zeros_like(total)
    acc[...] = jnp.zeros_like(acc)
    first = jnp.concatenate([starts_of(token)[0]] * part_heads, axis=0)
    own = jnp.concatenate([token] * part_heads, axis=0)
    scale = math.log2(math.e) / math.sqrt(NOPE + ROPE)

    def attend(k, part_no):
        line = line_of(k)
        keys = keys_buf[pl.ds(line * 4, 4)].reshape(tile_keys, keys_buf.shape[3])
        here = slice(part_no * part_rows, (part_no + 1) * part_rows)
        scores = scale * lax.dot_general(query[here, :], keys, pair, preferred_element_type=f32)
        index = line * tile_keys + iota(scores.shape, 1)
        scores = jnp.where((index <= own) & (index >= first), scores, MASKED)
        old = peak[part_no, :, :1]
        new = jnp.maximum(old, jnp.max(scores, axis=1, keepdims=True))
        terms = jnp.exp2(scores - new)
        fade = jnp.exp2(old - new)
        total[part_no, :, :1] = total[part_no, :, :1] * fade + jnp.sum(
            terms, axis=1, keepdims=True
        )
        peak[part_no, :, :1] = new
        acc[part_no] = acc[part_no] * fade + jnp.dot(
            terms.astype(bf16), keys[:, :KV_RANK], preferred_element_type=f32
        )

    key_ring(1)
    meet_keys(0)

    @pl.loop(0, 4)
    def _(k):
        share_keys_in(k).wait_recv()

        @pl.when(k <= z)
        def _():
            attend(k, 0)

        @pl.when(k <= 1)
        def _():
            key_ring(k + 2)

        @pl.when(k <= 2)
        def _():
            meet_keys(k + 1)

        @pl.when(k <= z)
        def _():
            attend(k, 1)

    loads[2].wait()
    loads[3].wait()
    for head in range(heads):
        part_no, member = head // part_heads, head % part_heads
        here = slice(member * tok_rows, (member + 1) * tok_rows)
        attended = (acc[part_no, here, :] / total[part_no, here, :1]).astype(bf16)
        heads_buf[:, head * V_HEAD : (head + 1) * V_HEAD] = jnp.dot(
            attended, value_up[head], preferred_element_type=f32
        ).astype(bf16)
    cols = hidden_ref.shape[1]
    half = cols // 2

    def swap(piece):
        return remote(
            attn_buf.at[piece],
            attn_in.at[piece],
            swap_send.at[piece],
            swap_recv.at[piece],
            sibling,
        )

    for piece in range(2):
        here = slice(piece * half, (piece + 1) * half)
        attn_buf[piece] = jnp.dot(
            heads_buf[...], out_proj[:, here], preferred_element_type=f32
        ).astype(bf16)
        swap(piece).start()
    def up(t):
        view = x_buf.at[z - t]
        device = (line_place(lax.rem(z + 1, 4), s), h)
        return remote(view, view, up_send.at[t], up_recv.at[t], device)

    def up_in(t):
        view = x_buf.at[z - t]
        return remote(view, view, up_send.at[t - 1], up_recv.at[t - 1], sibling)

    def low(t):
        view = x_buf.at[z + t]
        device = (line_place(lax.rem(z + 3, 4), s), h)
        return remote(view, view, down_send.at[t], down_recv.at[t], device)

    def low_in(t):
        view = x_buf.at[z + t]
        return remote(view, view, down_send.at[t - 1], down_recv.at[t - 1], sibling)

    def go(k, step):
        other = across(s, step)
        index = 3 * k + step - 1
        return remote(
            stage.at[k, lax.rem(other, 4)],
            rows_in.at[k, h, c],
            go_send.at[index],
            go_recv.at[index],
            (other, h),
        )

    def go_in(k, step):
        index = 3 * k + step - 1
        view = rows_in.at[k, h, lax.rem(across(s, step), 4)]
        return remote(view, view, go_send.at[index], go_recv.at[index], sibling)

    def share(k, step):
        view = rows_in.at[k, h, lax.rem(across(s, step), 4)]
        index = 4 * k + step
        return remote(view, view, share_send.at[index], share_recv.at[index], sibling)

    def share_in(k, step):
        view = rows_in.at[k, 1 - h, lax.rem(across(s, step), 4)]
        index = 4 * k + step
        return remote(view, view, share_send.at[index], share_recv.at[index], sibling)

    def part(k):
        return remote(res.at[k, 1 - h], sib_in.at[k], part_send.at[k], part_recv.at[k], sibling)

    def ret(k, step):
        other = across(s, step)
        index = 3 * k + step - 1
        return remote(
            res.at[k, h, lax.rem(other, 4)],
            ret_in.at[k, c],
            ret_send.at[index],
            ret_recv.at[index],
            (other, h),
        )

    def ret_back(k, step):
        index = 3 * k + step - 1
        view = ret_in.at[k, lax.rem(across(s, step), 4)]
        return remote(view, view, ret_send.at[index], ret_recv.at[index], sibling)

    def home(k):
        owner = (line_place(turn_line(z, k), s), h)
        return remote(z_out.at[k], z_in.at[z], home_send.at[k], home_recv.at[z], owner)

    def home_in(back):
        line = lax.rem(z + back, 4)
        return remote(z_in.at[line], z_in.at[line], home_send.at[0], home_recv.at[line], sibling)

    slots = stage.shape[2]
    expert_count = router_ref.shape[0]
    four = 4 * slots
    before = (iota((tok_rows, tok_rows), 0) < iota((tok_rows, tok_rows), 1)).astype(bf16)
    after = (iota((tok_rows, tok_rows), 0) > iota((tok_rows, tok_rows), 1)).astype(bf16)

    def one_hot(flags):
        return jnp.where(flags, 1.0, 0.0).astype(bf16)

    def tail_of(block):
        return keys_buf[block, :, :, KV_RANK:].reshape(tok_rows, 128)

    def prepare(k):
        line = turn_line(z, k)
        tail = tail_of(line * 4 + c)
        shape = (four, 128)
        named = one_hot(iota(shape, 1) == ROPE + 4 * z + lax.div(iota(shape, 0), slots))
        slot = lax.rem(iota((four, tok_rows), 0), slots).astype(f32)
        member = lax.dot_general(named, tail, pair, preferred_element_type=f32)
        rank = jnp.dot(member.astype(bf16), before, preferred_element_type=f32)
        pick_buf[k] = one_hot((rank == slot) & (member > 0.0))
        shape = (128, four)
        named = one_hot(iota(shape, 0) == ROPE + 4 * z + lax.div(iota(shape, 1), slots))
        slot = lax.rem(iota((tok_rows, four), 1), slots).astype(f32)
        member = jnp.dot(tail, named, preferred_element_type=f32)
        rank = jnp.dot(after, member.astype(bf16), preferred_element_type=f32)
        place_buf[k] = one_hot((rank == slot) & (member > 0.0))
        named = one_hot(iota((slots, 128), 1) == ROPE + s)
        slot = iota((slots, tok_rows), 0).astype(f32)
        for block in range(4):
            tail = tail_of(line * 4 + block)
            member = lax.dot_general(named, tail, pair, preferred_element_type=f32)
            rank = jnp.dot(member.astype(bf16), before, preferred_element_type=f32)
            mine = one_hot((rank == slot) & (member > 0.0))
            chosen = jnp.dot(mine, tail, preferred_element_type=f32)
            known = iota((slots, 128), 1)
            known = (known >= ROPE) & (known < ROPE + expert_count)
            chosen_buf[k, block * slots : (block + 1) * slots] = jnp.where(known, chosen, 0.0)

    prepare(0)
    router = router_ref[...]
    high = router.astype(bf16)
    rest = router - high.astype(f32)
    middle = rest.astype(bf16)
    last = (rest - middle.astype(f32)).astype(bf16)
    top_pad = jnp.zeros((ROPE, cols), bf16)
    low_pad = jnp.zeros((128 - ROPE - 3 * expert_count, cols), bf16)
    router_buf[...] = jnp.concatenate([top_pad, high, middle, last, low_pad], axis=0)

    for piece in range(2):
        swap(piece).wait_recv()

    def joined(piece):
        here = slice(piece * half, (piece + 1) * half)
        both = attn_buf[piece].astype(f32) + attn_in[piece].astype(f32)
        return hidden_ref[:, here].astype(f32) + both

    sums = [joined(0), joined(1)]
    square = sums[0] * sums[0] + sums[1] * sums[1]
    inverse = lax.rsqrt(jnp.sum(square, axis=1, keepdims=True) / cols + EPSILON)
    mine = jnp.where(h == 0, sums[0], sums[1])
    mixed[...] = mine
    gain = ffn_gain_ref[...]
    own_gain = jnp.where(h == 0, gain[:, :half], gain[:, half:])
    x_buf[z] = (mine * inverse * own_gain).astype(bf16)

    def ring(t):
        @pl.when((t >= 1) & (t <= z))
        def _():
            up_in(t).wait_recv()

        @pl.when((t <= z) & (z < 3))
        def _():
            up(t).start()

        @pl.when((t >= 1) & (t <= 3 - z))
        def _():
            low_in(t).wait_recv()

        @pl.when((t <= 3 - z) & (z > 0))
        def _():
            low(t).start()

    def pick(k):
        rows = jnp.dot(pick_buf[k], x_buf[turn_line(z, k)], preferred_element_type=f32)
        stage[k] = rows.astype(bf16).reshape(4, slots, half)
        for step in (3, 1, 2):
            go(k, step).start()
        rows_in[k, h, c] = stage[k, c]
        share(k, 0).start()

    def meet_rows(k):
        for step in (1, 2, 3):
            go_in(k, step).wait_recv()
            share(k, step).start()

    def work(k):
        for step in range(4):
            share_in(k, step).wait_recv()
        rows = jnp.concatenate(
            [rows_in[k, 0].reshape(four, half), rows_in[k, 1].reshape(four, half)], axis=1
        )
        logit = lax.dot_general(rows, router_buf[...], pair, preferred_element_type=f32)
        logit = logit + (
            pltpu.roll(logit, 128 - expert_count, 1) + pltpu.roll(logit, 128 - 2 * expert_count, 1)
        )
        score = 1.0 / (1.0 + jnp.exp(-logit))
        chosen = jnp.where(chosen_buf[k] > 0.0, score, 0.0)
        own = jnp.where(iota(chosen.shape, 1) == ROPE + s, chosen, 0.0)
        own = jnp.sum(own, axis=1, keepdims=True)
        every = jnp.sum(chosen, axis=1, keepdims=True)
        weight = ROUTE_SCALE * own / jnp.where(every > 0.0, every, 1.0)
        gate = lax.dot_general(rows, gate_up[0], pair, preferred_element_type=f32)
        rise = lax.dot_general(rows, gate_up[1], pair, preferred_element_type=f32)
        act = (gate / (1.0 + jnp.exp(-gate)) * rise * weight).astype(bf16)
        out = jnp.dot(act, down[...], preferred_element_type=f32).astype(bf16)
        res[k, 0] = out[:, :half].reshape(4, slots, half)
        res[k, 1] = out[:, half:].reshape(4, slots, half)
        part(k).start()

    def send_back(k):
        part(k).wait_recv()
        res[k, h] = (res[k, h].astype(f32) + sib_in[k].astype(f32)).astype(bf16)
        for step in (3, 1, 2):
            ret(k, step).start()
        ret_in[k, c] = res[k, h, c]

    def place(k):
        for step in (1, 2, 3):
            ret_back(k, step).wait_recv()
        return jnp.dot(place_buf[k], ret_in[k].reshape(four, half), preferred_element_type=f32)

    def decode_rows():
        shape = (DEC_SLOTS * BLOCK, slot_ref.shape[1])
        wanted = (2 * s + h) * DEC_SLOTS + lax.div(iota(shape, 0), BLOCK)
        named = one_hot(slot_ref[...] == wanted)
        span = keys_buf.shape[0] * tok_rows
        shape = (slot_ref.shape[1], span)
        spread = one_hot(lax.div(iota(shape, 1), BLOCK) == iota(shape, 0))
        blocks = jnp.dot(named, spread, preferred_element_type=f32)
        shape = (DEC_SLOTS * BLOCK, span)
        same = lax.rem(iota(shape, 1), BLOCK) == lax.rem(iota(shape, 0), BLOCK)
        picked = one_hot(same & (blocks > 0.0))
        return jnp.dot(
            picked, keys_buf[...].reshape(span, keys_buf.shape[3]), preferred_element_type=f32
        ).astype(bf16)

    @pl.loop(0, 6)
    def _(t):
        @pl.when(t <= 3)
        def _():
            ring(t)
            pick(t)

        @pl.when(t == 0)
        def _():
            @pl.loop(1, 4)
            def _(k):
                prepare(k)

        @pl.when(t == 1)
        def _():
            loads[4].wait()
            loads[5].wait()

        @pl.when((t >= 1) & (t <= 4))
        def _():
            meet_rows(t - 1)

        @pl.when(t >= 3)
        def _():
            send_back(t - 2)

        @pl.when((t >= 1) & (t <= 4))
        def _():
            work(t - 1)

    send_back(0)

    decode_ref[...] = decode_rows()

    @pl.loop(1, 4)
    def _(k):
        z_out[k] = place(k).astype(bf16)
        home(k).start()

    result = mixed[...] + place(0)
    for back in (1, 2, 3):
        home_in(back).wait_recv()
        result = result + z_in[lax.rem(z + back, 4)].astype(f32)
    out_ref[...] = result.astype(out_ref.dtype)
    for piece in range(2):
        swap(piece).wait_send()

    @pl.loop(0, 4)
    def _(k):
        @pl.when((k <= z) & (z < 3))
        def _():
            up(k).wait_send()

        @pl.when((k <= 3 - z) & (z > 0))
        def _():
            low(k).wait_send()

        for step in (1, 2, 3):
            go(k, step).wait_send()
            ret(k, step).wait_send()
        for step in range(4):
            share(k, step).wait_send()
        part(k).wait_send()

        @pl.when(k > 0)
        def _():
            home(k).wait_send()

    @pl.loop(0, 4)
    def _(k):
        @pl.when((k <= z) & (z < 3))
        def _():
            key_up_move(k).wait_send()

        @pl.when((k <= 3 - z) & (z > 0))
        def _():
            key_low_move(k).wait_send()

        for step in (1, 2, 3):
            plane(k, step).wait_send()
        share_keys(k).wait_send()


def layer(
    req_len,
    req_offset,
    hidden,
    attn_gain,
    kv_down,
    kv_gain,
    expert_ids,
    decode_slot,
    ffn_gain,
    router,
    queries,
    key_up,
    value_up,
    out_proj,
    gate_up,
    down,
    seq_count,
):
    tok_rows, cols = hidden.shape
    half = cols // 2
    heads = key_up.shape[0]
    width = KV_RANK + 128
    slots = max(2, tok_rows * TOP * 4 // (3 * router.shape[1]))
    lanes = np.arange(128) % (ROPE // 2)
    frequency = np.exp(-math.log(ROPE_BASE) * lanes * (2.0 / ROPE)).astype(np.float32)[None, :]
    bf16, f32 = jnp.bfloat16, jnp.float32
    vmem = pl.BlockSpec(memory_space=pltpu.VMEM)
    smem = pl.BlockSpec(memory_space=pltpu.SMEM)
    hbm = pl.BlockSpec(memory_space=pl.ANY)
    dma = pltpu.SemaphoreType.DMA
    part_rows = heads * tok_rows // 2
    sizes = [6] + [4] * 4 + [12] * 2 + [4] * 2 + [2] * 2
    sizes += [4] * 4 + [12] * 2 + [16] * 2 + [4] * 2 + [12] * 2 + [4] * 2
    return pl.pallas_call(
        layer_kernel,
        out_shape=(
            jax.ShapeDtypeStruct((tok_rows, half), bf16),
            jax.ShapeDtypeStruct((DEC_SLOTS * BLOCK, width), bf16),
        ),
        in_specs=[smem] * 2 + [vmem] * 9 + [hbm] * 6,
        out_specs=(vmem, vmem),
        scratch_shapes=[
            pltpu.VMEM((seq_count, 2, tok_rows // 2, width), bf16),
            pltpu.VMEM(queries.shape, bf16),
            pltpu.VMEM(key_up.shape, bf16),
            pltpu.VMEM(value_up.shape, bf16),
            pltpu.VMEM(out_proj.shape, bf16),
            pltpu.VMEM((heads * tok_rows, width), bf16),
            pltpu.VMEM((2, part_rows, KV_RANK), f32),
            pltpu.VMEM((2, part_rows, 128), f32),
            pltpu.VMEM((2, part_rows, 128), f32),
            pltpu.VMEM((tok_rows, heads * V_HEAD), bf16),
            pltpu.VMEM((2, tok_rows, half), bf16),
            pltpu.VMEM((2, tok_rows, half), bf16),
            pltpu.VMEM((tok_rows, half), f32),
            pltpu.VMEM((4, tok_rows, half), bf16),
            pltpu.VMEM((4, 4, slots, half), bf16),
            pltpu.VMEM((4, 2, 4, slots, half), bf16),
            pltpu.VMEM((4, 2, 4, slots, half), bf16),
            pltpu.VMEM((4, 4, slots, half), bf16),
            pltpu.VMEM((4, 4, slots, half), bf16),
            pltpu.VMEM((4, tok_rows, half), bf16),
            pltpu.VMEM((4, tok_rows, half), bf16),
            pltpu.VMEM((4, 4 * slots, tok_rows), bf16),
            pltpu.VMEM((4, tok_rows, 4 * slots), bf16),
            pltpu.VMEM((4, 4 * slots, 128), f32),
            pltpu.VMEM((128, cols), bf16),
            pltpu.VMEM(gate_up.shape, bf16),
            pltpu.VMEM(down.shape, bf16),
        ]
        + [dma((size,)) for size in sizes],
        compiler_params=pltpu.CompilerParams(
            collective_id=0, has_side_effects=True, vmem_limit_bytes=60 * 1024 * 1024
        ),
    )(
        req_len,
        req_offset,
        jnp.asarray(frequency),
        hidden,
        attn_gain[None, :],
        kv_down.T,
        kv_gain[None, :],
        expert_ids.T,
        decode_slot[None, :],
        ffn_gain[None, :],
        router.T,
        queries,
        key_up,
        value_up,
        out_proj,
        gate_up,
        down,
    )


def body(
    hidden,
    queries,
    req_len,
    req_offset,
    expert_ids,
    decode_slot,
    attn_gain,
    kv_down,
    kv_gain,
    key_up,
    value_up,
    out_proj,
    ffn_gain,
    router,
    expert_gate_up,
    expert_down,
):
    head_count = lax.axis_size("head")
    seq_place = lax.axis_index("seq")
    head_place = lax.axis_index("head")
    tok_rows = hidden.shape[0]
    heads_here = key_up.shape[0]
    my_index = seq_place * tok_rows + jnp.arange(tok_rows, dtype=jnp.int32)
    my_request = request_of(req_len, my_index)
    my_turn = angles(position_of(req_len, req_offset, my_index), ROPE)
    normed = rms_rows(hidden, attn_gain).astype(jnp.bfloat16)
    head_view = queries.reshape(tok_rows, heads_here, NOPE + ROPE)
    query_rope = rotate(head_view[:, :, NOPE:], my_turn[:, None, :]).astype(jnp.bfloat16)
    query_latent = jnp.einsum(
        "thn,hnc->thc", head_view[:, :, :NOPE], key_up, preferred_element_type=jnp.float32
    ).astype(jnp.bfloat16)
    query_rows = tok_rows * heads_here
    flat_latent = query_latent.reshape(query_rows, KV_RANK)
    flat_rope = query_rope.reshape(query_rows, ROPE)
    row_token = jnp.repeat(my_index, heads_here)
    row_request = jnp.repeat(my_request, heads_here)
    score_scale = 1.0 / math.sqrt(NOPE + ROPE)
    my_device = seq_place * head_count + head_place
    slot_ids = my_device * DEC_SLOTS + jnp.arange(DEC_SLOTS, dtype=jnp.int32)
    block_ids = jnp.arange(decode_slot.shape[0], dtype=jnp.int32)
    slot_match = decode_slot[None, :] == slot_ids[:, None]
    source_block = jnp.sum(jnp.where(slot_match, block_ids[None, :], 0), axis=1)
    slot_filled = jnp.any(slot_match, axis=1)
    kv_full = jnp.dot(normed, kv_down, preferred_element_type=jnp.float32)
    latent = rms_rows(kv_full[:, :KV_RANK], kv_gain).astype(jnp.bfloat16)
    key_rope = rotate(kv_full[:, KV_RANK:], my_turn).astype(jnp.bfloat16)
    run_peak = jnp.full((query_rows,), MASKED, jnp.float32)
    run_total = jnp.zeros((query_rows,), jnp.float32)
    run_acc = jnp.zeros((query_rows, KV_RANK), jnp.float32)
    expert_count = router.shape[1]
    expert_axis = jnp.arange(expert_count, dtype=jnp.int32)
    seq_count = lax.axis_size("seq")
    fast = seq_count == 16 and head_count == 2 and expert_count == 16
    if fast:
        output, slot_rows = layer(
            req_len,
            req_offset,
            hidden,
            attn_gain,
            kv_down,
            kv_gain,
            expert_ids,
            decode_slot,
            ffn_gain,
            router,
            queries,
            key_up,
            value_up,
            out_proj,
            jnp.swapaxes(expert_gate_up[0], 1, 2),
            expert_down[0],
            seq_count,
        )
        decode_latent = slot_rows[:, :KV_RANK].reshape(DEC_SLOTS, BLOCK, KV_RANK)
        decode_rope = slot_rows[:, KV_RANK : KV_RANK + ROPE].reshape(DEC_SLOTS, BLOCK * ROPE)
        return (output, decode_latent, decode_rope)
    else:
        piece_latent = lax.all_gather(latent, "seq", axis=0, tiled=True)
        piece_rope = lax.all_gather(key_rope, "seq", axis=0, tiled=True)
    piece_rows = piece_latent.shape[0]
    block_width = key_width(piece_rows)

    def key_block(block_no, loop_state):
        peak_now, total_now, acc_now = loop_state
        offset_rows = block_no * block_width
        block_latent = lax.dynamic_slice_in_dim(piece_latent, offset_rows, block_width, 0)
        block_rope = lax.dynamic_slice_in_dim(piece_rope, offset_rows, block_width, 0)
        key_index = offset_rows + jnp.arange(block_width, dtype=jnp.int32)
        key_request = request_of(req_len, key_index)
        contract = (((1,), (1,)), ((), ()))
        scores = lax.dot_general(
            flat_latent, block_latent, contract, preferred_element_type=jnp.float32
        )
        scores = (
            scores
            + lax.dot_general(flat_rope, block_rope, contract, preferred_element_type=jnp.float32)
        ) * score_scale
        allowed = (key_index[None, :] <= row_token[:, None]) & (
            key_request[None, :] == row_request[:, None]
        )
        scores = jnp.where(allowed, scores, MASKED)
        new_peak = jnp.maximum(peak_now, jnp.max(scores, axis=1))
        exp_terms = jnp.where(allowed, jnp.exp(scores - new_peak[:, None]), 0.0)
        fade_factor = jnp.exp(peak_now - new_peak)
        total_now = total_now * fade_factor + jnp.sum(exp_terms, axis=1)
        acc_now = acc_now * fade_factor[:, None] + jnp.dot(
            exp_terms.astype(jnp.bfloat16), block_latent, preferred_element_type=jnp.float32
        )
        return (new_peak, total_now, acc_now)

    run_peak, run_total, run_acc = lax.fori_loop(
        0, piece_rows // block_width, key_block, (run_peak, run_total, run_acc)
    )
    block_count = piece_rows // BLOCK
    pick_matrix = (
        source_block[:, None] == jnp.arange(block_count, dtype=jnp.int32)[None, :]
    ) & slot_filled[:, None]
    pick_matrix = pick_matrix.astype(jnp.bfloat16)
    slot_latent = jnp.dot(
        pick_matrix,
        piece_latent.reshape(block_count, BLOCK * KV_RANK),
        preferred_element_type=jnp.float32,
    )
    slot_rope = jnp.dot(
        pick_matrix,
        piece_rope.reshape(block_count, BLOCK * ROPE),
        preferred_element_type=jnp.float32,
    )
    folded = (run_peak, run_total, run_acc, slot_latent, slot_rope)
    run_total = folded[1]
    run_acc = folded[2]
    slot_latent = folded[3]
    slot_rope = folded[4]
    attended = (
        (run_acc / run_total[:, None]).astype(jnp.bfloat16).reshape(tok_rows, heads_here, KV_RANK)
    )
    head_out = jnp.einsum(
        "thc,hcv->thv", attended, value_up, preferred_element_type=jnp.float32
    ).astype(jnp.bfloat16)
    attn_part = jnp.dot(
        head_out.reshape(tok_rows, heads_here * V_HEAD),
        out_proj,
        preferred_element_type=jnp.float32,
    )
    decode_latent = slot_latent.astype(jnp.bfloat16).reshape(DEC_SLOTS, BLOCK, KV_RANK)
    decode_rope = slot_rope.astype(jnp.bfloat16)
    mixed_rows = hidden.astype(jnp.float32) + lax.psum(
        attn_part.astype(jnp.bfloat16), "head"
    ).astype(jnp.float32)
    moe_in = rms_rows(mixed_rows, ffn_gain).astype(jnp.bfloat16)
    capacity = max(2, tok_rows * TOP * 4 // (3 * expert_count))
    gate_score = jax.nn.sigmoid(
        jnp.dot(moe_in.astype(jnp.float32), router, precision=lax.Precision.HIGHEST)
    )
    id_match = expert_ids[:, :, None] == expert_axis[None, None, :]
    chosen = jnp.sum(jnp.where(id_match, gate_score[:, None, :], 0.0), axis=2)
    gate_weight = ROUTE_SCALE * chosen / jnp.sum(chosen, axis=1, keepdims=True)
    flat_ids = expert_ids.reshape(-1)
    one_hot = (flat_ids[:, None] == expert_axis[None, :]).astype(jnp.int32)
    earlier = ranks(one_hot.T.astype(jnp.bfloat16)).T
    slot_rank = jnp.sum(earlier * one_hot, axis=1)
    flat_slot = flat_ids * capacity + slot_rank
    owner_token = jnp.repeat(jnp.arange(tok_rows, dtype=jnp.int32), TOP)
    slot_token = jnp.zeros((expert_count * capacity,), jnp.int32).at[flat_slot].set(owner_token)
    slot_used = jnp.zeros((expert_count * capacity,), jnp.bool_).at[flat_slot].set(True)
    send_rows = jnp.where(
        slot_used[:, None], moe_in[slot_token], jnp.zeros((), jnp.bfloat16)
    ).reshape(expert_count, capacity, D)
    gate_up_local = expert_gate_up[0]
    down_local = expert_down[0]
    quarter_cols = D // head_count
    arrived = lax.all_to_all(send_rows, "seq", split_axis=0, concat_axis=0, tiled=True)
    sources, item_count, width_cols = arrived.shape
    flat_rows = arrived.reshape(sources * item_count, width_cols)
    gate_part = jnp.dot(flat_rows, gate_up_local[0], preferred_element_type=jnp.float32)
    up_part = jnp.dot(flat_rows, gate_up_local[1], preferred_element_type=jnp.float32)
    activated = (jax.nn.silu(gate_part) * up_part).astype(jnp.bfloat16)
    part_out = (
        jnp.dot(activated, down_local, preferred_element_type=jnp.float32)
        .astype(jnp.bfloat16)
        .reshape(sources, item_count, width_cols)
    )
    returned = lax.all_to_all(part_out, "seq", split_axis=0, concat_axis=0, tiled=True)
    back_cols = returned.shape[2]
    picked = returned.reshape(expert_count * capacity, back_cols)[flat_slot].reshape(
        tok_rows, TOP, back_cols
    )
    weighted = jnp.sum(picked.astype(jnp.float32) * gate_weight[:, :, None], axis=1)
    moe_out = lax.psum_scatter(
        weighted.astype(jnp.bfloat16), "head", scatter_dimension=1, tiled=True
    ).astype(jnp.float32)
    residual_part = lax.dynamic_slice_in_dim(mixed_rows, head_place * quarter_cols, quarter_cols, 1)
    output = (residual_part + moe_out).astype(jnp.bfloat16)
    return (output, decode_latent, decode_rope)


def solution(mesh):
    placed = (
        P("seq", None),
        P("seq", "head"),
        P(),
        P(),
        P("seq", None),
        P(),
        P(),
        P(),
        P(),
        P("head", None, None),
        P("head", None, None),
        P("head", None),
        P(),
        P(),
        P("seq", None, None, "head"),
        P("seq", "head", None),
    )
    return jax.shard_map(
        body,
        mesh=mesh,
        in_specs=placed,
        out_specs=(P("seq", "head"), P(("seq", "head"), None, None), P(("seq", "head"), None)),
        check_vma=False,
    )
```

```python
import functools
import math

import jax
import jax.numpy as jnp
import numpy as np
from jax import lax
from jax.experimental import pallas as pl
from jax.experimental.pallas import tpu as pltpu
from jax.sharding import PartitionSpec as P

D = 2048
NOPE = 128
ROPE = 64
V_HEAD = 128
KV_RANK = 512
TOP = 6
BLOCK = 16
DEC_SLOTS = 4


ROPE_BASE = 50000.0
ROUTE_SCALE = 2.446
EPSILON = 1e-06
MASKED = -1e30
PIECES = 2


def rms_rows(values, scale_gain):
    values = values.astype(jnp.float32)
    inverse = lax.rsqrt(jnp.mean(values * values, axis=-1, keepdims=True) + EPSILON)
    return values * inverse * scale_gain


def angles(position, rope_width):
    half_width = rope_width // 2
    freq_steps = jnp.arange(half_width).astype(jnp.float32) * (2.0 / rope_width)
    frequency = jnp.exp(-math.log(ROPE_BASE) * freq_steps)
    return position.astype(jnp.float32)[:, None] * frequency[None, :]


def rotate(values, rot_angle):
    half_width = values.shape[-1] // 2
    first_half = values[..., :half_width].astype(jnp.float32)
    second_half = values[..., half_width:].astype(jnp.float32)
    cosine = jnp.cos(rot_angle)
    sine_part = jnp.sin(rot_angle)
    return jnp.concatenate(
        [
            first_half * cosine - second_half * sine_part,
            first_half * sine_part + second_half * cosine,
        ],
        axis=-1,
    )


def running(lengths):
    index = jnp.arange(lengths.shape[0])
    return jnp.sum(jnp.where(index[None, :] <= index[:, None], lengths[None, :], 0), axis=1)


def ranks(member):
    count = member.shape[-1]
    index = jnp.arange(count)
    before = (index[:, None] < index[None, :]).astype(jnp.bfloat16)
    return jnp.dot(member, before, preferred_element_type=jnp.float32).astype(jnp.int32)


def request_of(req_len, token_index):
    req_ends = running(req_len)
    return jnp.sum((token_index[:, None] >= req_ends[None, :]).astype(jnp.int32), axis=1)


def position_of(req_len, req_offset, token_index):
    request = request_of(req_len, token_index)
    req_ends = running(req_len)
    starts = req_ends - req_len
    member = request[:, None] == jnp.arange(req_len.shape[0])[None, :]
    start_at = jnp.sum(jnp.where(member, starts[None, :], 0), axis=1)
    offset = jnp.sum(jnp.where(member, req_offset[None, :], 0), axis=1)
    return offset + token_index - start_at


def key_width(piece_rows):
    for option_width in (1024, 512, 256, 128):
        return option_width
    return piece_rows


MESH = pl.DeviceIdType.MESH


def flip(place, step):
    return place + step * (1 - 2 * lax.rem(lax.div(place, step), 2))


def line_place(line, s):
    return line * 4 + lax.rem(s, 4)


def across(s, step):
    if step & 1:
        s = flip(s, 1)
    if step & 2:
        s = flip(s, 2)
    return s


def turn_line(z, k):
    upper = lax.div(z, 2)
    near = z + upper * (3 - 2 * z)
    late = lax.div(k, 2)
    line = late * k + (1 - late) * (near + k * (1 - 2 * near))
    return line + upper * (3 - 2 * line)


def layer_kernel(
    req_len_ref,
    req_offset_ref,
    freq_ref,
    hidden_ref,
    gain_ref,
    kv_gain_ref,
    ids_ref,
    slot_ref,
    ffn_gain_ref,
    router_ref,
    kv_hbm,
    queries_hbm,
    key_up_hbm,
    value_up_hbm,
    out_proj_hbm,
    gate_up_hbm,
    down_hbm,
    out_ref,
    latent_ref,
    rope_ref,
    kv_buf,
    keys_buf,
    queries,
    key_up,
    value_up,
    out_proj,
    query,
    acc,
    peak,
    total,
    heads_buf,
    attn_buf,
    attn_in,
    mixed,
    x_buf,
    stage,
    rows_in,
    res,
    sib_in,
    ret_in,
    z_out,
    z_in,
    pick_buf,
    place_buf,
    chosen_buf,
    router_buf,
    gate_up,
    down,
    load_sem,
    ku_send,
    ku_recv,
    kl_send,
    kl_recv,
    plane_send,
    plane_recv,
    share_keys_send,
    share_keys_recv,
    swap_send,
    swap_recv,
    up_send,
    up_recv,
    down_send,
    down_recv,
    go_send,
    go_recv,
    share_send,
    share_recv,
    part_send,
    part_recv,
    ret_send,
    ret_recv,
    home_send,
    home_recv,
):
    s, h = lax.axis_index("seq"), lax.axis_index("head")
    z, c = lax.div(s, 4), lax.rem(s, 4)
    bf16, f32 = jnp.bfloat16, jnp.float32
    pair = (((1,), (1,)), ((), ()))
    tok_rows = hidden_ref.shape[0]
    rows_half = tok_rows // 2
    heads = key_up.shape[0]
    part_heads = heads // 2
    part_rows = part_heads * tok_rows
    tile_keys = 4 * tok_rows
    sibling = (s, 1 - h)
    pairs = [(queries_hbm, queries), (key_up_hbm, key_up)]
    pairs += [(value_up_hbm, value_up), (out_proj_hbm, out_proj)]
    pairs += [(gate_up_hbm, gate_up), (down_hbm, down)]
    pairs += [(kv_hbm, kv_buf)]
    loads = [pltpu.make_async_copy(*both, load_sem.at[i]) for i, both in enumerate(pairs)]
    for index in (6, 0, 1):
        loads[index].start()

    barrier = pltpu.get_barrier_semaphore()
    peers = [(line_place(lax.rem(z + back, 4), s), h) for back in range(1, 4)]
    peers += [(across(s, step), h) for step in range(1, 4)] + [sibling]
    for peer in peers:
        pl.semaphore_signal(barrier, inc=1, device_id=peer, device_id_type=MESH)

    def iota(shape, dim):
        return lax.broadcasted_iota(jnp.int32, shape, dim)

    def remote(src, dst, send, recv, device):
        return pltpu.make_async_remote_copy(
            src_ref=src,
            dst_ref=dst,
            send_sem=send,
            recv_sem=recv,
            device_id=device,
            device_id_type=MESH,
        )

    def key_up_move(t):
        view = keys_buf.at[(z - t) * 4 + c, h]
        device = (line_place(lax.rem(z + 1, 4), s), h)
        return remote(view, view, ku_send.at[t], ku_recv.at[t], device)

    def key_up_in(t):
        view = keys_buf.at[(z - t) * 4 + c, h]
        return remote(view, view, ku_send.at[t - 1], ku_recv.at[t - 1], sibling)

    def key_low_move(t):
        view = keys_buf.at[(z + t) * 4 + c, h]
        device = (line_place(lax.rem(z + 3, 4), s), h)
        return remote(view, view, kl_send.at[t], kl_recv.at[t], device)

    def key_low_in(t):
        view = keys_buf.at[(z + t) * 4 + c, h]
        return remote(view, view, kl_send.at[t - 1], kl_recv.at[t - 1], sibling)

    def line_of(k):
        return jnp.where(k <= z, z - k, k)

    def plane(k, step):
        view = keys_buf.at[line_of(k) * 4 + c, h]
        index = 3 * k + step - 1
        device = (across(s, step), h)
        return remote(view, view, plane_send.at[index], plane_recv.at[index], device)

    def plane_in(k, step):
        view = keys_buf.at[line_of(k) * 4 + lax.rem(across(s, step), 4), h]
        index = 3 * k + step - 1
        return remote(view, view, plane_send.at[index], plane_recv.at[index], sibling)

    def share_keys(k):
        view = keys_buf.at[pl.ds(line_of(k) * 4, 4), h]
        return remote(view, view, share_keys_send.at[k], share_keys_recv.at[k], sibling)

    def share_keys_in(k):
        view = keys_buf.at[pl.ds(line_of(k) * 4, 4), 1 - h]
        return remote(view, view, share_keys_send.at[k], share_keys_recv.at[k], sibling)

    def starts_of(token):
        first = jnp.zeros_like(token)
        offset = jnp.full_like(token, req_offset_ref[0])
        end = req_len_ref[0]
        for r in range(1, req_len_ref.shape[0]):
            later = token >= end
            first = jnp.where(later, end, first)
            offset = jnp.where(later, req_offset_ref[r], offset)
            end = end + req_len_ref[r]
        return first, offset

    def turns(token):
        first, offset = starts_of(token)
        angle = (offset + token - first).astype(f32) * freq_ref[...]
        lane = iota(angle.shape, 1)
        sine = jnp.sin(angle)
        sine = jnp.where(lane < ROPE // 2, -sine, sine)
        rotary = lane < ROPE
        return jnp.where(rotary, jnp.cos(angle), 0.0), jnp.where(rotary, sine, 0.0)

    def spin(values, turn):
        lane = iota(values.shape, 1)
        other = jnp.where(
            lane < ROPE // 2,
            pltpu.roll(values, 128 - ROPE // 2, 1),
            pltpu.roll(values, ROPE // 2, 1),
        )
        return (values * turn[0] + other * turn[1]).astype(bf16)

    base = s * tok_rows
    rows = hidden_ref[pl.ds(pl.multiple_of(h * rows_half, rows_half), rows_half), :].astype(f32)
    inverse = lax.rsqrt(jnp.mean(rows * rows, axis=1, keepdims=True) + EPSILON)
    normed = (rows * inverse * gain_ref[...]).astype(bf16)
    loads[6].wait()
    full = lax.dot_general(normed, kv_buf[:KV_RANK], pair, preferred_element_type=f32)
    end = lax.dot_general(
        normed, kv_buf[KV_RANK + ROPE - 128 :], pair, preferred_element_type=f32
    )
    inverse = lax.rsqrt(jnp.mean(full * full, axis=1, keepdims=True) + EPSILON)
    keys_buf[s, h, :, :KV_RANK] = (full * inverse * kv_gain_ref[...]).astype(bf16)
    half_token = base + h * rows_half + iota((rows_half, 1), 0)
    key_rope = spin(pltpu.roll(end, ROPE, 1), turns(half_token))
    named = jnp.zeros((128, tok_rows), f32)
    place = iota(named.shape, 0) - ROPE
    for k in range(ids_ref.shape[0]):
        named = jnp.where(ids_ref[k : k + 1, :] == place, 1.0, named)
    row_pick = iota((rows_half, tok_rows), 1) == h * rows_half + iota((rows_half, tok_rows), 0)
    row_pick = jnp.where(row_pick, 1.0, 0.0).astype(bf16)
    mask = lax.dot_general(row_pick, named.astype(bf16), pair, preferred_element_type=f32)
    keys_buf[s, h, :, KV_RANK:] = (key_rope.astype(f32) + mask).astype(bf16)
    pl.semaphore_wait(barrier, len(peers))

    def key_ring(t):
        @pl.when((t >= 1) & (t <= z))
        def _():
            key_up_in(t).wait_recv()

        @pl.when((t <= z) & (z < 3))
        def _():
            key_up_move(t).start()

        @pl.when((t >= 1) & (t <= 3 - z))
        def _():
            key_low_in(t).wait_recv()

        @pl.when((t <= 3 - z) & (z > 0))
        def _():
            key_low_move(t).start()

        for step in (3, 1, 2):
            plane(t, step).start()

    def meet_keys(k):
        for step in (1, 2, 3):
            plane_in(k, step).wait_recv()
        share_keys(k).start()

    key_ring(0)
    for index in range(2, 6):
        loads[index].start()
    token = base + iota((tok_rows, 1), 0)
    scale = math.log2(math.e) / math.sqrt(NOPE + ROPE)
    turn = [scale * part for part in turns(token)]
    loads[0].wait()
    loads[1].wait()
    for two in range(heads // 2):
        left = queries[:, 384 * two : 384 * two + 128]
        middle = queries[:, 384 * two + 128 : 384 * two + 256].astype(f32)
        right = queries[:, 384 * two + 256 : 384 * two + 384].astype(f32)
        lane = iota(middle.shape, 1)
        turned = pltpu.roll(right, 64, 1)
        nope = jnp.where(lane < 64, pltpu.roll(middle, 64, 1), turned).astype(bf16)
        for odd, columns, rotary in ((0, left, middle), (1, nope, turned)):
            head = 2 * two + odd
            here = slice(head * tok_rows, (head + 1) * tok_rows)
            latent = jnp.dot(columns, key_up[head], preferred_element_type=f32)
            query[here, :KV_RANK] = (scale * latent).astype(bf16)
            query[here, KV_RANK:] = spin(rotary, turn)
    first = jnp.concatenate([starts_of(token)[0]] * part_heads, axis=0)
    own = jnp.concatenate([token] * part_heads, axis=0)
    def attend(k, part_no, leading=False):
        line = line_of(k)
        keys = keys_buf[pl.ds(line * 4, 4)].reshape(tile_keys, keys_buf.shape[3])
        here = slice(part_no * part_rows, (part_no + 1) * part_rows)
        scores = lax.dot_general(query[here, :], keys, pair, preferred_element_type=f32)
        index = line * tile_keys + iota(scores.shape, 1)
        allowed = index >= first
        if leading:
            allowed = allowed & (index <= own)
        scores = jnp.where(allowed, scores, MASKED)
        new = jnp.max(scores, axis=1, keepdims=True)
        if not leading:
            old = peak[part_no, :, :1]
            new = jnp.maximum(old, new)
            fade = jnp.exp2(old - new)
        terms = jnp.exp2(scores - new)
        norm = jnp.sum(terms, axis=1, keepdims=True)
        mixture = jnp.dot(terms.astype(bf16), keys[:, :KV_RANK], preferred_element_type=f32)
        if not leading:
            norm = total[part_no, :, :1] * fade + norm
            mixture = acc[part_no] * fade + mixture
        peak[part_no, :, :1] = new
        total[part_no, :, :1] = norm
        acc[part_no] = mixture

    key_ring(1)
    meet_keys(0)
    key_ring(2)
    share_keys_in(0).wait_recv()
    attend(0, 0, True)
    key_ring(3)
    meet_keys(1)
    attend(0, 1, True)

    @pl.loop(1, 4)
    def _(k):
        share_keys_in(k).wait_recv()

        @pl.when(k <= z)
        def _():
            attend(k, 0)

        @pl.when(k <= 2)
        def _():
            meet_keys(k + 1)

        @pl.when(k <= z)
        def _():
            attend(k, 1)

    loads[2].wait()
    loads[3].wait()
    for head in range(heads):
        part_no, member = head // part_heads, head % part_heads
        here = slice(member * tok_rows, (member + 1) * tok_rows)
        attended = (acc[part_no, here, :] / total[part_no, here, :1]).astype(bf16)
        heads_buf[:, head * V_HEAD : (head + 1) * V_HEAD] = jnp.dot(
            attended, value_up[head], preferred_element_type=f32
        ).astype(bf16)
    cols = hidden_ref.shape[1]
    half = cols // 2

    def swap(piece):
        return remote(
            attn_buf.at[piece],
            attn_in.at[piece],
            swap_send.at[piece],
            swap_recv.at[piece],
            sibling,
        )

    for piece in range(2):
        here = slice(piece * half, (piece + 1) * half)
        attn_buf[piece] = jnp.dot(
            heads_buf[...], out_proj[:, here], preferred_element_type=f32
        ).astype(bf16)
        swap(piece).start()
    def part_of(q):
        return pl.ds(q * (half // PIECES), half // PIECES)

    def up(t, q):
        view = x_buf.at[z - t, :, part_of(q)]
        device = (line_place(lax.rem(z + 1, 4), s), h)
        index = PIECES * t + q
        return remote(view, view, up_send.at[index], up_recv.at[index], device)

    def up_in(t, q):
        view = x_buf.at[z - t, :, part_of(q)]
        index = PIECES * (t - 1) + q
        return remote(view, view, up_send.at[index], up_recv.at[index], sibling)

    def low(t, q):
        view = x_buf.at[z + t, :, part_of(q)]
        device = (line_place(lax.rem(z + 3, 4), s), h)
        index = PIECES * t + q
        return remote(view, view, down_send.at[index], down_recv.at[index], device)

    def low_in(t, q):
        view = x_buf.at[z + t, :, part_of(q)]
        index = PIECES * (t - 1) + q
        return remote(view, view, down_send.at[index], down_recv.at[index], sibling)

    def go(k, step, q):
        other = across(s, step)
        index = PIECES * (3 * k + step - 1) + q
        return remote(
            stage.at[k, lax.rem(other, 4), :, part_of(q)],
            rows_in.at[k, h, c, :, part_of(q)],
            go_send.at[index],
            go_recv.at[index],
            (other, h),
        )

    def go_in(k, step, q):
        index = PIECES * (3 * k + step - 1) + q
        view = rows_in.at[k, h, lax.rem(across(s, step), 4), :, part_of(q)]
        return remote(view, view, go_send.at[index], go_recv.at[index], sibling)

    def share(k, step):
        view = rows_in.at[k, h, lax.rem(across(s, step), 4)]
        index = 4 * k + step
        return remote(view, view, share_send.at[index], share_recv.at[index], sibling)

    def share_in(k, step):
        view = rows_in.at[k, 1 - h, lax.rem(across(s, step), 4)]
        index = 4 * k + step
        return remote(view, view, share_send.at[index], share_recv.at[index], sibling)

    def part(k):
        return remote(res.at[k, 1 - h], sib_in.at[k], part_send.at[k], part_recv.at[k], sibling)

    def ret(k, step, q):
        other = across(s, step)
        index = PIECES * (3 * k + step - 1) + q
        return remote(
            res.at[k, h, lax.rem(other, 4), :, part_of(q)],
            ret_in.at[k, c, :, part_of(q)],
            ret_send.at[index],
            ret_recv.at[index],
            (other, h),
        )

    def ret_back(k, step, q):
        index = PIECES * (3 * k + step - 1) + q
        view = ret_in.at[k, lax.rem(across(s, step), 4), :, part_of(q)]
        return remote(view, view, ret_send.at[index], ret_recv.at[index], sibling)

    def home(k, q):
        owner = (line_place(turn_line(z, k), s), h)
        return remote(
            z_out.at[k, :, part_of(q)],
            z_in.at[z, :, part_of(q)],
            home_send.at[PIECES * k + q],
            home_recv.at[PIECES * z + q],
            owner,
        )

    def home_in(back, q):
        line = lax.rem(z + back, 4)
        view = z_in.at[line, :, part_of(q)]
        return remote(view, view, home_send.at[q], home_recv.at[PIECES * line + q], sibling)

    slots = stage.shape[2]
    expert_count = router_ref.shape[0]
    four = 4 * slots
    before = (iota((tok_rows, tok_rows), 0) < iota((tok_rows, tok_rows), 1)).astype(bf16)
    after = (iota((tok_rows, tok_rows), 0) > iota((tok_rows, tok_rows), 1)).astype(bf16)

    def one_hot(flags):
        return jnp.where(flags, 1.0, 0.0).astype(bf16)

    def tail_of(block):
        return keys_buf[block, :, :, KV_RANK:].reshape(tok_rows, 128)

    def prepare(k):
        line = turn_line(z, k)
        tail = tail_of(line * 4 + c)
        shape = (four, 128)
        named = one_hot(iota(shape, 1) == ROPE + 4 * z + lax.div(iota(shape, 0), slots))
        slot = lax.rem(iota((four, tok_rows), 0), slots).astype(f32)
        member = lax.dot_general(named, tail, pair, preferred_element_type=f32)
        rank = jnp.dot(member.astype(bf16), before, preferred_element_type=f32)
        pick_buf[k] = one_hot((rank == slot) & (member > 0.0))
        shape = (128, four)
        named = one_hot(iota(shape, 0) == ROPE + 4 * z + lax.div(iota(shape, 1), slots))
        slot = lax.rem(iota((tok_rows, four), 1), slots).astype(f32)
        member = jnp.dot(tail, named, preferred_element_type=f32)
        rank = jnp.dot(after, member.astype(bf16), preferred_element_type=f32)
        place_buf[k] = one_hot((rank == slot) & (member > 0.0))
        named = one_hot(iota((slots, 128), 1) == ROPE + s)
        slot = iota((slots, tok_rows), 0).astype(f32)
        for block in range(4):
            tail = tail_of(line * 4 + block)
            member = lax.dot_general(named, tail, pair, preferred_element_type=f32)
            rank = jnp.dot(member.astype(bf16), before, preferred_element_type=f32)
            mine = one_hot((rank == slot) & (member > 0.0))
            chosen = jnp.dot(mine, tail, preferred_element_type=f32)
            known = iota((slots, 128), 1)
            known = (known >= ROPE) & (known < ROPE + expert_count)
            chosen_buf[k, block * slots : (block + 1) * slots] = jnp.where(known, chosen, 0.0)

    prepare(0)
    router = router_ref[...]
    high = router.astype(bf16)
    rest = router - high.astype(f32)
    middle = rest.astype(bf16)
    last = (rest - middle.astype(f32)).astype(bf16)
    top_pad = jnp.zeros((ROPE, cols), bf16)
    low_pad = jnp.zeros((128 - ROPE - 3 * expert_count, cols), bf16)
    router_buf[...] = jnp.concatenate([top_pad, high, middle, last, low_pad], axis=0)

    for piece in range(2):
        swap(piece).wait_recv()

    def joined(piece):
        here = slice(piece * half, (piece + 1) * half)
        both = attn_buf[piece].astype(f32) + attn_in[piece].astype(f32)
        return hidden_ref[:, here].astype(f32) + both

    sums = [joined(0), joined(1)]
    square = sums[0] * sums[0] + sums[1] * sums[1]
    inverse = lax.rsqrt(jnp.sum(square, axis=1, keepdims=True) / cols + EPSILON)
    mine = jnp.where(h == 0, sums[0], sums[1])
    mixed[...] = mine
    gain = ffn_gain_ref[...]
    own_gain = jnp.where(h == 0, gain[:, :half], gain[:, half:])
    x_buf[z] = (mine * inverse * own_gain).astype(bf16)

    def ring(t, q):
        @pl.when((t >= 1) & (t <= z))
        def _():
            up_in(t, q).wait_recv()

        @pl.when((t <= z) & (z < 3))
        def _():
            up(t, q).start()

        @pl.when((t >= 1) & (t <= 3 - z))
        def _():
            low_in(t, q).wait_recv()

        @pl.when((t <= 3 - z) & (z > 0))
        def _():
            low(t, q).start()

    def pick(k, q):
        here = part_of(q)
        rows = jnp.dot(
            pick_buf[k], x_buf[turn_line(z, k), :, here], preferred_element_type=f32
        )
        stage[k, :, :, here] = rows.astype(bf16).reshape(4, slots, half // PIECES)
        for step in (3, 1, 2):
            go(k, step, q).start()
        rows_in[k, h, c, :, here] = stage[k, c, :, here]

    def meet_rows(k):
        share(k, 0).start()
        for step in (1, 2, 3):
            for q in range(PIECES):
                go_in(k, step, q).wait_recv()
            share(k, step).start()

    def work(k):
        for step in range(4):
            share_in(k, step).wait_recv()
        rows = jnp.concatenate(
            [rows_in[k, 0].reshape(four, half), rows_in[k, 1].reshape(four, half)], axis=1
        )
        logit = lax.dot_general(rows, router_buf[...], pair, preferred_element_type=f32)
        logit = logit + (
            pltpu.roll(logit, 128 - expert_count, 1) + pltpu.roll(logit, 128 - 2 * expert_count, 1)
        )
        score = 1.0 / (1.0 + jnp.exp(-logit))
        chosen = jnp.where(chosen_buf[k] > 0.0, score, 0.0)
        own = jnp.where(iota(chosen.shape, 1) == ROPE + s, chosen, 0.0)
        own = jnp.sum(own, axis=1, keepdims=True)
        every = jnp.sum(chosen, axis=1, keepdims=True)
        weight = ROUTE_SCALE * own / jnp.where(every > 0.0, every, 1.0)
        gate = lax.dot_general(rows, gate_up[0], pair, preferred_element_type=f32)
        rise = lax.dot_general(rows, gate_up[1], pair, preferred_element_type=f32)
        act = (gate / (1.0 + jnp.exp(-gate)) * rise * weight).astype(bf16)
        for owner in (1 - h, h):
            here = pl.ds(pl.multiple_of(owner * half, half), half)
            out = jnp.dot(act, down[:, here], preferred_element_type=f32).astype(bf16)
            res[k, owner] = out.reshape(4, slots, half)
            if owner is not h:
                part(k).start()

    def send_back(k):
        part(k).wait_recv()
        for q in range(PIECES):
            here = part_of(q)
            both = res[k, h, :, :, here].astype(f32) + sib_in[k, :, :, here].astype(f32)
            res[k, h, :, :, here] = both.astype(bf16)
            for step in (3, 1, 2):
                ret(k, step, q).start()
            ret_in[k, c, :, here] = res[k, h, c, :, here]

    def place(k, q):
        for step in (1, 2, 3):
            ret_back(k, step, q).wait_recv()
        rows = ret_in[k, :, :, part_of(q)].reshape(four, half // PIECES)
        return jnp.dot(place_buf[k], rows, preferred_element_type=f32)

    def go_home(k):
        for q in range(PIECES):
            z_out[k, :, part_of(q)] = place(k, q).astype(bf16)
            home(k, q).start()

    def decode_rows():
        span = keys_buf.shape[0] * tok_rows
        keys = keys_buf[...].reshape(span, keys_buf.shape[3])
        shape = (slot_ref.shape[1], span)
        spread = one_hot(lax.div(iota(shape, 1), BLOCK) == iota(shape, 0))
        device_slot = (2 * s + h) * DEC_SLOTS

        def rows_of(slot, row, values):
            named = one_hot(slot_ref[...] == slot)
            blocks = jnp.dot(named, spread, preferred_element_type=f32)
            same = lax.rem(iota(blocks.shape, 1), BLOCK) == row
            picked = one_hot(same & (blocks > 0.0))
            return jnp.dot(picked, values, preferred_element_type=f32)

        place = iota((DEC_SLOTS * BLOCK, 1), 0)
        latent = rows_of(
            device_slot + lax.div(place, BLOCK), lax.rem(place, BLOCK), keys[:, :KV_RANK]
        )
        latent_ref[...] = latent.astype(bf16)
        place = iota((8 * BLOCK, 1), 0)
        slot = lax.rem(place, 8)
        slot = jnp.where(slot < DEC_SLOTS, device_slot + slot, -1)
        rope = rows_of(slot, lax.div(place, 8), keys[:, KV_RANK:])
        pieces = []
        for two in range(BLOCK // 2):
            left = rope[16 * two : 16 * two + 8]
            right = pltpu.roll(rope[16 * two + 8 : 16 * two + 16], ROPE, 1)
            pieces.append(jnp.where(iota(left.shape, 1) < ROPE, left, right))
        flat = jnp.concatenate(pieces, axis=1)
        rope_ref[...] = flat[:DEC_SLOTS].astype(bf16)

    @pl.loop(0, 6)
    def _(t):
        @pl.when(t <= 3)
        def _():
            for q in range(PIECES):
                ring(t, q)
                pick(t, q)

        @pl.when(t == 0)
        def _():
            @pl.loop(1, 4)
            def _(k):
                prepare(k)

        @pl.when(t == 1)
        def _():
            loads[4].wait()
            loads[5].wait()

        @pl.when((t >= 1) & (t <= 4))
        def _():
            meet_rows(t - 1)

        @pl.when(t >= 3)
        def _():
            send_back(t - 2)

        @pl.when((t >= 1) & (t <= 4))
        def _():
            work(t - 1)

        @pl.when(t == 4)
        def _():
            go_home(1)

    @pl.loop(2, 4)
    def _(k):
        go_home(k)

    send_back(0)
    decode_rows()
    for q in range(PIECES):
        here = part_of(q)
        mixed[:, here] = mixed[:, here] + place(0, q)
    for q in range(PIECES):
        here = part_of(q)
        result = mixed[:, here]
        for back in (1, 2, 3):
            home_in(back, q).wait_recv()
            result = result + z_in[lax.rem(z + back, 4), :, here].astype(f32)
        out_ref[:, here] = result.astype(out_ref.dtype)
    for piece in range(2):
        swap(piece).wait_send()

    @pl.loop(0, 4)
    def _(k):
        for q in range(PIECES):
            @pl.when((k <= z) & (z < 3))
            def _():
                up(k, q).wait_send()

            @pl.when((k <= 3 - z) & (z > 0))
            def _():
                low(k, q).wait_send()

            for step in (1, 2, 3):
                go(k, step, q).wait_send()
                ret(k, step, q).wait_send()

            @pl.when(k > 0)
            def _():
                home(k, q).wait_send()

        for step in range(4):
            share(k, step).wait_send()
        part(k).wait_send()

    @pl.loop(0, 4)
    def _(k):
        @pl.when((k <= z) & (z < 3))
        def _():
            key_up_move(k).wait_send()

        @pl.when((k <= 3 - z) & (z > 0))
        def _():
            key_low_move(k).wait_send()

        for step in (1, 2, 3):
            plane(k, step).wait_send()
        share_keys(k).wait_send()


def layer(
    req_len,
    req_offset,
    hidden,
    attn_gain,
    kv_down,
    kv_gain,
    expert_ids,
    decode_slot,
    ffn_gain,
    router,
    queries,
    key_up,
    value_up,
    out_proj,
    gate_up,
    down,
    seq_count,
):
    tok_rows, cols = hidden.shape
    half = cols // 2
    heads = key_up.shape[0]
    width = KV_RANK + 128
    slots = max(2, tok_rows * TOP * 4 // (3 * router.shape[1]))
    lanes = np.arange(128) % (ROPE // 2)
    frequency = np.exp(-math.log(ROPE_BASE) * lanes * (2.0 / ROPE)).astype(np.float32)[None, :]
    bf16, f32 = jnp.bfloat16, jnp.float32
    vmem = pl.BlockSpec(memory_space=pltpu.VMEM)
    smem = pl.BlockSpec(memory_space=pltpu.SMEM)
    hbm = pl.BlockSpec(memory_space=pl.ANY)
    dma = pltpu.SemaphoreType.DMA
    part_rows = heads * tok_rows // 2
    sizes = [7] + [4] * 4 + [12] * 2 + [4] * 2 + [2] * 2
    sizes += [4 * PIECES] * 4 + [12 * PIECES] * 2 + [16] * 2 + [4] * 2
    sizes += [12 * PIECES] * 2 + [4 * PIECES] * 2
    return pl.pallas_call(
        layer_kernel,
        out_shape=(
            jax.ShapeDtypeStruct((tok_rows, half), bf16),
            jax.ShapeDtypeStruct((DEC_SLOTS * BLOCK, KV_RANK), bf16),
            jax.ShapeDtypeStruct((DEC_SLOTS, BLOCK * ROPE), bf16),
        ),
        in_specs=[smem] * 2 + [vmem] * 8 + [hbm] * 7,
        out_specs=(vmem, vmem, vmem),
        scratch_shapes=[
            pltpu.VMEM(kv_down.shape[::-1], bf16),
            pltpu.VMEM((seq_count, 2, tok_rows // 2, width), bf16),
            pltpu.VMEM(queries.shape, bf16),
            pltpu.VMEM(key_up.shape, bf16),
            pltpu.VMEM(value_up.shape, bf16),
            pltpu.VMEM(out_proj.shape, bf16),
            pltpu.VMEM((heads * tok_rows, width), bf16),
            pltpu.VMEM((2, part_rows, KV_RANK), f32),
            pltpu.VMEM((2, part_rows, 128), f32),
            pltpu.VMEM((2, part_rows, 128), f32),
            pltpu.VMEM((tok_rows, heads * V_HEAD), bf16),
            pltpu.VMEM((2, tok_rows, half), bf16),
            pltpu.VMEM((2, tok_rows, half), bf16),
            pltpu.VMEM((tok_rows, half), f32),
            pltpu.VMEM((4, tok_rows, half), bf16),
            pltpu.VMEM((4, 4, slots, half), bf16),
            pltpu.VMEM((4, 2, 4, slots, half), bf16),
            pltpu.VMEM((4, 2, 4, slots, half), bf16),
            pltpu.VMEM((4, 4, slots, half), bf16),
            pltpu.VMEM((4, 4, slots, half), bf16),
            pltpu.VMEM((4, tok_rows, half), bf16),
            pltpu.VMEM((4, tok_rows, half), bf16),
            pltpu.VMEM((4, 4 * slots, tok_rows), bf16),
            pltpu.VMEM((4, tok_rows, 4 * slots), bf16),
            pltpu.VMEM((4, 4 * slots, 128), f32),
            pltpu.VMEM((128, cols), bf16),
            pltpu.VMEM(gate_up.shape, bf16),
            pltpu.VMEM(down.shape, bf16),
        ]
        + [dma((size,)) for size in sizes],
        compiler_params=pltpu.CompilerParams(
            collective_id=0, has_side_effects=True, vmem_limit_bytes=60 * 1024 * 1024
        ),
    )(
        req_len,
        req_offset,
        jnp.asarray(frequency),
        hidden,
        attn_gain[None, :],
        kv_gain[None, :],
        expert_ids.T,
        decode_slot[None, :],
        ffn_gain[None, :],
        router.T,
        kv_down.T,
        queries,
        key_up,
        value_up,
        out_proj,
        gate_up,
        down,
    )


def body(
    hidden,
    queries,
    req_len,
    req_offset,
    expert_ids,
    decode_slot,
    attn_gain,
    kv_down,
    kv_gain,
    key_up,
    value_up,
    out_proj,
    ffn_gain,
    router,
    expert_gate_up,
    expert_down,
):
    head_count = lax.axis_size("head")
    seq_place = lax.axis_index("seq")
    head_place = lax.axis_index("head")
    tok_rows = hidden.shape[0]
    heads_here = key_up.shape[0]
    my_index = seq_place * tok_rows + jnp.arange(tok_rows, dtype=jnp.int32)
    my_request = request_of(req_len, my_index)
    my_turn = angles(position_of(req_len, req_offset, my_index), ROPE)
    normed = rms_rows(hidden, attn_gain).astype(jnp.bfloat16)
    head_view = queries.reshape(tok_rows, heads_here, NOPE + ROPE)
    query_rope = rotate(head_view[:, :, NOPE:], my_turn[:, None, :]).astype(jnp.bfloat16)
    query_latent = jnp.einsum(
        "thn,hnc->thc", head_view[:, :, :NOPE], key_up, preferred_element_type=jnp.float32
    ).astype(jnp.bfloat16)
    query_rows = tok_rows * heads_here
    flat_latent = query_latent.reshape(query_rows, KV_RANK)
    flat_rope = query_rope.reshape(query_rows, ROPE)
    row_token = jnp.repeat(my_index, heads_here)
    row_request = jnp.repeat(my_request, heads_here)
    score_scale = 1.0 / math.sqrt(NOPE + ROPE)
    my_device = seq_place * head_count + head_place
    slot_ids = my_device * DEC_SLOTS + jnp.arange(DEC_SLOTS, dtype=jnp.int32)
    block_ids = jnp.arange(decode_slot.shape[0], dtype=jnp.int32)
    slot_match = decode_slot[None, :] == slot_ids[:, None]
    source_block = jnp.sum(jnp.where(slot_match, block_ids[None, :], 0), axis=1)
    slot_filled = jnp.any(slot_match, axis=1)
    kv_full = jnp.dot(normed, kv_down, preferred_element_type=jnp.float32)
    latent = rms_rows(kv_full[:, :KV_RANK], kv_gain).astype(jnp.bfloat16)
    key_rope = rotate(kv_full[:, KV_RANK:], my_turn).astype(jnp.bfloat16)
    run_peak = jnp.full((query_rows,), MASKED, jnp.float32)
    run_total = jnp.zeros((query_rows,), jnp.float32)
    run_acc = jnp.zeros((query_rows, KV_RANK), jnp.float32)
    expert_count = router.shape[1]
    expert_axis = jnp.arange(expert_count, dtype=jnp.int32)
    seq_count = lax.axis_size("seq")
    fast = seq_count == 16 and head_count == 2 and expert_count == 16
    if fast:
        output, decode_latent, decode_rope = layer(
            req_len,
            req_offset,
            hidden,
            attn_gain,
            kv_down,
            kv_gain,
            expert_ids,
            decode_slot,
            ffn_gain,
            router,
            queries,
            key_up,
            value_up,
            out_proj,
            jnp.swapaxes(expert_gate_up[0], 1, 2),
            expert_down[0],
            seq_count,
        )
        decode_latent = decode_latent.reshape(DEC_SLOTS, BLOCK, KV_RANK)
        return (output, decode_latent, decode_rope)
    else:
        piece_latent = lax.all_gather(latent, "seq", axis=0, tiled=True)
        piece_rope = lax.all_gather(key_rope, "seq", axis=0, tiled=True)
    piece_rows = piece_latent.shape[0]
    block_width = key_width(piece_rows)

    def key_block(block_no, loop_state):
        peak_now, total_now, acc_now = loop_state
        offset_rows = block_no * block_width
        block_latent = lax.dynamic_slice_in_dim(piece_latent, offset_rows, block_width, 0)
        block_rope = lax.dynamic_slice_in_dim(piece_rope, offset_rows, block_width, 0)
        key_index = offset_rows + jnp.arange(block_width, dtype=jnp.int32)
        key_request = request_of(req_len, key_index)
        contract = (((1,), (1,)), ((), ()))
        scores = lax.dot_general(
            flat_latent, block_latent, contract, preferred_element_type=jnp.float32
        )
        scores = (
            scores
            + lax.dot_general(flat_rope, block_rope, contract, preferred_element_type=jnp.float32)
        ) * score_scale
        allowed = (key_index[None, :] <= row_token[:, None]) & (
            key_request[None, :] == row_request[:, None]
        )
        scores = jnp.where(allowed, scores, MASKED)
        new_peak = jnp.maximum(peak_now, jnp.max(scores, axis=1))
        exp_terms = jnp.where(allowed, jnp.exp(scores - new_peak[:, None]), 0.0)
        fade_factor = jnp.exp(peak_now - new_peak)
        total_now = total_now * fade_factor + jnp.sum(exp_terms, axis=1)
        acc_now = acc_now * fade_factor[:, None] + jnp.dot(
            exp_terms.astype(jnp.bfloat16), block_latent, preferred_element_type=jnp.float32
        )
        return (new_peak, total_now, acc_now)

    run_peak, run_total, run_acc = lax.fori_loop(
        0, piece_rows // block_width, key_block, (run_peak, run_total, run_acc)
    )
    block_count = piece_rows // BLOCK
    pick_matrix = (
        source_block[:, None] == jnp.arange(block_count, dtype=jnp.int32)[None, :]
    ) & slot_filled[:, None]
    pick_matrix = pick_matrix.astype(jnp.bfloat16)
    slot_latent = jnp.dot(
        pick_matrix,
        piece_latent.reshape(block_count, BLOCK * KV_RANK),
        preferred_element_type=jnp.float32,
    )
    slot_rope = jnp.dot(
        pick_matrix,
        piece_rope.reshape(block_count, BLOCK * ROPE),
        preferred_element_type=jnp.float32,
    )
    folded = (run_peak, run_total, run_acc, slot_latent, slot_rope)
    run_total = folded[1]
    run_acc = folded[2]
    slot_latent = folded[3]
    slot_rope = folded[4]
    attended = (
        (run_acc / run_total[:, None]).astype(jnp.bfloat16).reshape(tok_rows, heads_here, KV_RANK)
    )
    head_out = jnp.einsum(
        "thc,hcv->thv", attended, value_up, preferred_element_type=jnp.float32
    ).astype(jnp.bfloat16)
    attn_part = jnp.dot(
        head_out.reshape(tok_rows, heads_here * V_HEAD),
        out_proj,
        preferred_element_type=jnp.float32,
    )
    decode_latent = slot_latent.astype(jnp.bfloat16).reshape(DEC_SLOTS, BLOCK, KV_RANK)
    decode_rope = slot_rope.astype(jnp.bfloat16)
    mixed_rows = hidden.astype(jnp.float32) + lax.psum(
        attn_part.astype(jnp.bfloat16), "head"
    ).astype(jnp.float32)
    moe_in = rms_rows(mixed_rows, ffn_gain).astype(jnp.bfloat16)
    capacity = max(2, tok_rows * TOP * 4 // (3 * expert_count))
    gate_score = jax.nn.sigmoid(
        jnp.dot(moe_in.astype(jnp.float32), router, precision=lax.Precision.HIGHEST)
    )
    id_match = expert_ids[:, :, None] == expert_axis[None, None, :]
    chosen = jnp.sum(jnp.where(id_match, gate_score[:, None, :], 0.0), axis=2)
    gate_weight = ROUTE_SCALE * chosen / jnp.sum(chosen, axis=1, keepdims=True)
    flat_ids = expert_ids.reshape(-1)
    one_hot = (flat_ids[:, None] == expert_axis[None, :]).astype(jnp.int32)
    earlier = ranks(one_hot.T.astype(jnp.bfloat16)).T
    slot_rank = jnp.sum(earlier * one_hot, axis=1)
    flat_slot = flat_ids * capacity + slot_rank
    owner_token = jnp.repeat(jnp.arange(tok_rows, dtype=jnp.int32), TOP)
    slot_token = jnp.zeros((expert_count * capacity,), jnp.int32).at[flat_slot].set(owner_token)
    slot_used = jnp.zeros((expert_count * capacity,), jnp.bool_).at[flat_slot].set(True)
    send_rows = jnp.where(
        slot_used[:, None], moe_in[slot_token], jnp.zeros((), jnp.bfloat16)
    ).reshape(expert_count, capacity, D)
    gate_up_local = expert_gate_up[0]
    down_local = expert_down[0]
    quarter_cols = D // head_count
    arrived = lax.all_to_all(send_rows, "seq", split_axis=0, concat_axis=0, tiled=True)
    sources, item_count, width_cols = arrived.shape
    flat_rows = arrived.reshape(sources * item_count, width_cols)
    gate_part = jnp.dot(flat_rows, gate_up_local[0], preferred_element_type=jnp.float32)
    up_part = jnp.dot(flat_rows, gate_up_local[1], preferred_element_type=jnp.float32)
    activated = (jax.nn.silu(gate_part) * up_part).astype(jnp.bfloat16)
    part_out = (
        jnp.dot(activated, down_local, preferred_element_type=jnp.float32)
        .astype(jnp.bfloat16)
        .reshape(sources, item_count, width_cols)
    )
    returned = lax.all_to_all(part_out, "seq", split_axis=0, concat_axis=0, tiled=True)
    back_cols = returned.shape[2]
    picked = returned.reshape(expert_count * capacity, back_cols)[flat_slot].reshape(
        tok_rows, TOP, back_cols
    )
    weighted = jnp.sum(picked.astype(jnp.float32) * gate_weight[:, :, None], axis=1)
    moe_out = lax.psum_scatter(
        weighted.astype(jnp.bfloat16), "head", scatter_dimension=1, tiled=True
    ).astype(jnp.float32)
    residual_part = lax.dynamic_slice_in_dim(mixed_rows, head_place * quarter_cols, quarter_cols, 1)
    output = (residual_part + moe_out).astype(jnp.bfloat16)
    return (output, decode_latent, decode_rope)


def solution(mesh):
    placed = (
        P("seq", None),
        P("seq", "head"),
        P(),
        P(),
        P("seq", None),
        P(),
        P(),
        P(),
        P(),
        P("head", None, None),
        P("head", None, None),
        P("head", None),
        P(),
        P(),
        P("seq", None, None, "head"),
        P("seq", "head", None),
    )
    return jax.shard_map(
        body,
        mesh=mesh,
        in_specs=placed,
        out_specs=(P("seq", "head"), P(("seq", "head"), None, None), P(("seq", "head"), None)),
        check_vma=False,
    )
```

```python
import functools
import math

import jax
import jax.numpy as jnp
import numpy as np
from jax import lax
from jax.experimental import pallas as pl
from jax.experimental.pallas import tpu as pltpu
from jax.sharding import PartitionSpec as P

D = 2048
NOPE = 128
ROPE = 64
V_HEAD = 128
KV_RANK = 512
TOP = 6
BLOCK = 16
DEC_SLOTS = 4


ROPE_BASE = 50000.0
ROUTE_SCALE = 2.446
EPSILON = 1e-06
MASKED = -1e30
PIECES = 2


def rms_rows(values, scale_gain):
    values = values.astype(jnp.float32)
    inverse = lax.rsqrt(jnp.mean(values * values, axis=-1, keepdims=True) + EPSILON)
    return values * inverse * scale_gain


def angles(position, rope_width):
    half_width = rope_width // 2
    freq_steps = jnp.arange(half_width).astype(jnp.float32) * (2.0 / rope_width)
    frequency = jnp.exp(-math.log(ROPE_BASE) * freq_steps)
    return position.astype(jnp.float32)[:, None] * frequency[None, :]


def rotate(values, rot_angle):
    half_width = values.shape[-1] // 2
    first_half = values[..., :half_width].astype(jnp.float32)
    second_half = values[..., half_width:].astype(jnp.float32)
    cosine = jnp.cos(rot_angle)
    sine_part = jnp.sin(rot_angle)
    return jnp.concatenate(
        [
            first_half * cosine - second_half * sine_part,
            first_half * sine_part + second_half * cosine,
        ],
        axis=-1,
    )


def running(lengths):
    index = jnp.arange(lengths.shape[0])
    return jnp.sum(jnp.where(index[None, :] <= index[:, None], lengths[None, :], 0), axis=1)


def ranks(member):
    count = member.shape[-1]
    index = jnp.arange(count)
    before = (index[:, None] < index[None, :]).astype(jnp.bfloat16)
    return jnp.dot(member, before, preferred_element_type=jnp.float32).astype(jnp.int32)


def request_of(req_len, token_index):
    req_ends = running(req_len)
    return jnp.sum((token_index[:, None] >= req_ends[None, :]).astype(jnp.int32), axis=1)


def position_of(req_len, req_offset, token_index):
    request = request_of(req_len, token_index)
    req_ends = running(req_len)
    starts = req_ends - req_len
    member = request[:, None] == jnp.arange(req_len.shape[0])[None, :]
    start_at = jnp.sum(jnp.where(member, starts[None, :], 0), axis=1)
    offset = jnp.sum(jnp.where(member, req_offset[None, :], 0), axis=1)
    return offset + token_index - start_at


def key_width(piece_rows):
    for option_width in (1024, 512, 256, 128):
        return option_width
    return piece_rows


MESH = pl.DeviceIdType.MESH


def flip(place, step):
    return place + step * (1 - 2 * lax.rem(lax.div(place, step), 2))


def line_place(line, s):
    return line * 4 + lax.rem(s, 4)


def across(s, step):
    if step & 1:
        s = flip(s, 1)
    if step & 2:
        s = flip(s, 2)
    return s


def turn_line(z, k):
    upper = lax.div(z, 2)
    near = z + upper * (3 - 2 * z)
    late = lax.div(k, 2)
    line = late * k + (1 - late) * (near + k * (1 - 2 * near))
    return line + upper * (3 - 2 * line)


def layer_kernel(
    req_len_ref,
    req_offset_ref,
    freq_ref,
    hidden_ref,
    gain_ref,
    kv_gain_ref,
    ids_ref,
    slot_ref,
    ffn_gain_ref,
    router_ref,
    kv_hbm,
    queries_hbm,
    key_up_hbm,
    value_up_hbm,
    out_proj_hbm,
    gate_up_hbm,
    down_hbm,
    out_ref,
    latent_ref,
    rope_ref,
    kv_buf,
    keys_buf,
    queries,
    key_up,
    value_up,
    out_proj,
    query,
    acc,
    peak,
    total,
    heads_buf,
    attn_buf,
    attn_in,
    mixed,
    x_buf,
    stage,
    rows_in,
    res,
    sib_in,
    ret_in,
    z_out,
    z_in,
    pick_buf,
    place_buf,
    chosen_buf,
    router_buf,
    gate_up,
    down,
    load_sem,
    ku_send,
    ku_recv,
    kl_send,
    kl_recv,
    plane_send,
    plane_recv,
    share_keys_send,
    share_keys_recv,
    swap_send,
    swap_recv,
    up_send,
    up_recv,
    down_send,
    down_recv,
    go_send,
    go_recv,
    share_send,
    share_recv,
    part_send,
    part_recv,
    ret_send,
    ret_recv,
    home_send,
    home_recv,
    relay_buf,
    relay_recv,
):
    s, h = lax.axis_index("seq"), lax.axis_index("head")
    z, c = lax.div(s, 4), lax.rem(s, 4)
    bf16, f32 = jnp.bfloat16, jnp.float32
    pair = (((1,), (1,)), ((), ()))
    tok_rows = hidden_ref.shape[0]
    rows_half = tok_rows // 2
    heads = key_up.shape[0]
    part_heads = heads // 2
    part_rows = part_heads * tok_rows
    tile_keys = 4 * tok_rows
    sibling = (s, 1 - h)
    pairs = [(queries_hbm, queries), (key_up_hbm, key_up)]
    pairs += [(value_up_hbm, value_up), (out_proj_hbm, out_proj)]
    pairs += [(gate_up_hbm, gate_up), (down_hbm, down)]
    pairs += [(kv_hbm, kv_buf)]
    loads = [pltpu.make_async_copy(*both, load_sem.at[i]) for i, both in enumerate(pairs)]
    for index in (6, 0, 1):
        loads[index].start()

    barrier = pltpu.get_barrier_semaphore()
    peers = [(line_place(lax.rem(z + back, 4), s), h) for back in range(1, 4)]
    peers += [(across(s, step), h) for step in range(1, 4)] + [sibling]
    for peer in peers:
        pl.semaphore_signal(barrier, inc=1, device_id=peer, device_id_type=MESH)

    def iota(shape, dim):
        return lax.broadcasted_iota(jnp.int32, shape, dim)

    def remote(src, dst, send, recv, device):
        return pltpu.make_async_remote_copy(
            src_ref=src,
            dst_ref=dst,
            send_sem=send,
            recv_sem=recv,
            device_id=device,
            device_id_type=MESH,
        )

    def key_up_move(t):
        view = keys_buf.at[(z - t) * 4 + c, h]
        device = (line_place(lax.rem(z + 1, 4), s), h)
        return remote(view, view, ku_send.at[t], ku_recv.at[t], device)

    def key_up_in(t):
        view = keys_buf.at[(z - t) * 4 + c, h]
        return remote(view, view, ku_send.at[t - 1], ku_recv.at[t - 1], sibling)

    def key_low_move(t):
        view = keys_buf.at[(z + t) * 4 + c, h]
        device = (line_place(lax.rem(z + 3, 4), s), h)
        return remote(view, view, kl_send.at[t], kl_recv.at[t], device)

    def key_low_in(t):
        view = keys_buf.at[(z + t) * 4 + c, h]
        return remote(view, view, kl_send.at[t - 1], kl_recv.at[t - 1], sibling)

    def line_of(k):
        return jnp.where(k <= z, z - k, k)

    def plane(k, step):
        view = keys_buf.at[line_of(k) * 4 + c, h]
        index = 3 * k + step - 1
        device = (across(s, step), h)
        return remote(view, view, plane_send.at[index], plane_recv.at[index], device)

    def plane_in(k, step):
        view = keys_buf.at[line_of(k) * 4 + lax.rem(across(s, step), 4), h]
        index = 3 * k + step - 1
        return remote(view, view, plane_send.at[index], plane_recv.at[index], sibling)

    def share_keys(k):
        view = keys_buf.at[pl.ds(line_of(k) * 4, 4), h]
        return remote(view, view, share_keys_send.at[k], share_keys_recv.at[k], sibling)

    def share_keys_in(k):
        view = keys_buf.at[pl.ds(line_of(k) * 4, 4), 1 - h]
        return remote(view, view, share_keys_send.at[k], share_keys_recv.at[k], sibling)

    def starts_of(token):
        first = jnp.zeros_like(token)
        offset = jnp.full_like(token, req_offset_ref[0])
        end = req_len_ref[0]
        for r in range(1, req_len_ref.shape[0]):
            later = token >= end
            first = jnp.where(later, end, first)
            offset = jnp.where(later, req_offset_ref[r], offset)
            end = end + req_len_ref[r]
        return first, offset

    def turns(token):
        first, offset = starts_of(token)
        angle = (offset + token - first).astype(f32) * freq_ref[...]
        lane = iota(angle.shape, 1)
        sine = jnp.sin(angle)
        sine = jnp.where(lane < ROPE // 2, -sine, sine)
        rotary = lane < ROPE
        return jnp.where(rotary, jnp.cos(angle), 0.0), jnp.where(rotary, sine, 0.0)

    def spin(values, turn):
        lane = iota(values.shape, 1)
        other = jnp.where(
            lane < ROPE // 2,
            pltpu.roll(values, 128 - ROPE // 2, 1),
            pltpu.roll(values, ROPE // 2, 1),
        )
        return (values * turn[0] + other * turn[1]).astype(bf16)

    base = s * tok_rows
    rows = hidden_ref[pl.ds(pl.multiple_of(h * rows_half, rows_half), rows_half), :].astype(f32)
    inverse = lax.rsqrt(jnp.mean(rows * rows, axis=1, keepdims=True) + EPSILON)
    normed = (rows * inverse * gain_ref[...]).astype(bf16)
    loads[6].wait()
    full = lax.dot_general(normed, kv_buf[:KV_RANK], pair, preferred_element_type=f32)
    end = lax.dot_general(
        normed, kv_buf[KV_RANK + ROPE - 128 :], pair, preferred_element_type=f32
    )
    inverse = lax.rsqrt(jnp.mean(full * full, axis=1, keepdims=True) + EPSILON)
    keys_buf[s, h, :, :KV_RANK] = (full * inverse * kv_gain_ref[...]).astype(bf16)
    half_token = base + h * rows_half + iota((rows_half, 1), 0)
    key_rope = spin(pltpu.roll(end, ROPE, 1), turns(half_token))
    named = jnp.zeros((128, tok_rows), f32)
    place = iota(named.shape, 0) - ROPE
    for k in range(ids_ref.shape[0]):
        named = jnp.where(ids_ref[k : k + 1, :] == place, 1.0, named)
    row_pick = iota((rows_half, tok_rows), 1) == h * rows_half + iota((rows_half, tok_rows), 0)
    row_pick = jnp.where(row_pick, 1.0, 0.0).astype(bf16)
    mask = lax.dot_general(row_pick, named.astype(bf16), pair, preferred_element_type=f32)
    keys_buf[s, h, :, KV_RANK:] = (key_rope.astype(f32) + mask).astype(bf16)
    pl.semaphore_wait(barrier, len(peers))

    def key_ring(t):
        @pl.when((t >= 1) & (t <= z))
        def _():
            key_up_in(t).wait_recv()

        @pl.when((t <= z) & (z < 3))
        def _():
            key_up_move(t).start()

        @pl.when((t >= 1) & (t <= 3 - z))
        def _():
            key_low_in(t).wait_recv()

        @pl.when((t <= 3 - z) & (z > 0))
        def _():
            key_low_move(t).start()

        for step in (3, 1, 2):
            plane(t, step).start()

    def meet_keys(k):
        for step in (1, 2, 3):
            plane_in(k, step).wait_recv()
        share_keys(k).start()

    key_ring(0)
    for index in range(2, 6):
        loads[index].start()
    token = base + iota((tok_rows, 1), 0)
    scale = math.log2(math.e) / math.sqrt(NOPE + ROPE)
    turn = [scale * part for part in turns(token)]
    loads[0].wait()
    loads[1].wait()
    for two in range(heads // 2):
        left = queries[:, 384 * two : 384 * two + 128]
        middle = queries[:, 384 * two + 128 : 384 * two + 256].astype(f32)
        right = queries[:, 384 * two + 256 : 384 * two + 384].astype(f32)
        lane = iota(middle.shape, 1)
        turned = pltpu.roll(right, 64, 1)
        nope = jnp.where(lane < 64, pltpu.roll(middle, 64, 1), turned).astype(bf16)
        for odd, columns, rotary in ((0, left, middle), (1, nope, turned)):
            head = 2 * two + odd
            here = slice(head * tok_rows, (head + 1) * tok_rows)
            latent = jnp.dot(columns, key_up[head], preferred_element_type=f32)
            query[here, :KV_RANK] = (scale * latent).astype(bf16)
            query[here, KV_RANK:] = spin(rotary, turn)
    first = jnp.concatenate([starts_of(token)[0]] * part_heads, axis=0)
    own = jnp.concatenate([token] * part_heads, axis=0)
    def attend(k, part_no, leading=False):
        line = line_of(k)
        keys = keys_buf[pl.ds(line * 4, 4)].reshape(tile_keys, keys_buf.shape[3])
        here = slice(part_no * part_rows, (part_no + 1) * part_rows)
        scores = lax.dot_general(query[here, :], keys, pair, preferred_element_type=f32)
        index = line * tile_keys + iota(scores.shape, 1)
        allowed = index >= first
        if leading:
            allowed = allowed & (index <= own)
        scores = jnp.where(allowed, scores, MASKED)
        new = jnp.max(scores, axis=1, keepdims=True)
        if not leading:
            old = peak[part_no, :, :1]
            new = jnp.maximum(old, new)
            fade = jnp.exp2(old - new)
        terms = jnp.exp2(scores - new)
        norm = jnp.sum(terms, axis=1, keepdims=True)
        mixture = jnp.dot(terms.astype(bf16), keys[:, :KV_RANK], preferred_element_type=f32)
        if not leading:
            norm = total[part_no, :, :1] * fade + norm
            mixture = acc[part_no] * fade + mixture
        peak[part_no, :, :1] = new
        total[part_no, :, :1] = norm
        acc[part_no] = mixture

    key_ring(1)
    meet_keys(0)
    key_ring(2)
    share_keys_in(0).wait_recv()
    attend(0, 0, True)
    key_ring(3)
    meet_keys(1)
    attend(0, 1, True)

    @pl.loop(1, 4)
    def _(k):
        share_keys_in(k).wait_recv()

        @pl.when(k <= z)
        def _():
            attend(k, 0)

        @pl.when(k <= 2)
        def _():
            meet_keys(k + 1)

        @pl.when(k <= z)
        def _():
            attend(k, 1)

    loads[2].wait()
    loads[3].wait()
    for head in range(heads):
        part_no, member = head // part_heads, head % part_heads
        here = slice(member * tok_rows, (member + 1) * tok_rows)
        attended = (acc[part_no, here, :] / total[part_no, here, :1]).astype(bf16)
        heads_buf[:, head * V_HEAD : (head + 1) * V_HEAD] = jnp.dot(
            attended, value_up[head], preferred_element_type=f32
        ).astype(bf16)
    cols = hidden_ref.shape[1]
    half = cols // 2

    def swap(piece):
        return remote(
            attn_buf.at[piece],
            attn_in.at[piece],
            swap_send.at[piece],
            swap_recv.at[piece],
            sibling,
        )

    for piece in range(2):
        here = slice(piece * half, (piece + 1) * half)
        attn_buf[piece] = jnp.dot(
            heads_buf[...], out_proj[:, here], preferred_element_type=f32
        ).astype(bf16)
        swap(piece).start()
    def part_of(q):
        return pl.ds(q * (half // PIECES), half // PIECES)

    def up(t, q):
        view = x_buf.at[z - t, :, part_of(q)]
        device = (line_place(lax.rem(z + 1, 4), s), h)
        index = PIECES * t + q
        return remote(view, view, up_send.at[index], up_recv.at[index], device)

    def up_in(t, q):
        view = x_buf.at[z - t, :, part_of(q)]
        index = PIECES * (t - 1) + q
        return remote(view, view, up_send.at[index], up_recv.at[index], sibling)

    def low(t, q):
        view = x_buf.at[z + t, :, part_of(q)]
        device = (line_place(lax.rem(z + 3, 4), s), h)
        index = PIECES * t + q
        return remote(view, view, down_send.at[index], down_recv.at[index], device)

    def low_in(t, q):
        view = x_buf.at[z + t, :, part_of(q)]
        index = PIECES * (t - 1) + q
        return remote(view, view, down_send.at[index], down_recv.at[index], sibling)

    def go(k, step, q):
        other = across(s, step)
        index = PIECES * (3 * k + step - 1) + q
        return remote(
            stage.at[k, lax.rem(other, 4), :, part_of(q)],
            rows_in.at[k, h, c, :, part_of(q)],
            go_send.at[index],
            go_recv.at[index],
            (other, h),
        )

    def go_in(k, step, q):
        index = PIECES * (3 * k + step - 1) + q
        view = rows_in.at[k, h, lax.rem(across(s, step), 4), :, part_of(q)]
        return remote(view, view, go_send.at[index], go_recv.at[index], sibling)

    def share(k, step):
        view = rows_in.at[k, h, lax.rem(across(s, step), 4)]
        index = 4 * k + step
        return remote(view, view, share_send.at[index], share_recv.at[index], sibling)

    def share_in(k, step):
        view = rows_in.at[k, 1 - h, lax.rem(across(s, step), 4)]
        index = 4 * k + step
        return remote(view, view, share_send.at[index], share_recv.at[index], sibling)

    def part(k):
        return remote(res.at[k, 1 - h], sib_in.at[k], part_send.at[k], part_recv.at[k], sibling)

    def ret(k, step, q):
        other = across(s, step)
        index = PIECES * (3 * k + step - 1) + q
        return remote(
            res.at[k, h, lax.rem(other, 4), :, part_of(q)],
            ret_in.at[k, c, :, part_of(q)],
            ret_send.at[index],
            ret_recv.at[index],
            (other, h),
        )

    def ret_back(k, step, q):
        index = PIECES * (3 * k + step - 1) + q
        view = ret_in.at[k, lax.rem(across(s, step), 4), :, part_of(q)]
        return remote(view, view, ret_send.at[index], ret_recv.at[index], sibling)

    def home(k, q):
        owner = (line_place(turn_line(z, k), s), h)
        return remote(
            z_out.at[k, :, part_of(q)],
            z_in.at[z, :, part_of(q)],
            home_send.at[PIECES * k + q],
            home_recv.at[PIECES * z + q],
            owner,
        )

    def relay(k, q):
        inner_side = (line_place(flip(z, 1), s), h)
        return remote(
            z_out.at[k, :, part_of(q)],
            relay_buf.at[k - 2, :, part_of(q)],
            home_send.at[PIECES * k + q],
            relay_recv.at[PIECES * (k - 2) + q],
            inner_side,
        )

    def home_in(line, q):
        view = z_in.at[line, :, part_of(q)]
        return remote(view, view, home_send.at[q], home_recv.at[PIECES * line + q], sibling)

    inner = lax.rem(z + lax.div(z, 2), 2)
    slots = stage.shape[2]
    expert_count = router_ref.shape[0]
    four = 4 * slots
    before = (iota((tok_rows, tok_rows), 0) < iota((tok_rows, tok_rows), 1)).astype(bf16)
    after = (iota((tok_rows, tok_rows), 0) > iota((tok_rows, tok_rows), 1)).astype(bf16)

    def one_hot(flags):
        return jnp.where(flags, 1.0, 0.0).astype(bf16)

    def tail_of(block):
        return keys_buf[block, :, :, KV_RANK:].reshape(tok_rows, 128)

    def prepare(k):
        line = turn_line(z, k)
        tail = tail_of(line * 4 + c)
        shape = (four, 128)
        named = one_hot(iota(shape, 1) == ROPE + 4 * z + lax.div(iota(shape, 0), slots))
        slot = lax.rem(iota((four, tok_rows), 0), slots).astype(f32)
        member = lax.dot_general(named, tail, pair, preferred_element_type=f32)
        rank = jnp.dot(member.astype(bf16), before, preferred_element_type=f32)
        pick_buf[k] = one_hot((rank == slot) & (member > 0.0))
        shape = (128, four)
        named = one_hot(iota(shape, 0) == ROPE + 4 * z + lax.div(iota(shape, 1), slots))
        slot = lax.rem(iota((tok_rows, four), 1), slots).astype(f32)
        member = jnp.dot(tail, named, preferred_element_type=f32)
        rank = jnp.dot(after, member.astype(bf16), preferred_element_type=f32)
        place_buf[k] = one_hot((rank == slot) & (member > 0.0))
        named = one_hot(iota((slots, 128), 1) == ROPE + s)
        slot = iota((slots, tok_rows), 0).astype(f32)
        for block in range(4):
            tail = tail_of(line * 4 + block)
            member = lax.dot_general(named, tail, pair, preferred_element_type=f32)
            rank = jnp.dot(member.astype(bf16), before, preferred_element_type=f32)
            mine = one_hot((rank == slot) & (member > 0.0))
            chosen = jnp.dot(mine, tail, preferred_element_type=f32)
            known = iota((slots, 128), 1)
            known = (known >= ROPE) & (known < ROPE + expert_count)
            chosen_buf[k, block * slots : (block + 1) * slots] = jnp.where(known, chosen, 0.0)

    prepare(0)
    router = router_ref[...]
    high = router.astype(bf16)
    rest = router - high.astype(f32)
    middle = rest.astype(bf16)
    last = (rest - middle.astype(f32)).astype(bf16)
    top_pad = jnp.zeros((ROPE, cols), bf16)
    low_pad = jnp.zeros((128 - ROPE - 3 * expert_count, cols), bf16)
    router_buf[...] = jnp.concatenate([top_pad, high, middle, last, low_pad], axis=0)

    for piece in range(2):
        swap(piece).wait_recv()

    def joined(piece):
        here = slice(piece * half, (piece + 1) * half)
        both = attn_buf[piece].astype(f32) + attn_in[piece].astype(f32)
        return hidden_ref[:, here].astype(f32) + both

    sums = [joined(0), joined(1)]
    square = sums[0] * sums[0] + sums[1] * sums[1]
    inverse = lax.rsqrt(jnp.sum(square, axis=1, keepdims=True) / cols + EPSILON)
    mine = jnp.where(h == 0, sums[0], sums[1])
    mixed[...] = mine
    gain = ffn_gain_ref[...]
    own_gain = jnp.where(h == 0, gain[:, :half], gain[:, half:])
    x_buf[z] = (mine * inverse * own_gain).astype(bf16)

    def ring(t, q):
        @pl.when((t >= 1) & (t <= z))
        def _():
            up_in(t, q).wait_recv()

        @pl.when((t <= z) & (z < 3))
        def _():
            up(t, q).start()

        @pl.when((t >= 1) & (t <= 3 - z))
        def _():
            low_in(t, q).wait_recv()

        @pl.when((t <= 3 - z) & (z > 0))
        def _():
            low(t, q).start()

    def pick(k, q):
        here = part_of(q)
        rows = jnp.dot(
            pick_buf[k], x_buf[turn_line(z, k), :, here], preferred_element_type=f32
        )
        stage[k, :, :, here] = rows.astype(bf16).reshape(4, slots, half // PIECES)
        for step in (3, 1, 2):
            go(k, step, q).start()
        rows_in[k, h, c, :, here] = stage[k, c, :, here]

    def meet_rows(k):
        share(k, 0).start()
        for step in (1, 2, 3):
            for q in range(PIECES):
                go_in(k, step, q).wait_recv()
            share(k, step).start()

    def work(k):
        for step in range(4):
            share_in(k, step).wait_recv()
        rows = jnp.concatenate(
            [rows_in[k, 0].reshape(four, half), rows_in[k, 1].reshape(four, half)], axis=1
        )
        logit = lax.dot_general(rows, router_buf[...], pair, preferred_element_type=f32)
        logit = logit + (
            pltpu.roll(logit, 128 - expert_count, 1) + pltpu.roll(logit, 128 - 2 * expert_count, 1)
        )
        score = 1.0 / (1.0 + jnp.exp(-logit))
        chosen = jnp.where(chosen_buf[k] > 0.0, score, 0.0)
        own = jnp.where(iota(chosen.shape, 1) == ROPE + s, chosen, 0.0)
        own = jnp.sum(own, axis=1, keepdims=True)
        every = jnp.sum(chosen, axis=1, keepdims=True)
        weight = ROUTE_SCALE * own / jnp.where(every > 0.0, every, 1.0)
        gate = lax.dot_general(rows, gate_up[0], pair, preferred_element_type=f32)
        rise = lax.dot_general(rows, gate_up[1], pair, preferred_element_type=f32)
        act = (gate / (1.0 + jnp.exp(-gate)) * rise * weight).astype(bf16)
        for owner in (1 - h, h):
            here = pl.ds(pl.multiple_of(owner * half, half), half)
            out = jnp.dot(act, down[:, here], preferred_element_type=f32).astype(bf16)
            res[k, owner] = out.reshape(4, slots, half)
            if owner is not h:
                part(k).start()

    def send_back(k):
        part(k).wait_recv()
        for q in range(PIECES):
            here = part_of(q)
            both = res[k, h, :, :, here].astype(f32) + sib_in[k, :, :, here].astype(f32)
            res[k, h, :, :, here] = both.astype(bf16)
            for step in (3, 1, 2):
                ret(k, step, q).start()
            ret_in[k, c, :, here] = res[k, h, c, :, here]

    def place(k, q):
        for step in (1, 2, 3):
            ret_back(k, step, q).wait_recv()
        rows = ret_in[k, :, :, part_of(q)].reshape(four, half // PIECES)
        return jnp.dot(place_buf[k], rows, preferred_element_type=f32)

    def go_home(k, between=None):
        sums = [place(k, q) for q in range(PIECES)]
        if between:
            between()
        for q in range(PIECES):
            if k == 1:
                z_out[k, :, part_of(q)] = sums[q].astype(bf16)
                home(k, q).start()
                continue

            @pl.when(inner == 0)
            def _():
                z_out[k, :, part_of(q)] = sums[q].astype(bf16)
                relay(k, q).start()

            @pl.when(inner == 1)
            def _():
                relay(k, q).wait_recv()
                both = sums[q] + relay_buf[k - 2, :, part_of(q)].astype(f32)
                z_out[k, :, part_of(q)] = both.astype(bf16)
                home(k, q).start()

    def decode_rows():
        span = keys_buf.shape[0] * tok_rows
        keys = keys_buf[...].reshape(span, keys_buf.shape[3])
        shape = (slot_ref.shape[1], span)
        spread = one_hot(lax.div(iota(shape, 1), BLOCK) == iota(shape, 0))
        device_slot = (2 * s + h) * DEC_SLOTS

        def rows_of(slot, row, values):
            named = one_hot(slot_ref[...] == slot)
            blocks = jnp.dot(named, spread, preferred_element_type=f32)
            same = lax.rem(iota(blocks.shape, 1), BLOCK) == row
            picked = one_hot(same & (blocks > 0.0))
            return jnp.dot(picked, values, preferred_element_type=f32)

        place = iota((DEC_SLOTS * BLOCK, 1), 0)
        latent = rows_of(
            device_slot + lax.div(place, BLOCK), lax.rem(place, BLOCK), keys[:, :KV_RANK]
        )
        latent_ref[...] = latent.astype(bf16)
        place = iota((8 * BLOCK, 1), 0)
        slot = lax.rem(place, 8)
        slot = jnp.where(slot < DEC_SLOTS, device_slot + slot, -1)
        rope = rows_of(slot, lax.div(place, 8), keys[:, KV_RANK:])
        pieces = []
        for two in range(BLOCK // 2):
            left = rope[16 * two : 16 * two + 8]
            right = pltpu.roll(rope[16 * two + 8 : 16 * two + 16], ROPE, 1)
            pieces.append(jnp.where(iota(left.shape, 1) < ROPE, left, right))
        flat = jnp.concatenate(pieces, axis=1)
        rope_ref[...] = flat[:DEC_SLOTS].astype(bf16)

    @pl.loop(0, 6)
    def _(t):
        @pl.when(t <= 3)
        def _():
            for q in range(PIECES):
                ring(t, q)
                pick(t, q)

        @pl.when(t == 0)
        def _():
            @pl.loop(1, 4)
            def _(k):
                prepare(k)

        @pl.when(t == 1)
        def _():
            loads[4].wait()
            loads[5].wait()

        @pl.when((t >= 1) & (t <= 4))
        def _():
            meet_rows(t - 1)

        @pl.when(t >= 3)
        def _():
            send_back(t - 2)

        @pl.when((t >= 1) & (t <= 4))
        def _():
            work(t - 1)

        @pl.when(t == 4)
        def _():
            go_home(1)

    go_home(2)
    go_home(3, lambda: send_back(0))
    decode_rows()
    for q in range(PIECES):
        here = part_of(q)
        mixed[:, here] = mixed[:, here] + place(0, q)
    for q in range(PIECES):
        here = part_of(q)
        result = mixed[:, here]
        for line in (flip(z, 1), 2 - lax.div(z, 2)):
            home_in(line, q).wait_recv()
            result = result + z_in[line, :, here].astype(f32)
        out_ref[:, here] = result.astype(out_ref.dtype)
    for piece in range(2):
        swap(piece).wait_send()

    @pl.loop(0, 4)
    def _(k):
        for q in range(PIECES):
            @pl.when((k <= z) & (z < 3))
            def _():
                up(k, q).wait_send()

            @pl.when((k <= 3 - z) & (z > 0))
            def _():
                low(k, q).wait_send()

            for step in (1, 2, 3):
                go(k, step, q).wait_send()
                ret(k, step, q).wait_send()

            @pl.when(k > 0)
            def _():
                home(k, q).wait_send()

        for step in range(4):
            share(k, step).wait_send()
        part(k).wait_send()

    @pl.loop(0, 4)
    def _(k):
        @pl.when((k <= z) & (z < 3))
        def _():
            key_up_move(k).wait_send()

        @pl.when((k <= 3 - z) & (z > 0))
        def _():
            key_low_move(k).wait_send()

        for step in (1, 2, 3):
            plane(k, step).wait_send()
        share_keys(k).wait_send()


def layer(
    req_len,
    req_offset,
    hidden,
    attn_gain,
    kv_down,
    kv_gain,
    expert_ids,
    decode_slot,
    ffn_gain,
    router,
    queries,
    key_up,
    value_up,
    out_proj,
    gate_up,
    down,
    seq_count,
):
    tok_rows, cols = hidden.shape
    half = cols // 2
    heads = key_up.shape[0]
    width = KV_RANK + 128
    slots = max(2, tok_rows * TOP * 4 // (3 * router.shape[1]))
    lanes = np.arange(128) % (ROPE // 2)
    frequency = np.exp(-math.log(ROPE_BASE) * lanes * (2.0 / ROPE)).astype(np.float32)[None, :]
    bf16, f32 = jnp.bfloat16, jnp.float32
    vmem = pl.BlockSpec(memory_space=pltpu.VMEM)
    smem = pl.BlockSpec(memory_space=pltpu.SMEM)
    hbm = pl.BlockSpec(memory_space=pl.ANY)
    dma = pltpu.SemaphoreType.DMA
    part_rows = heads * tok_rows // 2
    sizes = [7] + [4] * 4 + [12] * 2 + [4] * 2 + [2] * 2
    sizes += [4 * PIECES] * 4 + [12 * PIECES] * 2 + [16] * 2 + [4] * 2
    sizes += [12 * PIECES] * 2 + [4 * PIECES] * 2
    return pl.pallas_call(
        layer_kernel,
        out_shape=(
            jax.ShapeDtypeStruct((tok_rows, half), bf16),
            jax.ShapeDtypeStruct((DEC_SLOTS * BLOCK, KV_RANK), bf16),
            jax.ShapeDtypeStruct((DEC_SLOTS, BLOCK * ROPE), bf16),
        ),
        in_specs=[smem] * 2 + [vmem] * 8 + [hbm] * 7,
        out_specs=(vmem, vmem, vmem),
        scratch_shapes=[
            pltpu.VMEM(kv_down.shape[::-1], bf16),
            pltpu.VMEM((seq_count, 2, tok_rows // 2, width), bf16),
            pltpu.VMEM(queries.shape, bf16),
            pltpu.VMEM(key_up.shape, bf16),
            pltpu.VMEM(value_up.shape, bf16),
            pltpu.VMEM(out_proj.shape, bf16),
            pltpu.VMEM((heads * tok_rows, width), bf16),
            pltpu.VMEM((2, part_rows, KV_RANK), f32),
            pltpu.VMEM((2, part_rows, 128), f32),
            pltpu.VMEM((2, part_rows, 128), f32),
            pltpu.VMEM((tok_rows, heads * V_HEAD), bf16),
            pltpu.VMEM((2, tok_rows, half), bf16),
            pltpu.VMEM((2, tok_rows, half), bf16),
            pltpu.VMEM((tok_rows, half), f32),
            pltpu.VMEM((4, tok_rows, half), bf16),
            pltpu.VMEM((4, 4, slots, half), bf16),
            pltpu.VMEM((4, 2, 4, slots, half), bf16),
            pltpu.VMEM((4, 2, 4, slots, half), bf16),
            pltpu.VMEM((4, 4, slots, half), bf16),
            pltpu.VMEM((4, 4, slots, half), bf16),
            pltpu.VMEM((4, tok_rows, half), bf16),
            pltpu.VMEM((4, tok_rows, half), bf16),
            pltpu.VMEM((4, 4 * slots, tok_rows), bf16),
            pltpu.VMEM((4, tok_rows, 4 * slots), bf16),
            pltpu.VMEM((4, 4 * slots, 128), f32),
            pltpu.VMEM((128, cols), bf16),
            pltpu.VMEM(gate_up.shape, bf16),
            pltpu.VMEM(down.shape, bf16),
        ]
        + [dma((size,)) for size in sizes]
        + [pltpu.VMEM((2, tok_rows, half), bf16), dma((2 * PIECES,))],
        compiler_params=pltpu.CompilerParams(
            collective_id=0, has_side_effects=True, vmem_limit_bytes=60 * 1024 * 1024
        ),
    )(
        req_len,
        req_offset,
        jnp.asarray(frequency),
        hidden,
        attn_gain[None, :],
        kv_gain[None, :],
        expert_ids.T,
        decode_slot[None, :],
        ffn_gain[None, :],
        router.T,
        kv_down.T,
        queries,
        key_up,
        value_up,
        out_proj,
        gate_up,
        down,
    )


def body(
    hidden,
    queries,
    req_len,
    req_offset,
    expert_ids,
    decode_slot,
    attn_gain,
    kv_down,
    kv_gain,
    key_up,
    value_up,
    out_proj,
    ffn_gain,
    router,
    expert_gate_up,
    expert_down,
):
    head_count = lax.axis_size("head")
    seq_place = lax.axis_index("seq")
    head_place = lax.axis_index("head")
    tok_rows = hidden.shape[0]
    heads_here = key_up.shape[0]
    my_index = seq_place * tok_rows + jnp.arange(tok_rows, dtype=jnp.int32)
    my_request = request_of(req_len, my_index)
    my_turn = angles(position_of(req_len, req_offset, my_index), ROPE)
    normed = rms_rows(hidden, attn_gain).astype(jnp.bfloat16)
    head_view = queries.reshape(tok_rows, heads_here, NOPE + ROPE)
    query_rope = rotate(head_view[:, :, NOPE:], my_turn[:, None, :]).astype(jnp.bfloat16)
    query_latent = jnp.einsum(
        "thn,hnc->thc", head_view[:, :, :NOPE], key_up, preferred_element_type=jnp.float32
    ).astype(jnp.bfloat16)
    query_rows = tok_rows * heads_here
    flat_latent = query_latent.reshape(query_rows, KV_RANK)
    flat_rope = query_rope.reshape(query_rows, ROPE)
    row_token = jnp.repeat(my_index, heads_here)
    row_request = jnp.repeat(my_request, heads_here)
    score_scale = 1.0 / math.sqrt(NOPE + ROPE)
    my_device = seq_place * head_count + head_place
    slot_ids = my_device * DEC_SLOTS + jnp.arange(DEC_SLOTS, dtype=jnp.int32)
    block_ids = jnp.arange(decode_slot.shape[0], dtype=jnp.int32)
    slot_match = decode_slot[None, :] == slot_ids[:, None]
    source_block = jnp.sum(jnp.where(slot_match, block_ids[None, :], 0), axis=1)
    slot_filled = jnp.any(slot_match, axis=1)
    kv_full = jnp.dot(normed, kv_down, preferred_element_type=jnp.float32)
    latent = rms_rows(kv_full[:, :KV_RANK], kv_gain).astype(jnp.bfloat16)
    key_rope = rotate(kv_full[:, KV_RANK:], my_turn).astype(jnp.bfloat16)
    run_peak = jnp.full((query_rows,), MASKED, jnp.float32)
    run_total = jnp.zeros((query_rows,), jnp.float32)
    run_acc = jnp.zeros((query_rows, KV_RANK), jnp.float32)
    expert_count = router.shape[1]
    expert_axis = jnp.arange(expert_count, dtype=jnp.int32)
    seq_count = lax.axis_size("seq")
    fast = seq_count == 16 and head_count == 2 and expert_count == 16
    if fast:
        output, decode_latent, decode_rope = layer(
            req_len,
            req_offset,
            hidden,
            attn_gain,
            kv_down,
            kv_gain,
            expert_ids,
            decode_slot,
            ffn_gain,
            router,
            queries,
            key_up,
            value_up,
            out_proj,
            jnp.swapaxes(expert_gate_up[0], 1, 2),
            expert_down[0],
            seq_count,
        )
        decode_latent = decode_latent.reshape(DEC_SLOTS, BLOCK, KV_RANK)
        return (output, decode_latent, decode_rope)
    else:
        piece_latent = lax.all_gather(latent, "seq", axis=0, tiled=True)
        piece_rope = lax.all_gather(key_rope, "seq", axis=0, tiled=True)
    piece_rows = piece_latent.shape[0]
    block_width = key_width(piece_rows)

    def key_block(block_no, loop_state):
        peak_now, total_now, acc_now = loop_state
        offset_rows = block_no * block_width
        block_latent = lax.dynamic_slice_in_dim(piece_latent, offset_rows, block_width, 0)
        block_rope = lax.dynamic_slice_in_dim(piece_rope, offset_rows, block_width, 0)
        key_index = offset_rows + jnp.arange(block_width, dtype=jnp.int32)
        key_request = request_of(req_len, key_index)
        contract = (((1,), (1,)), ((), ()))
        scores = lax.dot_general(
            flat_latent, block_latent, contract, preferred_element_type=jnp.float32
        )
        scores = (
            scores
            + lax.dot_general(flat_rope, block_rope, contract, preferred_element_type=jnp.float32)
        ) * score_scale
        allowed = (key_index[None, :] <= row_token[:, None]) & (
            key_request[None, :] == row_request[:, None]
        )
        scores = jnp.where(allowed, scores, MASKED)
        new_peak = jnp.maximum(peak_now, jnp.max(scores, axis=1))
        exp_terms = jnp.where(allowed, jnp.exp(scores - new_peak[:, None]), 0.0)
        fade_factor = jnp.exp(peak_now - new_peak)
        total_now = total_now * fade_factor + jnp.sum(exp_terms, axis=1)
        acc_now = acc_now * fade_factor[:, None] + jnp.dot(
            exp_terms.astype(jnp.bfloat16), block_latent, preferred_element_type=jnp.float32
        )
        return (new_peak, total_now, acc_now)

    run_peak, run_total, run_acc = lax.fori_loop(
        0, piece_rows // block_width, key_block, (run_peak, run_total, run_acc)
    )
    block_count = piece_rows // BLOCK
    pick_matrix = (
        source_block[:, None] == jnp.arange(block_count, dtype=jnp.int32)[None, :]
    ) & slot_filled[:, None]
    pick_matrix = pick_matrix.astype(jnp.bfloat16)
    slot_latent = jnp.dot(
        pick_matrix,
        piece_latent.reshape(block_count, BLOCK * KV_RANK),
        preferred_element_type=jnp.float32,
    )
    slot_rope = jnp.dot(
        pick_matrix,
        piece_rope.reshape(block_count, BLOCK * ROPE),
        preferred_element_type=jnp.float32,
    )
    folded = (run_peak, run_total, run_acc, slot_latent, slot_rope)
    run_total = folded[1]
    run_acc = folded[2]
    slot_latent = folded[3]
    slot_rope = folded[4]
    attended = (
        (run_acc / run_total[:, None]).astype(jnp.bfloat16).reshape(tok_rows, heads_here, KV_RANK)
    )
    head_out = jnp.einsum(
        "thc,hcv->thv", attended, value_up, preferred_element_type=jnp.float32
    ).astype(jnp.bfloat16)
    attn_part = jnp.dot(
        head_out.reshape(tok_rows, heads_here * V_HEAD),
        out_proj,
        preferred_element_type=jnp.float32,
    )
    decode_latent = slot_latent.astype(jnp.bfloat16).reshape(DEC_SLOTS, BLOCK, KV_RANK)
    decode_rope = slot_rope.astype(jnp.bfloat16)
    mixed_rows = hidden.astype(jnp.float32) + lax.psum(
        attn_part.astype(jnp.bfloat16), "head"
    ).astype(jnp.float32)
    moe_in = rms_rows(mixed_rows, ffn_gain).astype(jnp.bfloat16)
    capacity = max(2, tok_rows * TOP * 4 // (3 * expert_count))
    gate_score = jax.nn.sigmoid(
        jnp.dot(moe_in.astype(jnp.float32), router, precision=lax.Precision.HIGHEST)
    )
    id_match = expert_ids[:, :, None] == expert_axis[None, None, :]
    chosen = jnp.sum(jnp.where(id_match, gate_score[:, None, :], 0.0), axis=2)
    gate_weight = ROUTE_SCALE * chosen / jnp.sum(chosen, axis=1, keepdims=True)
    flat_ids = expert_ids.reshape(-1)
    one_hot = (flat_ids[:, None] == expert_axis[None, :]).astype(jnp.int32)
    earlier = ranks(one_hot.T.astype(jnp.bfloat16)).T
    slot_rank = jnp.sum(earlier * one_hot, axis=1)
    flat_slot = flat_ids * capacity + slot_rank
    owner_token = jnp.repeat(jnp.arange(tok_rows, dtype=jnp.int32), TOP)
    slot_token = jnp.zeros((expert_count * capacity,), jnp.int32).at[flat_slot].set(owner_token)
    slot_used = jnp.zeros((expert_count * capacity,), jnp.bool_).at[flat_slot].set(True)
    send_rows = jnp.where(
        slot_used[:, None], moe_in[slot_token], jnp.zeros((), jnp.bfloat16)
    ).reshape(expert_count, capacity, D)
    gate_up_local = expert_gate_up[0]
    down_local = expert_down[0]
    quarter_cols = D // head_count
    arrived = lax.all_to_all(send_rows, "seq", split_axis=0, concat_axis=0, tiled=True)
    sources, item_count, width_cols = arrived.shape
    flat_rows = arrived.reshape(sources * item_count, width_cols)
    gate_part = jnp.dot(flat_rows, gate_up_local[0], preferred_element_type=jnp.float32)
    up_part = jnp.dot(flat_rows, gate_up_local[1], preferred_element_type=jnp.float32)
    activated = (jax.nn.silu(gate_part) * up_part).astype(jnp.bfloat16)
    part_out = (
        jnp.dot(activated, down_local, preferred_element_type=jnp.float32)
        .astype(jnp.bfloat16)
        .reshape(sources, item_count, width_cols)
    )
    returned = lax.all_to_all(part_out, "seq", split_axis=0, concat_axis=0, tiled=True)
    back_cols = returned.shape[2]
    picked = returned.reshape(expert_count * capacity, back_cols)[flat_slot].reshape(
        tok_rows, TOP, back_cols
    )
    weighted = jnp.sum(picked.astype(jnp.float32) * gate_weight[:, :, None], axis=1)
    moe_out = lax.psum_scatter(
        weighted.astype(jnp.bfloat16), "head", scatter_dimension=1, tiled=True
    ).astype(jnp.float32)
    residual_part = lax.dynamic_slice_in_dim(mixed_rows, head_place * quarter_cols, quarter_cols, 1)
    output = (residual_part + moe_out).astype(jnp.bfloat16)
    return (output, decode_latent, decode_rope)


def solution(mesh):
    placed = (
        P("seq", None),
        P("seq", "head"),
        P(),
        P(),
        P("seq", None),
        P(),
        P(),
        P(),
        P(),
        P("head", None, None),
        P("head", None, None),
        P("head", None),
        P(),
        P(),
        P("seq", None, None, "head"),
        P("seq", "head", None),
    )
    return jax.shard_map(
        body,
        mesh=mesh,
        in_specs=placed,
        out_specs=(P("seq", "head"), P(("seq", "head"), None, None), P(("seq", "head"), None)),
        check_vma=False,
    )
```

```python
import functools
import math

import jax
import jax.numpy as jnp
import numpy as np
from jax import lax
from jax.experimental import pallas as pl
from jax.experimental.pallas import tpu as pltpu
from jax.sharding import PartitionSpec as P

D = 2048
NOPE = 128
ROPE = 64
V_HEAD = 128
KV_RANK = 512
TOP = 6
BLOCK = 16
DEC_SLOTS = 4


ROPE_BASE = 50000.0
ROUTE_SCALE = 2.446
EPSILON = 1e-06
MASKED = -1e30
PIECES = 2


def rms_rows(values, scale_gain):
    values = values.astype(jnp.float32)
    inverse = lax.rsqrt(jnp.mean(values * values, axis=-1, keepdims=True) + EPSILON)
    return values * inverse * scale_gain


def angles(position, rope_width):
    half_width = rope_width // 2
    freq_steps = jnp.arange(half_width).astype(jnp.float32) * (2.0 / rope_width)
    frequency = jnp.exp(-math.log(ROPE_BASE) * freq_steps)
    return position.astype(jnp.float32)[:, None] * frequency[None, :]


def rotate(values, rot_angle):
    half_width = values.shape[-1] // 2
    first_half = values[..., :half_width].astype(jnp.float32)
    second_half = values[..., half_width:].astype(jnp.float32)
    cosine = jnp.cos(rot_angle)
    sine_part = jnp.sin(rot_angle)
    return jnp.concatenate(
        [
            first_half * cosine - second_half * sine_part,
            first_half * sine_part + second_half * cosine,
        ],
        axis=-1,
    )


def running(lengths):
    index = jnp.arange(lengths.shape[0])
    return jnp.sum(jnp.where(index[None, :] <= index[:, None], lengths[None, :], 0), axis=1)


def ranks(member):
    count = member.shape[-1]
    index = jnp.arange(count)
    before = (index[:, None] < index[None, :]).astype(jnp.bfloat16)
    return jnp.dot(member, before, preferred_element_type=jnp.float32).astype(jnp.int32)


def request_of(req_len, token_index):
    req_ends = running(req_len)
    return jnp.sum((token_index[:, None] >= req_ends[None, :]).astype(jnp.int32), axis=1)


def position_of(req_len, req_offset, token_index):
    request = request_of(req_len, token_index)
    req_ends = running(req_len)
    starts = req_ends - req_len
    member = request[:, None] == jnp.arange(req_len.shape[0])[None, :]
    start_at = jnp.sum(jnp.where(member, starts[None, :], 0), axis=1)
    offset = jnp.sum(jnp.where(member, req_offset[None, :], 0), axis=1)
    return offset + token_index - start_at


def key_width(piece_rows):
    for option_width in (1024, 512, 256, 128):
        return option_width
    return piece_rows


MESH = pl.DeviceIdType.MESH


def flip(place, step):
    return place + step * (1 - 2 * lax.rem(lax.div(place, step), 2))


def line_place(line, s):
    return line * 4 + lax.rem(s, 4)


def across(s, step):
    if step & 1:
        s = flip(s, 1)
    if step & 2:
        s = flip(s, 2)
    return s


def turn_line(z, k):
    upper = lax.div(z, 2)
    near = z + upper * (3 - 2 * z)
    late = lax.div(k, 2)
    line = late * k + (1 - late) * (near + k * (1 - 2 * near))
    return line + upper * (3 - 2 * line)


def layer_kernel(
    req_len_ref,
    req_offset_ref,
    freq_ref,
    hidden_ref,
    gain_ref,
    kv_gain_ref,
    ids_ref,
    slot_ref,
    ffn_gain_ref,
    router_ref,
    kv_hbm,
    queries_hbm,
    key_up_hbm,
    value_up_hbm,
    out_proj_hbm,
    gate_up_hbm,
    down_hbm,
    out_ref,
    latent_ref,
    rope_ref,
    kv_buf,
    keys_buf,
    queries,
    key_up,
    value_up,
    out_proj,
    query,
    acc,
    peak,
    total,
    heads_buf,
    attn_buf,
    attn_in,
    mixed,
    x_buf,
    stage,
    rows_in,
    res,
    sib_in,
    ret_in,
    z_out,
    z_in,
    pick_buf,
    place_buf,
    chosen_buf,
    router_buf,
    gate_up,
    down,
    load_sem,
    ku_send,
    ku_recv,
    kl_send,
    kl_recv,
    plane_send,
    plane_recv,
    share_keys_send,
    share_keys_recv,
    swap_send,
    swap_recv,
    up_send,
    up_recv,
    down_send,
    down_recv,
    go_send,
    go_recv,
    share_send,
    share_recv,
    part_send,
    part_recv,
    ret_send,
    ret_recv,
    home_send,
    home_recv,
    relay_buf,
    relay_recv,
):
    s, h = lax.axis_index("seq"), lax.axis_index("head")
    z, c = lax.div(s, 4), lax.rem(s, 4)
    bf16, f32 = jnp.bfloat16, jnp.float32
    pair = (((1,), (1,)), ((), ()))
    tok_rows = hidden_ref.shape[0]
    rows_half = tok_rows // 2
    heads = key_up.shape[0]
    part_heads = heads // 2
    part_rows = part_heads * tok_rows
    tile_keys = 4 * tok_rows
    sibling = (s, 1 - h)
    pairs = [(queries_hbm, queries), (key_up_hbm, key_up)]
    pairs += [(value_up_hbm, value_up), (out_proj_hbm, out_proj)]
    pairs += [(gate_up_hbm, gate_up), (down_hbm, down)]
    pairs += [(kv_hbm, kv_buf)]
    loads = [pltpu.make_async_copy(*both, load_sem.at[i]) for i, both in enumerate(pairs)]
    for index in (6, 0, 1):
        loads[index].start()

    barrier = pltpu.get_barrier_semaphore()
    peers = [(line_place(lax.rem(z + back, 4), s), h) for back in range(1, 4)]
    peers += [(across(s, step), h) for step in range(1, 4)] + [sibling]
    for peer in peers:
        pl.semaphore_signal(barrier, inc=1, device_id=peer, device_id_type=MESH)

    def iota(shape, dim):
        return lax.broadcasted_iota(jnp.int32, shape, dim)

    def remote(src, dst, send, recv, device):
        return pltpu.make_async_remote_copy(
            src_ref=src,
            dst_ref=dst,
            send_sem=send,
            recv_sem=recv,
            device_id=device,
            device_id_type=MESH,
        )

    def key_up_move(t):
        view = keys_buf.at[(z - t) * 4 + c, h]
        device = (line_place(lax.rem(z + 1, 4), s), h)
        return remote(view, view, ku_send.at[t], ku_recv.at[t], device)

    def key_up_in(t):
        view = keys_buf.at[(z - t) * 4 + c, h]
        return remote(view, view, ku_send.at[t - 1], ku_recv.at[t - 1], sibling)

    def key_low_move(t):
        view = keys_buf.at[(z + t) * 4 + c, h]
        device = (line_place(lax.rem(z + 3, 4), s), h)
        return remote(view, view, kl_send.at[t], kl_recv.at[t], device)

    def key_low_in(t):
        view = keys_buf.at[(z + t) * 4 + c, h]
        return remote(view, view, kl_send.at[t - 1], kl_recv.at[t - 1], sibling)

    def line_of(k):
        return jnp.where(k <= z, z - k, k)

    def plane(k, step):
        view = keys_buf.at[line_of(k) * 4 + c, h]
        index = 3 * k + step - 1
        device = (across(s, step), h)
        return remote(view, view, plane_send.at[index], plane_recv.at[index], device)

    def plane_in(k, step):
        view = keys_buf.at[line_of(k) * 4 + lax.rem(across(s, step), 4), h]
        index = 3 * k + step - 1
        return remote(view, view, plane_send.at[index], plane_recv.at[index], sibling)

    def share_keys(k):
        view = keys_buf.at[pl.ds(line_of(k) * 4, 4), h]
        return remote(view, view, share_keys_send.at[k], share_keys_recv.at[k], sibling)

    def share_keys_in(k):
        view = keys_buf.at[pl.ds(line_of(k) * 4, 4), 1 - h]
        return remote(view, view, share_keys_send.at[k], share_keys_recv.at[k], sibling)

    def starts_of(token):
        first = jnp.zeros_like(token)
        offset = jnp.full_like(token, req_offset_ref[0])
        end = req_len_ref[0]
        for r in range(1, req_len_ref.shape[0]):
            later = token >= end
            first = jnp.where(later, end, first)
            offset = jnp.where(later, req_offset_ref[r], offset)
            end = end + req_len_ref[r]
        return first, offset

    def turns(token):
        first, offset = starts_of(token)
        angle = (offset + token - first).astype(f32) * freq_ref[...]
        lane = iota(angle.shape, 1)
        sine = jnp.sin(angle)
        sine = jnp.where(lane < ROPE // 2, -sine, sine)
        rotary = lane < ROPE
        return jnp.where(rotary, jnp.cos(angle), 0.0), jnp.where(rotary, sine, 0.0)

    def spin(values, turn):
        lane = iota(values.shape, 1)
        other = jnp.where(
            lane < ROPE // 2,
            pltpu.roll(values, 128 - ROPE // 2, 1),
            pltpu.roll(values, ROPE // 2, 1),
        )
        return (values * turn[0] + other * turn[1]).astype(bf16)

    base = s * tok_rows
    rows = hidden_ref[pl.ds(pl.multiple_of(h * rows_half, rows_half), rows_half), :].astype(f32)
    inverse = lax.rsqrt(jnp.mean(rows * rows, axis=1, keepdims=True) + EPSILON)
    normed = (rows * inverse * gain_ref[...]).astype(bf16)
    loads[6].wait()
    full = lax.dot_general(normed, kv_buf[:KV_RANK], pair, preferred_element_type=f32)
    end = lax.dot_general(
        normed, kv_buf[KV_RANK + ROPE - 128 :], pair, preferred_element_type=f32
    )
    inverse = lax.rsqrt(jnp.mean(full * full, axis=1, keepdims=True) + EPSILON)
    keys_buf[s, h, :, :KV_RANK] = (full * inverse * kv_gain_ref[...]).astype(bf16)
    half_token = base + h * rows_half + iota((rows_half, 1), 0)
    key_rope = spin(pltpu.roll(end, ROPE, 1), turns(half_token))
    named = jnp.zeros((128, tok_rows), f32)
    place = iota(named.shape, 0) - ROPE
    for k in range(ids_ref.shape[0]):
        named = jnp.where(ids_ref[k : k + 1, :] == place, 1.0, named)
    row_pick = iota((rows_half, tok_rows), 1) == h * rows_half + iota((rows_half, tok_rows), 0)
    row_pick = jnp.where(row_pick, 1.0, 0.0).astype(bf16)
    mask = lax.dot_general(row_pick, named.astype(bf16), pair, preferred_element_type=f32)
    keys_buf[s, h, :, KV_RANK:] = (key_rope.astype(f32) + mask).astype(bf16)
    pl.semaphore_wait(barrier, len(peers))

    def key_ring(t):
        @pl.when((t >= 1) & (t <= z))
        def _():
            key_up_in(t).wait_recv()

        @pl.when((t <= z) & (z < 3))
        def _():
            key_up_move(t).start()

        @pl.when((t >= 1) & (t <= 3 - z))
        def _():
            key_low_in(t).wait_recv()

        @pl.when((t <= 3 - z) & (z > 0))
        def _():
            key_low_move(t).start()

        for step in (3, 1, 2):
            plane(t, step).start()

    def meet_keys(k):
        for step in (1, 2, 3):
            plane_in(k, step).wait_recv()
        share_keys(k).start()

    key_ring(0)
    for index in range(2, 6):
        loads[index].start()
    token = base + iota((tok_rows, 1), 0)
    scale = math.log2(math.e) / math.sqrt(NOPE + ROPE)
    turn = [scale * part for part in turns(token)]
    loads[0].wait()
    loads[1].wait()
    for two in range(heads // 2):
        if two == heads // 4:
            key_ring(1)
        left = queries[:, 384 * two : 384 * two + 128]
        middle = queries[:, 384 * two + 128 : 384 * two + 256].astype(f32)
        right = queries[:, 384 * two + 256 : 384 * two + 384].astype(f32)
        lane = iota(middle.shape, 1)
        turned = pltpu.roll(right, 64, 1)
        nope = jnp.where(lane < 64, pltpu.roll(middle, 64, 1), turned).astype(bf16)
        for odd, columns, rotary in ((0, left, middle), (1, nope, turned)):
            head = 2 * two + odd
            here = slice(head * tok_rows, (head + 1) * tok_rows)
            latent = jnp.dot(columns, key_up[head], preferred_element_type=f32)
            query[here, :KV_RANK] = (scale * latent).astype(bf16)
            query[here, KV_RANK:] = spin(rotary, turn)
    first = jnp.concatenate([starts_of(token)[0]] * part_heads, axis=0)
    own = jnp.concatenate([token] * part_heads, axis=0)
    def attend(k, part_no, leading=False):
        line = line_of(k)
        keys = keys_buf[pl.ds(line * 4, 4)].reshape(tile_keys, keys_buf.shape[3])
        here = slice(part_no * part_rows, (part_no + 1) * part_rows)
        scores = lax.dot_general(query[here, :], keys, pair, preferred_element_type=f32)
        index = line * tile_keys + iota(scores.shape, 1)
        allowed = index >= first
        if leading:
            allowed = allowed & (index <= own)
        scores = jnp.where(allowed, scores, MASKED)
        new = jnp.max(scores, axis=1, keepdims=True)
        if not leading:
            old = peak[part_no, :, :1]
            new = jnp.maximum(old, new)
            fade = jnp.exp2(old - new)
        terms = jnp.exp2(scores - new)
        norm = jnp.sum(terms, axis=1, keepdims=True)
        mixture = jnp.dot(terms.astype(bf16), keys[:, :KV_RANK], preferred_element_type=f32)
        if not leading:
            norm = total[part_no, :, :1] * fade + norm
            mixture = acc[part_no] * fade + mixture
        peak[part_no, :, :1] = new
        total[part_no, :, :1] = norm
        acc[part_no] = mixture

    meet_keys(0)
    key_ring(2)
    share_keys_in(0).wait_recv()
    attend(0, 0, True)
    key_ring(3)
    meet_keys(1)
    attend(0, 1, True)

    @pl.loop(1, 4)
    def _(k):
        share_keys_in(k).wait_recv()

        @pl.when(k <= z)
        def _():
            attend(k, 0)

        @pl.when(k <= 2)
        def _():
            meet_keys(k + 1)

        @pl.when(k <= z)
        def _():
            attend(k, 1)

    loads[2].wait()
    loads[3].wait()
    for head in range(heads):
        part_no, member = head // part_heads, head % part_heads
        here = slice(member * tok_rows, (member + 1) * tok_rows)
        attended = (acc[part_no, here, :] / total[part_no, here, :1]).astype(bf16)
        heads_buf[:, head * V_HEAD : (head + 1) * V_HEAD] = jnp.dot(
            attended, value_up[head], preferred_element_type=f32
        ).astype(bf16)
    cols = hidden_ref.shape[1]
    half = cols // 2

    def swap(piece):
        return remote(
            attn_buf.at[piece],
            attn_in.at[piece],
            swap_send.at[piece],
            swap_recv.at[piece],
            sibling,
        )

    for piece in range(2):
        here = slice(piece * half, (piece + 1) * half)
        attn_buf[piece] = jnp.dot(
            heads_buf[...], out_proj[:, here], preferred_element_type=f32
        ).astype(bf16)
        swap(piece).start()
    def part_of(q):
        return pl.ds(q * (half // PIECES), half // PIECES)

    def up(t, q):
        view = x_buf.at[z - t, :, part_of(q)]
        device = (line_place(lax.rem(z + 1, 4), s), h)
        index = PIECES * t + q
        return remote(view, view, up_send.at[index], up_recv.at[index], device)

    def up_in(t, q):
        view = x_buf.at[z - t, :, part_of(q)]
        index = PIECES * (t - 1) + q
        return remote(view, view, up_send.at[index], up_recv.at[index], sibling)

    def low(t, q):
        view = x_buf.at[z + t, :, part_of(q)]
        device = (line_place(lax.rem(z + 3, 4), s), h)
        index = PIECES * t + q
        return remote(view, view, down_send.at[index], down_recv.at[index], device)

    def low_in(t, q):
        view = x_buf.at[z + t, :, part_of(q)]
        index = PIECES * (t - 1) + q
        return remote(view, view, down_send.at[index], down_recv.at[index], sibling)

    def go(k, step, q):
        other = across(s, step)
        index = PIECES * (3 * k + step - 1) + q
        return remote(
            stage.at[k, lax.rem(other, 4), :, part_of(q)],
            rows_in.at[k, h, c, :, part_of(q)],
            go_send.at[index],
            go_recv.at[index],
            (other, h),
        )

    def go_in(k, step, q):
        index = PIECES * (3 * k + step - 1) + q
        view = rows_in.at[k, h, lax.rem(across(s, step), 4), :, part_of(q)]
        return remote(view, view, go_send.at[index], go_recv.at[index], sibling)

    def share(k, step):
        view = rows_in.at[k, h, lax.rem(across(s, step), 4)]
        index = 4 * k + step
        return remote(view, view, share_send.at[index], share_recv.at[index], sibling)

    def share_in(k, step):
        view = rows_in.at[k, 1 - h, lax.rem(across(s, step), 4)]
        index = 4 * k + step
        return remote(view, view, share_send.at[index], share_recv.at[index], sibling)

    def part(k):
        return remote(res.at[k, 1 - h], sib_in.at[k], part_send.at[k], part_recv.at[k], sibling)

    def ret(k, step, q):
        other = across(s, step)
        index = PIECES * (3 * k + step - 1) + q
        return remote(
            res.at[k, h, lax.rem(other, 4), :, part_of(q)],
            ret_in.at[k, c, :, part_of(q)],
            ret_send.at[index],
            ret_recv.at[index],
            (other, h),
        )

    def ret_back(k, step, q):
        index = PIECES * (3 * k + step - 1) + q
        view = ret_in.at[k, lax.rem(across(s, step), 4), :, part_of(q)]
        return remote(view, view, ret_send.at[index], ret_recv.at[index], sibling)

    def home(k, q):
        owner = (line_place(turn_line(z, k), s), h)
        return remote(
            z_out.at[k, :, part_of(q)],
            z_in.at[z, :, part_of(q)],
            home_send.at[PIECES * k + q],
            home_recv.at[PIECES * z + q],
            owner,
        )

    def relay(k, q):
        inner_side = (line_place(flip(z, 1), s), h)
        return remote(
            z_out.at[k, :, part_of(q)],
            relay_buf.at[k - 2, :, part_of(q)],
            home_send.at[PIECES * k + q],
            relay_recv.at[PIECES * (k - 2) + q],
            inner_side,
        )

    def home_in(line, q):
        view = z_in.at[line, :, part_of(q)]
        return remote(view, view, home_send.at[q], home_recv.at[PIECES * line + q], sibling)

    inner = lax.rem(z + lax.div(z, 2), 2)
    slots = stage.shape[2]
    expert_count = router_ref.shape[0]
    four = 4 * slots
    before = (iota((tok_rows, tok_rows), 0) < iota((tok_rows, tok_rows), 1)).astype(bf16)
    after = (iota((tok_rows, tok_rows), 0) > iota((tok_rows, tok_rows), 1)).astype(bf16)

    def one_hot(flags):
        return jnp.where(flags, 1.0, 0.0).astype(bf16)

    def tail_of(block):
        return keys_buf[block, :, :, KV_RANK:].reshape(tok_rows, 128)

    def prepare(k):
        line = turn_line(z, k)
        tail = tail_of(line * 4 + c)
        shape = (four, 128)
        named = one_hot(iota(shape, 1) == ROPE + 4 * z + lax.div(iota(shape, 0), slots))
        slot = lax.rem(iota((four, tok_rows), 0), slots).astype(f32)
        member = lax.dot_general(named, tail, pair, preferred_element_type=f32)
        rank = jnp.dot(member.astype(bf16), before, preferred_element_type=f32)
        pick_buf[k] = one_hot((rank == slot) & (member > 0.0))
        shape = (128, four)
        named = one_hot(iota(shape, 0) == ROPE + 4 * z + lax.div(iota(shape, 1), slots))
        slot = lax.rem(iota((tok_rows, four), 1), slots).astype(f32)
        member = jnp.dot(tail, named, preferred_element_type=f32)
        rank = jnp.dot(after, member.astype(bf16), preferred_element_type=f32)
        place_buf[k] = one_hot((rank == slot) & (member > 0.0))
        named = one_hot(iota((slots, 128), 1) == ROPE + s)
        slot = iota((slots, tok_rows), 0).astype(f32)
        for block in range(4):
            tail = tail_of(line * 4 + block)
            member = lax.dot_general(named, tail, pair, preferred_element_type=f32)
            rank = jnp.dot(member.astype(bf16), before, preferred_element_type=f32)
            mine = one_hot((rank == slot) & (member > 0.0))
            chosen = jnp.dot(mine, tail, preferred_element_type=f32)
            known = iota((slots, 128), 1)
            known = (known >= ROPE) & (known < ROPE + expert_count)
            chosen_buf[k, block * slots : (block + 1) * slots] = jnp.where(known, chosen, 0.0)

    prepare(0)
    router = router_ref[...]
    high = router.astype(bf16)
    rest = router - high.astype(f32)
    middle = rest.astype(bf16)
    last = (rest - middle.astype(f32)).astype(bf16)
    top_pad = jnp.zeros((ROPE, cols), bf16)
    low_pad = jnp.zeros((128 - ROPE - 3 * expert_count, cols), bf16)
    router_buf[...] = jnp.concatenate([top_pad, high, middle, last, low_pad], axis=0)

    for piece in range(2):
        swap(piece).wait_recv()

    def joined(piece):
        here = slice(piece * half, (piece + 1) * half)
        both = attn_buf[piece].astype(f32) + attn_in[piece].astype(f32)
        return hidden_ref[:, here].astype(f32) + both

    sums = [joined(0), joined(1)]
    square = sums[0] * sums[0] + sums[1] * sums[1]
    inverse = lax.rsqrt(jnp.sum(square, axis=1, keepdims=True) / cols + EPSILON)
    mine = jnp.where(h == 0, sums[0], sums[1])
    mixed[...] = mine
    gain = ffn_gain_ref[...]
    own_gain = jnp.where(h == 0, gain[:, :half], gain[:, half:])
    x_buf[z] = (mine * inverse * own_gain).astype(bf16)

    def ring(t, q):
        @pl.when((t >= 1) & (t <= z))
        def _():
            up_in(t, q).wait_recv()

        @pl.when((t <= z) & (z < 3))
        def _():
            up(t, q).start()

        @pl.when((t >= 1) & (t <= 3 - z))
        def _():
            low_in(t, q).wait_recv()

        @pl.when((t <= 3 - z) & (z > 0))
        def _():
            low(t, q).start()

    def pick(k, q):
        here = part_of(q)
        rows = jnp.dot(
            pick_buf[k], x_buf[turn_line(z, k), :, here], preferred_element_type=f32
        )
        stage[k, :, :, here] = rows.astype(bf16).reshape(4, slots, half // PIECES)
        for step in (3, 1, 2):
            go(k, step, q).start()
        rows_in[k, h, c, :, here] = stage[k, c, :, here]

    def meet_rows(k):
        for step in (1, 2, 3):
            for q in range(PIECES):
                go_in(k, step, q).wait_recv()
            share(k, step).start()

    def work(k):
        for step in range(4):
            share_in(k, step).wait_recv()
        rows = jnp.concatenate(
            [rows_in[k, 0].reshape(four, half), rows_in[k, 1].reshape(four, half)], axis=1
        )
        logit = lax.dot_general(rows, router_buf[...], pair, preferred_element_type=f32)
        logit = logit + (
            pltpu.roll(logit, 128 - expert_count, 1) + pltpu.roll(logit, 128 - 2 * expert_count, 1)
        )
        score = 1.0 / (1.0 + jnp.exp(-logit))
        chosen = jnp.where(chosen_buf[k] > 0.0, score, 0.0)
        own = jnp.where(iota(chosen.shape, 1) == ROPE + s, chosen, 0.0)
        own = jnp.sum(own, axis=1, keepdims=True)
        every = jnp.sum(chosen, axis=1, keepdims=True)
        weight = ROUTE_SCALE * own / jnp.where(every > 0.0, every, 1.0)
        gate = lax.dot_general(rows, gate_up[0], pair, preferred_element_type=f32)
        rise = lax.dot_general(rows, gate_up[1], pair, preferred_element_type=f32)
        act = (gate / (1.0 + jnp.exp(-gate)) * rise * weight).astype(bf16)
        for owner in (1 - h, h):
            here = pl.ds(pl.multiple_of(owner * half, half), half)
            out = jnp.dot(act, down[:, here], preferred_element_type=f32).astype(bf16)
            res[k, owner] = out.reshape(4, slots, half)
            if owner is not h:
                part(k).start()

    def send_back(k):
        part(k).wait_recv()
        for q in range(PIECES):
            here = part_of(q)
            both = res[k, h, :, :, here].astype(f32) + sib_in[k, :, :, here].astype(f32)
            res[k, h, :, :, here] = both.astype(bf16)
            for step in (3, 1, 2):
                ret(k, step, q).start()
            ret_in[k, c, :, here] = res[k, h, c, :, here]

    def place(k, q):
        for step in (1, 2, 3):
            ret_back(k, step, q).wait_recv()
        rows = ret_in[k, :, :, part_of(q)].reshape(four, half // PIECES)
        return jnp.dot(place_buf[k], rows, preferred_element_type=f32)

    def go_home(k, between=None):
        sums = [place(k, q) for q in range(PIECES)]
        if between:
            between()
        for q in range(PIECES):
            if k == 1:
                z_out[k, :, part_of(q)] = sums[q].astype(bf16)
                home(k, q).start()
                continue

            @pl.when(inner == 0)
            def _():
                z_out[k, :, part_of(q)] = sums[q].astype(bf16)
                relay(k, q).start()

            @pl.when(inner == 1)
            def _():
                relay(k, q).wait_recv()
                both = sums[q] + relay_buf[k - 2, :, part_of(q)].astype(f32)
                z_out[k, :, part_of(q)] = both.astype(bf16)
                home(k, q).start()

    def decode_rows():
        span = keys_buf.shape[0] * tok_rows
        keys = keys_buf[...].reshape(span, keys_buf.shape[3])
        shape = (slot_ref.shape[1], span)
        spread = one_hot(lax.div(iota(shape, 1), BLOCK) == iota(shape, 0))
        device_slot = (2 * s + h) * DEC_SLOTS

        def rows_of(slot, row, values):
            named = one_hot(slot_ref[...] == slot)
            blocks = jnp.dot(named, spread, preferred_element_type=f32)
            same = lax.rem(iota(blocks.shape, 1), BLOCK) == row
            picked = one_hot(same & (blocks > 0.0))
            return jnp.dot(picked, values, preferred_element_type=f32)

        place = iota((DEC_SLOTS * BLOCK, 1), 0)
        latent = rows_of(
            device_slot + lax.div(place, BLOCK), lax.rem(place, BLOCK), keys[:, :KV_RANK]
        )
        latent_ref[...] = latent.astype(bf16)
        place = iota((8 * BLOCK, 1), 0)
        slot = lax.rem(place, 8)
        slot = jnp.where(slot < DEC_SLOTS, device_slot + slot, -1)
        rope = rows_of(slot, lax.div(place, 8), keys[:, KV_RANK:])
        pieces = []
        for two in range(BLOCK // 2):
            left = rope[16 * two : 16 * two + 8]
            right = pltpu.roll(rope[16 * two + 8 : 16 * two + 16], ROPE, 1)
            pieces.append(jnp.where(iota(left.shape, 1) < ROPE, left, right))
        flat = jnp.concatenate(pieces, axis=1)
        rope_ref[...] = flat[:DEC_SLOTS].astype(bf16)

    @pl.loop(0, 6)
    def _(t):
        @pl.when(t <= 3)
        def _():
            for q in range(PIECES):
                ring(t, q)
                pick(t, q)
            share(t, 0).start()

        @pl.when(t == 0)
        def _():
            @pl.loop(1, 4)
            def _(k):
                prepare(k)

        @pl.when(t == 1)
        def _():
            loads[4].wait()
            loads[5].wait()

        @pl.when((t >= 1) & (t <= 4))
        def _():
            meet_rows(t - 1)

        @pl.when(t >= 3)
        def _():
            send_back(t - 2)

        @pl.when((t >= 1) & (t <= 4))
        def _():
            work(t - 1)

        @pl.when(t == 4)
        def _():
            go_home(1)

    go_home(2)
    go_home(3, lambda: send_back(0))
    decode_rows()
    for q in range(PIECES):
        here = part_of(q)
        mixed[:, here] = mixed[:, here] + place(0, q)
    for q in range(PIECES):
        here = part_of(q)
        result = mixed[:, here]
        for line in (flip(z, 1), 2 - lax.div(z, 2)):
            home_in(line, q).wait_recv()
            result = result + z_in[line, :, here].astype(f32)
        out_ref[:, here] = result.astype(out_ref.dtype)
    for piece in range(2):
        swap(piece).wait_send()

    @pl.loop(0, 4)
    def _(k):
        for q in range(PIECES):
            @pl.when((k <= z) & (z < 3))
            def _():
                up(k, q).wait_send()

            @pl.when((k <= 3 - z) & (z > 0))
            def _():
                low(k, q).wait_send()

            for step in (1, 2, 3):
                go(k, step, q).wait_send()
                ret(k, step, q).wait_send()

            @pl.when(k > 0)
            def _():
                home(k, q).wait_send()

        for step in range(4):
            share(k, step).wait_send()
        part(k).wait_send()

    @pl.loop(0, 4)
    def _(k):
        @pl.when((k <= z) & (z < 3))
        def _():
            key_up_move(k).wait_send()

        @pl.when((k <= 3 - z) & (z > 0))
        def _():
            key_low_move(k).wait_send()

        for step in (1, 2, 3):
            plane(k, step).wait_send()
        share_keys(k).wait_send()


def layer(
    req_len,
    req_offset,
    hidden,
    attn_gain,
    kv_down,
    kv_gain,
    expert_ids,
    decode_slot,
    ffn_gain,
    router,
    queries,
    key_up,
    value_up,
    out_proj,
    gate_up,
    down,
    seq_count,
):
    tok_rows, cols = hidden.shape
    half = cols // 2
    heads = key_up.shape[0]
    width = KV_RANK + 128
    slots = max(2, tok_rows * TOP * 4 // (3 * router.shape[1]))
    lanes = np.arange(128) % (ROPE // 2)
    frequency = np.exp(-math.log(ROPE_BASE) * lanes * (2.0 / ROPE)).astype(np.float32)[None, :]
    bf16, f32 = jnp.bfloat16, jnp.float32
    vmem = pl.BlockSpec(memory_space=pltpu.VMEM)
    smem = pl.BlockSpec(memory_space=pltpu.SMEM)
    hbm = pl.BlockSpec(memory_space=pl.ANY)
    dma = pltpu.SemaphoreType.DMA
    part_rows = heads * tok_rows // 2
    sizes = [7] + [4] * 4 + [12] * 2 + [4] * 2 + [2] * 2
    sizes += [4 * PIECES] * 4 + [12 * PIECES] * 2 + [16] * 2 + [4] * 2
    sizes += [12 * PIECES] * 2 + [4 * PIECES] * 2
    return pl.pallas_call(
        layer_kernel,
        out_shape=(
            jax.ShapeDtypeStruct((tok_rows, half), bf16),
            jax.ShapeDtypeStruct((DEC_SLOTS * BLOCK, KV_RANK), bf16),
            jax.ShapeDtypeStruct((DEC_SLOTS, BLOCK * ROPE), bf16),
        ),
        in_specs=[smem] * 2 + [vmem] * 8 + [hbm] * 7,
        out_specs=(vmem, vmem, vmem),
        scratch_shapes=[
            pltpu.VMEM(kv_down.shape[::-1], bf16),
            pltpu.VMEM((seq_count, 2, tok_rows // 2, width), bf16),
            pltpu.VMEM(queries.shape, bf16),
            pltpu.VMEM(key_up.shape, bf16),
            pltpu.VMEM(value_up.shape, bf16),
            pltpu.VMEM(out_proj.shape, bf16),
            pltpu.VMEM((heads * tok_rows, width), bf16),
            pltpu.VMEM((2, part_rows, KV_RANK), f32),
            pltpu.VMEM((2, part_rows, 128), f32),
            pltpu.VMEM((2, part_rows, 128), f32),
            pltpu.VMEM((tok_rows, heads * V_HEAD), bf16),
            pltpu.VMEM((2, tok_rows, half), bf16),
            pltpu.VMEM((2, tok_rows, half), bf16),
            pltpu.VMEM((tok_rows, half), f32),
            pltpu.VMEM((4, tok_rows, half), bf16),
            pltpu.VMEM((4, 4, slots, half), bf16),
            pltpu.VMEM((4, 2, 4, slots, half), bf16),
            pltpu.VMEM((4, 2, 4, slots, half), bf16),
            pltpu.VMEM((4, 4, slots, half), bf16),
            pltpu.VMEM((4, 4, slots, half), bf16),
            pltpu.VMEM((4, tok_rows, half), bf16),
            pltpu.VMEM((4, tok_rows, half), bf16),
            pltpu.VMEM((4, 4 * slots, tok_rows), bf16),
            pltpu.VMEM((4, tok_rows, 4 * slots), bf16),
            pltpu.VMEM((4, 4 * slots, 128), f32),
            pltpu.VMEM((128, cols), bf16),
            pltpu.VMEM(gate_up.shape, bf16),
            pltpu.VMEM(down.shape, bf16),
        ]
        + [dma((size,)) for size in sizes]
        + [pltpu.VMEM((2, tok_rows, half), bf16), dma((2 * PIECES,))],
        compiler_params=pltpu.CompilerParams(
            collective_id=0, has_side_effects=True, vmem_limit_bytes=60 * 1024 * 1024
        ),
    )(
        req_len,
        req_offset,
        jnp.asarray(frequency),
        hidden,
        attn_gain[None, :],
        kv_gain[None, :],
        expert_ids.T,
        decode_slot[None, :],
        ffn_gain[None, :],
        router.T,
        kv_down.T,
        queries,
        key_up,
        value_up,
        out_proj,
        gate_up,
        down,
    )


def body(
    hidden,
    queries,
    req_len,
    req_offset,
    expert_ids,
    decode_slot,
    attn_gain,
    kv_down,
    kv_gain,
    key_up,
    value_up,
    out_proj,
    ffn_gain,
    router,
    expert_gate_up,
    expert_down,
):
    head_count = lax.axis_size("head")
    seq_place = lax.axis_index("seq")
    head_place = lax.axis_index("head")
    tok_rows = hidden.shape[0]
    heads_here = key_up.shape[0]
    my_index = seq_place * tok_rows + jnp.arange(tok_rows, dtype=jnp.int32)
    my_request = request_of(req_len, my_index)
    my_turn = angles(position_of(req_len, req_offset, my_index), ROPE)
    normed = rms_rows(hidden, attn_gain).astype(jnp.bfloat16)
    head_view = queries.reshape(tok_rows, heads_here, NOPE + ROPE)
    query_rope = rotate(head_view[:, :, NOPE:], my_turn[:, None, :]).astype(jnp.bfloat16)
    query_latent = jnp.einsum(
        "thn,hnc->thc", head_view[:, :, :NOPE], key_up, preferred_element_type=jnp.float32
    ).astype(jnp.bfloat16)
    query_rows = tok_rows * heads_here
    flat_latent = query_latent.reshape(query_rows, KV_RANK)
    flat_rope = query_rope.reshape(query_rows, ROPE)
    row_token = jnp.repeat(my_index, heads_here)
    row_request = jnp.repeat(my_request, heads_here)
    score_scale = 1.0 / math.sqrt(NOPE + ROPE)
    my_device = seq_place * head_count + head_place
    slot_ids = my_device * DEC_SLOTS + jnp.arange(DEC_SLOTS, dtype=jnp.int32)
    block_ids = jnp.arange(decode_slot.shape[0], dtype=jnp.int32)
    slot_match = decode_slot[None, :] == slot_ids[:, None]
    source_block = jnp.sum(jnp.where(slot_match, block_ids[None, :], 0), axis=1)
    slot_filled = jnp.any(slot_match, axis=1)
    kv_full = jnp.dot(normed, kv_down, preferred_element_type=jnp.float32)
    latent = rms_rows(kv_full[:, :KV_RANK], kv_gain).astype(jnp.bfloat16)
    key_rope = rotate(kv_full[:, KV_RANK:], my_turn).astype(jnp.bfloat16)
    run_peak = jnp.full((query_rows,), MASKED, jnp.float32)
    run_total = jnp.zeros((query_rows,), jnp.float32)
    run_acc = jnp.zeros((query_rows, KV_RANK), jnp.float32)
    expert_count = router.shape[1]
    expert_axis = jnp.arange(expert_count, dtype=jnp.int32)
    seq_count = lax.axis_size("seq")
    fast = seq_count == 16 and head_count == 2 and expert_count == 16
    if fast:
        output, decode_latent, decode_rope = layer(
            req_len,
            req_offset,
            hidden,
            attn_gain,
            kv_down,
            kv_gain,
            expert_ids,
            decode_slot,
            ffn_gain,
            router,
            queries,
            key_up,
            value_up,
            out_proj,
            jnp.swapaxes(expert_gate_up[0], 1, 2),
            expert_down[0],
            seq_count,
        )
        decode_latent = decode_latent.reshape(DEC_SLOTS, BLOCK, KV_RANK)
        return (output, decode_latent, decode_rope)
    else:
        piece_latent = lax.all_gather(latent, "seq", axis=0, tiled=True)
        piece_rope = lax.all_gather(key_rope, "seq", axis=0, tiled=True)
    piece_rows = piece_latent.shape[0]
    block_width = key_width(piece_rows)

    def key_block(block_no, loop_state):
        peak_now, total_now, acc_now = loop_state
        offset_rows = block_no * block_width
        block_latent = lax.dynamic_slice_in_dim(piece_latent, offset_rows, block_width, 0)
        block_rope = lax.dynamic_slice_in_dim(piece_rope, offset_rows, block_width, 0)
        key_index = offset_rows + jnp.arange(block_width, dtype=jnp.int32)
        key_request = request_of(req_len, key_index)
        contract = (((1,), (1,)), ((), ()))
        scores = lax.dot_general(
            flat_latent, block_latent, contract, preferred_element_type=jnp.float32
        )
        scores = (
            scores
            + lax.dot_general(flat_rope, block_rope, contract, preferred_element_type=jnp.float32)
        ) * score_scale
        allowed = (key_index[None, :] <= row_token[:, None]) & (
            key_request[None, :] == row_request[:, None]
        )
        scores = jnp.where(allowed, scores, MASKED)
        new_peak = jnp.maximum(peak_now, jnp.max(scores, axis=1))
        exp_terms = jnp.where(allowed, jnp.exp(scores - new_peak[:, None]), 0.0)
        fade_factor = jnp.exp(peak_now - new_peak)
        total_now = total_now * fade_factor + jnp.sum(exp_terms, axis=1)
        acc_now = acc_now * fade_factor[:, None] + jnp.dot(
            exp_terms.astype(jnp.bfloat16), block_latent, preferred_element_type=jnp.float32
        )
        return (new_peak, total_now, acc_now)

    run_peak, run_total, run_acc = lax.fori_loop(
        0, piece_rows // block_width, key_block, (run_peak, run_total, run_acc)
    )
    block_count = piece_rows // BLOCK
    pick_matrix = (
        source_block[:, None] == jnp.arange(block_count, dtype=jnp.int32)[None, :]
    ) & slot_filled[:, None]
    pick_matrix = pick_matrix.astype(jnp.bfloat16)
    slot_latent = jnp.dot(
        pick_matrix,
        piece_latent.reshape(block_count, BLOCK * KV_RANK),
        preferred_element_type=jnp.float32,
    )
    slot_rope = jnp.dot(
        pick_matrix,
        piece_rope.reshape(block_count, BLOCK * ROPE),
        preferred_element_type=jnp.float32,
    )
    folded = (run_peak, run_total, run_acc, slot_latent, slot_rope)
    run_total = folded[1]
    run_acc = folded[2]
    slot_latent = folded[3]
    slot_rope = folded[4]
    attended = (
        (run_acc / run_total[:, None]).astype(jnp.bfloat16).reshape(tok_rows, heads_here, KV_RANK)
    )
    head_out = jnp.einsum(
        "thc,hcv->thv", attended, value_up, preferred_element_type=jnp.float32
    ).astype(jnp.bfloat16)
    attn_part = jnp.dot(
        head_out.reshape(tok_rows, heads_here * V_HEAD),
        out_proj,
        preferred_element_type=jnp.float32,
    )
    decode_latent = slot_latent.astype(jnp.bfloat16).reshape(DEC_SLOTS, BLOCK, KV_RANK)
    decode_rope = slot_rope.astype(jnp.bfloat16)
    mixed_rows = hidden.astype(jnp.float32) + lax.psum(
        attn_part.astype(jnp.bfloat16), "head"
    ).astype(jnp.float32)
    moe_in = rms_rows(mixed_rows, ffn_gain).astype(jnp.bfloat16)
    capacity = max(2, tok_rows * TOP * 4 // (3 * expert_count))
    gate_score = jax.nn.sigmoid(
        jnp.dot(moe_in.astype(jnp.float32), router, precision=lax.Precision.HIGHEST)
    )
    id_match = expert_ids[:, :, None] == expert_axis[None, None, :]
    chosen = jnp.sum(jnp.where(id_match, gate_score[:, None, :], 0.0), axis=2)
    gate_weight = ROUTE_SCALE * chosen / jnp.sum(chosen, axis=1, keepdims=True)
    flat_ids = expert_ids.reshape(-1)
    one_hot = (flat_ids[:, None] == expert_axis[None, :]).astype(jnp.int32)
    earlier = ranks(one_hot.T.astype(jnp.bfloat16)).T
    slot_rank = jnp.sum(earlier * one_hot, axis=1)
    flat_slot = flat_ids * capacity + slot_rank
    owner_token = jnp.repeat(jnp.arange(tok_rows, dtype=jnp.int32), TOP)
    slot_token = jnp.zeros((expert_count * capacity,), jnp.int32).at[flat_slot].set(owner_token)
    slot_used = jnp.zeros((expert_count * capacity,), jnp.bool_).at[flat_slot].set(True)
    send_rows = jnp.where(
        slot_used[:, None], moe_in[slot_token], jnp.zeros((), jnp.bfloat16)
    ).reshape(expert_count, capacity, D)
    gate_up_local = expert_gate_up[0]
    down_local = expert_down[0]
    quarter_cols = D // head_count
    arrived = lax.all_to_all(send_rows, "seq", split_axis=0, concat_axis=0, tiled=True)
    sources, item_count, width_cols = arrived.shape
    flat_rows = arrived.reshape(sources * item_count, width_cols)
    gate_part = jnp.dot(flat_rows, gate_up_local[0], preferred_element_type=jnp.float32)
    up_part = jnp.dot(flat_rows, gate_up_local[1], preferred_element_type=jnp.float32)
    activated = (jax.nn.silu(gate_part) * up_part).astype(jnp.bfloat16)
    part_out = (
        jnp.dot(activated, down_local, preferred_element_type=jnp.float32)
        .astype(jnp.bfloat16)
        .reshape(sources, item_count, width_cols)
    )
    returned = lax.all_to_all(part_out, "seq", split_axis=0, concat_axis=0, tiled=True)
    back_cols = returned.shape[2]
    picked = returned.reshape(expert_count * capacity, back_cols)[flat_slot].reshape(
        tok_rows, TOP, back_cols
    )
    weighted = jnp.sum(picked.astype(jnp.float32) * gate_weight[:, :, None], axis=1)
    moe_out = lax.psum_scatter(
        weighted.astype(jnp.bfloat16), "head", scatter_dimension=1, tiled=True
    ).astype(jnp.float32)
    residual_part = lax.dynamic_slice_in_dim(mixed_rows, head_place * quarter_cols, quarter_cols, 1)
    output = (residual_part + moe_out).astype(jnp.bfloat16)
    return (output, decode_latent, decode_rope)


def solution(mesh):
    placed = (
        P("seq", None),
        P("seq", "head"),
        P(),
        P(),
        P("seq", None),
        P(),
        P(),
        P(),
        P(),
        P("head", None, None),
        P("head", None, None),
        P("head", None),
        P(),
        P(),
        P("seq", None, None, "head"),
        P("seq", "head", None),
    )
    return jax.shard_map(
        body,
        mesh=mesh,
        in_specs=placed,
        out_specs=(P("seq", "head"), P(("seq", "head"), None, None), P(("seq", "head"), None)),
        check_vma=False,
    )
```
